32 devices in a mesh: dp: 4 (over z), tensor: 8 (over y, x, core).
Axes of the slice: x: 2, y: 2, z: 4, core: 2. Of those that a mesh axis runs over, the one named last changes fastest.
Arguments:
- activations: bfloat16 [16384, 4096], P('dp', 'tensor'), may hold values from -6 to 6
- out_grads: bfloat16 [16384, 14336], P('dp', 'tensor'), may hold values from -6 to 6
- proj_in: bfloat16 [4096, 64], P('tensor'), may hold values from -0.09375 to 0.09375
- proj_out: bfloat16 [14336, 64], P('tensor'), may hold values from -0.046875 to 0.046875
- example_ids: int32 [4, 4096], P('dp'), may hold values from 0 to 511, never falling along the last dimension, each value on 1 to 16 neighbouring positions
- queries: float32 [1024, 4096], P('dp', 'tensor'), may hold values from -6 to 6
Outputs:
- preconditioned: float32 [4096, 1024], P('tensor')
- scores: float32 [1024, 2048], P('tensor', 'dp')
The draws below stay inside these ranges and needn't reach their ends.
Inputs may be any that keep to these rules, and one draw needn't show every extreme that they name: `example_ids`: each row is non-decreasing; every number of 0 to 511 appears in each row, at most 2 * 8 times, and some number exactly that often.
All inputs are finite; a program needn't handle non-finite values.
Results may differ from the reference program's by a relative error of at most 0.0003.
Values sent between devices are 32-bit elements; how exact they have to be, the bound alone decides.
No kernel may reach another device: no remote copies, remote signals or barrier semaphores. Data moves between devices by JAX's collectives and lax.ppermute only.
A program may use at most 128 MiB of HBM per device.

```python
import math
import jax
import jax.numpy as jnp
import numpy as np
from jax import lax

D = 4096
FF = 14336
R_IN = 64
R_OUT = 64
TOK_PER = 8
TOK_DEV = 4096
NQ = 1024
ITERS = 4
EX_DEV = 512
COMP = 4096
TOKENS = 16384
EXAMPLES = 2048
N_DP = 4


def shard_levels(rng, dims, shards, least, largest):
    def one(dim, parts):
        heights = jax.random.uniform(jax.random.fold_in(jax.random.fold_in(rng, 6), dim), (parts,), jnp.float32, least / len(shards), largest / len(shards))
        return jnp.repeat(jnp.exp(heights), dims[dim] // parts).reshape((-1,) + (1,) * (len(dims) - dim - 1))

    factor_of = one(*shards[0])
    for cut in shards[1:]:
        factor_of = factor_of * one(*cut)
    return factor_of


def length_profile(count, total, most, slope):
    weights = [(1 << 20) // math.isqrt(grade ** slope) + 1 for grade in range(2, count + 1)]
    spare, counts = total - most - (count - 1), [1] * (count - 1)
    while spare > 0:
        candidates = [i for i in range(count - 1) if counts[i] < most]
        whole, left = sum([weights[i] for i in candidates]), spare
        for i in candidates:
            more = min(most - counts[i], max(1, left * weights[i] // whole), spare)
            counts[i] = counts[i] + more
            spare = spare - more
    return np.array([most] + counts)


def ragged(stream_key, amount, total, bound, slope):
    if amount == 2:
        one = jax.random.randint(stream_key, (), max(1, total - bound), min(bound, total - 1) + 1)
        return jnp.stack([one, total - one])
    lengths = jnp.asarray(length_profile(amount, total, bound, slope), jnp.int32)
    pairs = (amount - 1) // 2
    donor, receiver = lengths[1:1 + 2 * pairs:2], lengths[2:2 + 2 * pairs:2]
    margin = jnp.minimum(donor - 1, bound - receiver)
    moved = jax.random.randint(jax.random.fold_in(stream_key, 1), (pairs,), 0, 1 << 20) % (margin + 1)
    lengths = lengths.at[1:1 + 2 * pairs:2].set(donor - moved).at[2:2 + 2 * pairs:2].set(receiver + moved)
    return lengths[jax.random.permutation(jax.random.fold_in(stream_key, 2), amount)]


def scatter_about(own_key, dims, spread, limit, split=(), kind=jnp.bfloat16):
    array = spread * jax.random.normal(own_key, dims, jnp.float32)
    if split:
        array = array * shard_levels(own_key, dims, split, -0.22, 0.18)
    return jnp.clip(array, -limit, limit).astype(kind)


def setup_inputs(seed: int = 0) -> dict:
    splits = jax.random.split(jax.random.key(seed), 7)
    return {
        "activations": scatter_about(splits[0], (TOKENS, D), 1.0, 6.0, ((0, 4), (1, 8))),
        "out_grads": scatter_about(splits[1], (TOKENS, FF), 1.0, 6.0, ((0, 4), (1, 8))),
        "proj_in": scatter_about(splits[2], (D, R_IN), D ** -0.5, 0.09375, ((0, 8),)),
        "proj_out": scatter_about(splits[3], (FF, R_OUT), FF ** -0.5, 0.046875, ((0, 8),)),
        "example_ids": jax.vmap(lambda own: jnp.searchsorted(jnp.cumsum(ragged(own, EX_DEV, TOK_DEV, 2 * TOK_PER, 1)), jnp.arange(TOK_DEV), side="right"))(jax.random.split(splits[4], N_DP)).reshape((N_DP, TOK_DEV)).astype(jnp.int32),
        "queries": scatter_about(splits[5], (NQ, COMP), 1.0, 6.0, ((0, 4), (1, 8)), jnp.float32),
    }


def make_sketch(activations, out_grads, proj_in, proj_out, example_ids):
    in_proj = jnp.dot(activations, proj_in, preferred_element_type=jnp.float32)
    out_proj = jnp.dot(out_grads, proj_out, preferred_element_type=jnp.float32)
    offsets = (jnp.arange(N_DP, dtype=jnp.int32) * EX_DEV)[:, None]
    global_ids = (example_ids + offsets).reshape(-1).astype(jnp.int32)

    def one_row(index):
        column = lax.dynamic_slice_in_dim(out_proj, index, 1, 1)
        return jax.ops.segment_sum(column * in_proj, global_ids, num_segments=EXAMPLES)
    stacked = lax.map(one_row, jnp.arange(R_OUT, dtype=jnp.int32))
    return jnp.transpose(stacked, (1, 0, 2)).reshape(EXAMPLES, R_OUT * R_IN)

def reference(activations, out_grads, proj_in, proj_out, example_ids, queries):
    high = lax.Precision.HIGHEST
    sketch = make_sketch(activations, out_grads, proj_in, proj_out, example_ids)
    comp = R_OUT * R_IN
    damping = 0.1 * jnp.sum(sketch * sketch) / (EXAMPLES * comp)

    def operate(vectors):
        inner = jnp.dot(sketch, vectors, precision=high)
        outer = jnp.dot(sketch.T, inner, precision=high)
        return outer / EXAMPLES + damping * vectors
    residual = queries.T
    direction = residual
    solution = jnp.zeros_like(residual)
    norm_now = lax.optimization_barrier(jnp.sum(residual * residual, axis=0))
    for step in range(ITERS):
        image = operate(direction)
        alpha = norm_now / lax.optimization_barrier(jnp.sum(direction * image, axis=0))
        solution = solution + alpha * direction
        residual = residual - alpha * image
        norm_next = lax.optimization_barrier(jnp.sum(residual * residual, axis=0))
        direction = residual + norm_next / norm_now * direction
        norm_now = norm_next
    scores = jnp.dot(sketch, solution, precision=high).T / jnp.sqrt(jnp.float32(comp))
    return (solution, scores)
```

```python
import functools

import jax
import jax.numpy as jnp
from jax import lax
from jax.experimental import pallas as pl
from jax.experimental.pallas import tpu as pltpu
from jax.sharding import PartitionSpec as P

ITERS = 4
EX_DEV = 512
MOST = 16
LANES = 128
WINDOW = 256
F32 = jnp.float32
BF16 = jnp.bfloat16
MIB = 1024 * 1024


def split2(values):
    high = values.astype(BF16)
    low = (values - high.astype(F32)).astype(BF16)
    return high, low


def dot_nn(left, right):
    return lax.dot_general(left, right, (((1,), (0,)), ((), ())), preferred_element_type=F32)


def dot_nt(left, right):
    return lax.dot_general(left, right, (((1,), (1,)), ((), ())), preferred_element_type=F32)


def project_kernel(order_ref, act_ref, grad_ref, wi_ref, wo_ref, out_ref):
    del order_ref
    out_ref[...] = dot_nn(act_ref[...], wi_ref[...]) + dot_nn(grad_ref[...], wo_ref[...])


def project(order, activations, out_grads, w_in, w_out, block):
    steps = order.shape[0]
    feats, hidden = activations.shape[1], out_grads.shape[1]
    lanes = w_in.shape[1]
    return pl.pallas_call(
        project_kernel,
        out_shape=jax.ShapeDtypeStruct((steps * block, lanes), F32),
        grid_spec=pltpu.PrefetchScalarGridSpec(
            num_scalar_prefetch=1,
            grid=(steps,),
            in_specs=[
                pl.BlockSpec((block, feats), lambda i, order: (order[i], 0)),
                pl.BlockSpec((block, hidden), lambda i, order: (order[i], 0)),
                pl.BlockSpec((feats, lanes), lambda i, order: (0, 0)),
                pl.BlockSpec((hidden, lanes), lambda i, order: (0, 0)),
            ],
            out_specs=pl.BlockSpec((block, lanes), lambda i, order: (i, 0)),
        ),
        compiler_params=pltpu.CompilerParams(vmem_limit_bytes=40 * MIB),
        cost_estimate=pl.CostEstimate(
            flops=2 * steps * block * (feats + hidden) * lanes,
            bytes_accessed=2 * steps * block * (feats + hidden),
            transcendentals=0,
        ),
    )(order, activations, out_grads, w_in, w_out)


def build_kernel(
    ranks, piece, ex_block,
    offs_ref, first_ref, near_ref, far_ref, ids_ref, pick_ref, b_ref,
    high_ref, low_ref, inner_ref, sq_ref,
    out_high, out_low, in_both, rows, sketch,
):
    step = pl.program_id(0)
    half_ranks = pick_ref.shape[0]
    pieces = near_ref.shape[0] // piece

    @pl.when(step == 0)
    def _():
        lane = lax.broadcasted_iota(jnp.int32, (piece, LANES), 1)
        for source, base in ((near_ref, 0), (far_ref, pieces)):
            for k in range(pieces):
                values = source[k * piece:(k + 1) * piece, :]
                at = pl.multiple_of(offs_ref[base + k], piece)
                high, low = split2(values)
                out_high[:, pl.ds(at, piece)] = dot_nt(pick_ref[...], high).astype(BF16)
                out_low[:, pl.ds(at, piece)] = dot_nt(pick_ref[...], low).astype(BF16)
                twice = jnp.where(lane < ranks, values, pltpu.roll(values, ranks, 1))
                high, low = split2(twice)
                in_both[pl.ds(at, piece), 0:LANES] = high
                in_both[pl.ds(at, piece), LANES:2 * LANES] = low
        sq_ref[...] = jnp.zeros_like(sq_ref)

    group = rows.shape[1] // half_ranks
    lane = lax.broadcasted_iota(jnp.int32, (group, LANES), 1)

    def one_group(g, slot):
        number = step * (ex_block // group) + g
        at = pl.multiple_of(first_ref[number] * LANES, LANES)
        ids = ids_ref[0:1, pl.ds(at, WINDOW)]
        oh = out_high[:, pl.ds(at, WINDOW)]
        ol = out_low[:, pl.ds(at, WINDOW)]
        zero = jnp.zeros_like(oh)
        masks = [
            jnp.broadcast_to((ids == number * group + e).astype(F32), oh.shape).astype(BF16)
            for e in range(group)
        ]
        del zero
        left = jnp.concatenate([oh * m for m in masks] + [ol * m for m in masks], axis=0)
        res = dot_nn(left, in_both[pl.ds(at, WINDOW), :])
        top = group * half_ranks
        rows[slot] = (
            (res[:top, :LANES] + res[top:, :LANES]) + (res[:top, LANES:] + res[top:, LANES:])
        )
        to = pl.multiple_of(g * group, group)
        for pair in range(half_ranks // 2):
            even = rows[slot, pl.ds(2 * pair, group, stride=half_ranks), :]
            odd = rows[slot, pl.ds(2 * pair + 1, group, stride=half_ranks), :]
            sketch[pl.ds(to, group), pair * LANES:(pair + 1) * LANES] = jnp.where(
                lane < ranks, even, odd
            )

    slots = rows.shape[0]

    @pl.loop(0, ex_block // group // slots)
    def _(turn):
        for slot in range(slots):
            one_group(turn * slots + slot, slot)

    values = sketch[...]
    high, low = split2(values)
    high_ref[...] = high
    low_ref[...] = low
    sq = jnp.sum((values * values).reshape(ex_block // 8, 8, -1), axis=0)
    total = sq[:, 0:LANES]
    for k in range(1, values.shape[1] // LANES):
        total = total + sq[:, k * LANES:(k + 1) * LANES]
    sq_ref[...] += total
    b_high, b_low = split2(b_ref[...])
    both = dot_nt(jnp.concatenate([b_high, b_low], axis=0), high)
    count = b_high.shape[0]
    inner_ref[...] = both[:count] + both[count:] + dot_nt(b_high, low)


def build(offs, first, near, far, ids, pick, b, ranks, piece):
    tokens = ids.shape[1]
    half_ranks = pick.shape[0]
    comps = b.shape[1]
    queries = b.shape[0]
    ex_block = 128
    group = 8
    whole = lambda i, *_: (0, 0)
    return pl.pallas_call(
        functools.partial(build_kernel, ranks, piece, ex_block),
        out_shape=(
            jax.ShapeDtypeStruct((EX_DEV, comps), BF16),
            jax.ShapeDtypeStruct((EX_DEV, comps), BF16),
            jax.ShapeDtypeStruct((queries, EX_DEV), F32),
            jax.ShapeDtypeStruct((8, LANES), F32),
        ),
        grid_spec=pltpu.PrefetchScalarGridSpec(
            num_scalar_prefetch=2,
            grid=(EX_DEV // ex_block,),
            in_specs=[
                pl.BlockSpec(near.shape, whole),
                pl.BlockSpec(far.shape, whole),
                pl.BlockSpec(ids.shape, whole),
                pl.BlockSpec(pick.shape, whole),
                pl.BlockSpec(b.shape, whole),
            ],
            out_specs=[
                pl.BlockSpec((ex_block, comps), lambda i, *_: (i, 0)),
                pl.BlockSpec((ex_block, comps), lambda i, *_: (i, 0)),
                pl.BlockSpec((queries, ex_block), lambda i, *_: (0, i)),
                pl.BlockSpec((8, LANES), whole),
            ],
            scratch_shapes=[
                pltpu.VMEM((half_ranks, tokens), BF16),
                pltpu.VMEM((half_ranks, tokens), BF16),
                pltpu.VMEM((tokens, 2 * LANES), BF16),
                pltpu.VMEM((2, group * half_ranks, LANES), F32),
                pltpu.VMEM((ex_block, comps), F32),
            ],
        ),
        compiler_params=pltpu.CompilerParams(vmem_limit_bytes=40 * MIB),
        cost_estimate=pl.CostEstimate(
            flops=2 * EX_DEV * half_ranks * 2 * WINDOW * 2 * LANES + 6 * EX_DEV * queries * comps,
            bytes_accessed=4 * EX_DEV * comps + 8 * near.shape[0] * LANES,
            transcendentals=0,
        ),
    )(offs, first, near, far, ids, pick, b)


def column(values, k):
    return values[:, k:k + 1]


def lanes_of(columns, shape):
    lane = lax.broadcasted_iota(jnp.int32, shape, 1)
    out = jnp.zeros(shape, F32)
    for k, one in enumerate(columns):
        out = jnp.where(lane == k, one, out)
    return out


def begin(first, examples, comps_all, mine, other, s_prev, state):
    total = mine + other
    inner, stats = total[:, :examples], total[:, examples:]
    norm = column(stats, 0)
    if first:
        damping = 0.1 * column(stats, 1) / (examples * comps_all)
        s, length, beta = inner, norm, None
    else:
        beta = norm / column(state, 0)
        s = inner + beta * s_prev
        length = norm + 2.0 * beta * column(stats, 1) + beta * beta * column(state, 1)
        damping = column(state, 2)
    bend = jnp.sum(s * s, axis=1, keepdims=True) / examples + damping * length
    return s, norm, length, damping, beta, norm / bend


def step_kernel(first, planes, examples, comps_all, *refs):
    refs = list(refs)
    take = lambda n: [refs.pop(0) for _ in range(n)]
    mine_ref, other_ref, r_ref = take(3)
    if not first:
        p_ref, x_ref, s_ref, y_ref, state_ref = take(5)
    highs, lows = take(planes), take(planes)
    msg_out, r_out, p_out, x_out, s_out, y_out, state_out = take(7)
    s_two, z_acc, stats_acc, scal = take(4)
    step = pl.program_id(0)
    count = mine_ref.shape[0]

    @pl.when(step == 0)
    def _():
        s, norm, length, damping, beta, alpha = begin(
            first, examples, comps_all, mine_ref[...], other_ref[...],
            None if first else s_ref[...], None if first else state_ref[...],
        )
        s_out[...] = s
        y_out[...] = alpha * s if first else y_ref[...] + alpha * s
        high, low = split2(s)
        s_two[0:count, :] = high
        s_two[count:2 * count, :] = low
        state_out[...] = lanes_of([norm, length, damping], state_out.shape)
        scal[...] = lanes_of([alpha, damping] + ([] if first else [beta]), scal.shape)
        z_acc[...] = jnp.zeros_like(z_acc)
        stats_acc[...] = jnp.zeros_like(stats_acc)

    alpha, damping = scal[:, 0:1], scal[:, 1:2]
    r = r_ref[...]
    if first:
        p = r
        x_out[...] = alpha * p
    else:
        p = r + scal[:, 2:3] * p_ref[...]
        x_out[...] = x_ref[...] + alpha * p
    p_out[...] = p
    q = jnp.zeros(r.shape, F32)
    for k in range(planes):
        part = slice(k * EX_DEV, (k + 1) * EX_DEV)
        both = dot_nn(s_two[:, part], highs[k][...])
        q = q + both[:count] + both[count:] + dot_nn(s_two[0:count, part], lows[k][...])
    r_new = r - alpha * (q / examples + damping * p)
    r_out[...] = r_new
    high, low = split2(r_new)
    stacked = jnp.concatenate([high, low], axis=0)
    for k in range(planes):
        part = slice(k * EX_DEV, (k + 1) * EX_DEV)
        both = dot_nt(stacked, highs[k][...])
        z_acc[:, part] += both[:count] + both[count:] + dot_nt(high, lows[k][...])
    stats_acc[...] += lanes_of(
        [
            jnp.sum(r_new * r_new, axis=1, keepdims=True),
            jnp.sum(r_new * p, axis=1, keepdims=True),
        ],
        stats_acc.shape,
    )

    @pl.when(step == pl.num_programs(0) - 1)
    def _():
        msg_out[:, 0:examples] = z_acc[...]
        msg_out[:, examples:] = stats_acc[...]


def one_step(first, examples, comps_all, mine, other, r, rest, highs, lows):
    planes = len(highs)
    count, comps = r.shape
    block = 256
    whole = lambda i: (0, 0)
    along = lambda i: (0, i)
    full = lambda a: pl.BlockSpec(a.shape, whole)
    piece = pl.BlockSpec((count, block), along)
    in_specs = [full(mine), full(other), piece]
    if not first:
        p, x, s, y, state = rest
        in_specs += [piece, piece, full(s), full(y), full(state)]
    in_specs += [pl.BlockSpec((EX_DEV, block), along)] * (2 * planes)
    wide = jax.ShapeDtypeStruct((count, examples), F32)
    long = jax.ShapeDtypeStruct((count, comps), F32)
    small = jax.ShapeDtypeStruct((count, LANES), F32)
    message = jax.ShapeDtypeStruct((count, examples + LANES), F32)
    return pl.pallas_call(
        functools.partial(step_kernel, first, planes, examples, comps_all),
        out_shape=(message, long, long, long, wide, wide, small),
        grid=(comps // block,),
        in_specs=in_specs,
        out_specs=[full(message), piece, piece, piece, full(wide), full(wide), full(small)],
        scratch_shapes=[
            pltpu.VMEM((2 * count, examples), BF16),
            pltpu.VMEM((count, examples), F32),
            pltpu.VMEM((count, LANES), F32),
            pltpu.VMEM((count, LANES), F32),
        ],
        compiler_params=pltpu.CompilerParams(vmem_limit_bytes=40 * MIB),
        cost_estimate=pl.CostEstimate(
            flops=12 * count * examples * comps,
            bytes_accessed=4 * examples * comps,
            transcendentals=0,
        ),
    )(mine, other, r, *rest, *highs, *lows)


def last_kernel(examples, comps_all, mine_ref, other_ref, r_ref, p_ref, x_ref, s_ref, y_ref, state_ref, x_out, y_out):
    s, _, _, _, beta, alpha = begin(
        False, examples, comps_all, mine_ref[...], other_ref[...], s_ref[...], state_ref[...]
    )
    scale = 1.0 / jnp.sqrt(F32(comps_all))
    y_out[...] = (y_ref[...] + alpha * s) * scale
    x_out[...] = x_ref[...] + alpha * (r_ref[...] + beta * p_ref[...])


def last_step(examples, comps_all, *arrays):
    x, y = arrays[4], arrays[6]
    return pl.pallas_call(
        functools.partial(last_kernel, examples, comps_all),
        out_shape=(jax.ShapeDtypeStruct(x.shape, F32), jax.ShapeDtypeStruct(y.shape, F32)),
        compiler_params=pltpu.CompilerParams(vmem_limit_bytes=40 * MIB),
    )(*arrays)


def per_device(n_dp, n_t, activations, out_grads, proj_in, proj_out, example_ids, queries):
    tokens = activations.shape[0]
    ranks = proj_in.shape[1]
    comps_all = proj_in.shape[1] * proj_out.shape[1]
    examples = EX_DEV * n_dp
    n_c = n_t // 2
    bits = n_c.bit_length() - 1
    j = lax.axis_index("tensor")
    i = lax.axis_index("dp")
    chip, core = j // 2, j % 2

    def swap(values, mask):
        return lax.ppermute(values, "tensor", [(a, a ^ mask) for a in range(n_t)])

    def shift(values, by):
        return lax.ppermute(values, "dp", [(a, (a + by) % n_dp) for a in range(n_dp)])

    near_chip = [chip ^ k for k in range(n_c)]

    q_chip = queries.shape[0] // n_c
    slots = [lax.dynamic_slice_in_dim(queries, near_chip[k] * q_chip, q_chip, 0) for k in range(n_c)]
    slots = [slots[0]] + [swap(slots[k], 2 * k) for k in range(1, n_c)]
    b = jnp.concatenate(slots, axis=1)

    ids_all = lax.all_gather(example_ids, "dp", axis=0, tiled=True)
    group = 8
    bounds = group * jnp.arange(EX_DEV // group, dtype=jnp.int32)
    starts = jnp.sum((ids_all[:, None, :] < bounds[None, :, None]).astype(jnp.int32), axis=-1)
    firsts = jnp.minimum(starts // LANES, (tokens - WINDOW) // LANES)

    w_in = jnp.pad(proj_in, ((0, 0), (0, ranks)))
    w_out = jnp.pad(proj_out, ((0, 0), (ranks, 0)))
    share = tokens // n_t
    blocks = jnp.stack(near_chip).astype(jnp.int32) * 2
    give = project(blocks + 1 - core, activations, out_grads, w_in, w_out, share)
    keep = project(blocks + core, activations, out_grads, w_in, w_out, share)
    kept = (keep + swap(give, 1)).reshape((n_c, share, LANES))
    half = share // 2
    own = []
    orders = (list(range(bits)), list(range(bits))[::-1])
    for part, order in enumerate(orders):
        held = {k: kept[k, part * half:(part + 1) * half] for k in range(n_c)}
        for bit in order:
            low = [k for k in held if not (k >> bit) & 1]
            came = swap(jnp.stack([held[k | (1 << bit)] for k in low]), 2 << bit)
            held = {k: held[k] + came[n] for n, k in enumerate(low)}
        own.append(held[0])

    rings = [jnp.concatenate(own, axis=0)]
    for _ in range(n_dp - 1):
        rings.append(shift(rings[-1], 1))
    slot_orders = []
    for order in orders:
        ks = [0]
        for bit in order[::-1]:
            ks = ks + [k | (1 << bit) for k in ks]
        slot_orders.append(ks)
    offs = jnp.stack(
        [
            (near_chip[k] * 2 + which) * share + part * half
            for which in (core, 1 - core)
            for part in range(2)
            for k in slot_orders[part]
        ]
    ).astype(jnp.int32)

    per = comps_all // ranks // n_t
    wanted = jnp.stack([(near_chip[k] * 2 + core) * per + a for k in range(n_c) for a in range(per)]) + ranks
    pick = (wanted[:, None] == jnp.arange(LANES)[None, :]).astype(BF16)

    highs, lows, inners, squares = [], [], [], []
    for away in range(n_dp):
        gathered = []
        for part, order in enumerate(orders):
            held = rings[away][part * half:(part + 1) * half]
            for bit in order[::-1]:
                held = jnp.concatenate([held, swap(held, 2 << bit)], axis=0)
            gathered.append(held)
        near = jnp.concatenate(gathered, axis=0)
        far = swap(near, 1)
        plane = (i - away) % n_dp
        ids = lax.dynamic_slice_in_dim(ids_all, plane, 1, 0)
        first = lax.dynamic_index_in_dim(firsts, plane, 0, keepdims=False)
        high, low, inner, square = build(offs, first, near, far, ids, pick, b, ranks, half)
        highs.append(high)
        lows.append(low)
        inners.append(inner)
        squares.append(square)

    square = jnp.sum(jnp.stack(squares))
    stats = jnp.concatenate(
        [
            jnp.sum(b * b, axis=1, keepdims=True),
            jnp.broadcast_to(square, (q_chip, 1)),
            jnp.zeros((q_chip, LANES - 2), F32),
        ],
        axis=1,
    )
    message = jnp.concatenate(inners + [stats], axis=1)
    r, rest = b, ()
    for step in range(ITERS - 1):
        other = swap(message, 1)
        message, r, p, x, s, y, state = one_step(
            step == 0, examples, comps_all, message, other, r, rest, highs, lows
        )
        rest = (p, x, s, y, state)
    other = swap(message, 1)
    x, y = last_step(examples, comps_all, message, other, r, *rest)

    per_slot = comps_all // n_t
    own_x = jnp.zeros((n_c * q_chip, per_slot), F32)
    for k in range(n_c):
        part = x[:, k * per_slot:(k + 1) * per_slot]
        if k:
            part = swap(part, 2 * k)
        own_x = lax.dynamic_update_slice_in_dim(own_x, part, near_chip[k] * q_chip, 0)
    q_plane = n_c * q_chip
    out = jnp.zeros((per_slot, n_dp * q_plane), F32)
    ring = own_x
    for away in range(n_dp):
        if away:
            ring = shift(ring, 1)
        out = lax.dynamic_update_slice_in_dim(out, ring.T, ((i - away) % n_dp) * q_plane, 1)

    part_q = q_chip // 2
    mine = lax.dynamic_slice_in_dim(y, core * part_q, part_q, 0)
    by_plane = jnp.zeros((n_dp, part_q, EX_DEV), F32)
    for away in range(n_dp):
        part = mine[:, away * EX_DEV:(away + 1) * EX_DEV]
        if away:
            part = shift(part, -away)
        by_plane = lax.dynamic_update_slice(by_plane, part[None], ((i + away) % n_dp, 0, 0))
    by_chip = jnp.zeros((n_c, part_q, EX_DEV), F32)
    for k in range(n_c):
        part = lax.dynamic_slice_in_dim(by_plane, near_chip[k], 1, 0)
        if k:
            part = swap(part, 2 * k)
        by_chip = lax.dynamic_update_slice(by_chip, part, (near_chip[k], 0, 0))
    n_half = n_c // 2
    give = lax.dynamic_slice_in_dim(by_chip, (1 - core) * n_half, n_half, 0)
    keep = lax.dynamic_slice_in_dim(by_chip, core * n_half, n_half, 0)
    came = swap(give, 1)
    scores = jnp.zeros((n_half, 2, part_q, EX_DEV), F32)
    scores = lax.dynamic_update_slice(scores, keep[:, None], (0, core, 0, 0))
    scores = lax.dynamic_update_slice(scores, came[:, None], (0, 1 - core, 0, 0))
    return (out, scores.reshape((n_half * q_chip, EX_DEV)))


def solution(mesh):
    in_specs = (
        P("dp", "tensor"),
        P("dp", "tensor"),
        P("tensor", None),
        P("tensor", None),
        P("dp", None),
        P("dp", "tensor"),
    )
    out_specs = (P("tensor", None), P("tensor", "dp"))
    body = functools.partial(per_device, mesh.shape["dp"], mesh.shape["tensor"])
    return jax.shard_map(body, mesh=mesh, in_specs=in_specs, out_specs=out_specs, check_vma=False)
```

```python
import functools

import jax
import jax.numpy as jnp
from jax import lax
from jax.experimental import pallas as pl
from jax.experimental.pallas import tpu as pltpu
from jax.sharding import PartitionSpec as P

ITERS = 4
EX_DEV = 512
LANES = 128
WINDOW = 256
F32 = jnp.float32
BF16 = jnp.bfloat16
MIB = 1024 * 1024


def split2(values):
    high = values.astype(BF16)
    low = (values - high.astype(F32)).astype(BF16)
    return high, low


def dot_nn(left, right):
    return lax.dot_general(left, right, (((1,), (0,)), ((), ())), preferred_element_type=F32)


def dot_nt(left, right):
    return lax.dot_general(left, right, (((1,), (1,)), ((), ())), preferred_element_type=F32)


def project_kernel(order_ref, act_ref, grad_ref, wi_ref, wo_ref, out_ref):
    del order_ref
    out_ref[...] = jnp.concatenate(
        [dot_nn(act_ref[...], wi_ref[...]), dot_nn(grad_ref[...], wo_ref[...])], axis=1
    )


def project(order, activations, out_grads, w_in, w_out, block):
    steps = order.shape[0]
    feats, hidden = activations.shape[1], out_grads.shape[1]
    return pl.pallas_call(
        project_kernel,
        out_shape=jax.ShapeDtypeStruct((steps * block, LANES), F32),
        grid_spec=pltpu.PrefetchScalarGridSpec(
            num_scalar_prefetch=1,
            grid=(steps,),
            in_specs=[
                pl.BlockSpec((block, feats), lambda i, order: (order[i], 0)),
                pl.BlockSpec((block, hidden), lambda i, order: (order[i], 0)),
                pl.BlockSpec(w_in.shape, lambda i, order: (0, 0)),
                pl.BlockSpec(w_out.shape, lambda i, order: (0, 0)),
            ],
            out_specs=pl.BlockSpec((block, LANES), lambda i, order: (i, 0)),
        ),
        compiler_params=pltpu.CompilerParams(vmem_limit_bytes=61 * MIB),
        cost_estimate=pl.CostEstimate(
            flops=2 * steps * block * (feats + hidden) * LANES,
            bytes_accessed=2 * steps * block * (feats + hidden),
            transcendentals=0,
        ),
    )(order, activations, out_grads, w_in, w_out)


def build_kernel(ranks, share, ex_block, n_sources, *refs):
    offs_ref, start_ref = refs[:2]
    sources = refs[2:2 + n_sources]
    ids_ref, pick_ref, b_ref = refs[2 + n_sources:5 + n_sources]
    high_ref, low_ref, inner_ref, sq_ref = refs[5 + n_sources:9 + n_sources]
    out_t, in_twice, ids_wide, rows, sketch = refs[9 + n_sources:]
    step = pl.program_id(0)
    half_ranks = pick_ref.shape[0]
    pairs = half_ranks // 2
    tokens = ids_ref.shape[1]

    @pl.when(step == 0)
    def _():
        lane = lax.broadcasted_iota(jnp.int32, (share, LANES), 1)
        block = 0
        for source in sources:
            for k in range(source.shape[0] // share):
                values = source[k * share:(k + 1) * share, :]
                at = pl.multiple_of(offs_ref[block] * share, share)
                block += 1
                high, low = split2(values)
                out_t[:, pl.ds(at, share)] = dot_nt(pick_ref[...], high) + dot_nt(pick_ref[...], low)
                in_twice[pl.ds(at, share), :] = jnp.where(
                    lane < ranks, values, pltpu.roll(values, ranks, 1)
                )
        ids_wide[...] = jnp.broadcast_to(ids_ref[...], ids_wide.shape)
        sq_ref[...] = jnp.zeros_like(sq_ref)

    slots = rows.shape[0]
    group = rows.shape[1] // pairs
    lane = lax.broadcasted_iota(jnp.int32, (LANES, LANES), 1)
    left_lanes = (lane < ranks).astype(F32).astype(BF16)
    right_lanes = (lane >= ranks).astype(F32).astype(BF16)

    def one_group(g, slot):
        number = step * (ex_block // group) + g
        start = start_ref[number]
        at = jnp.minimum(lax.div(start, LANES) * LANES, tokens - WINDOW)
        turn = lax.rem(WINDOW - (start - at), WINDOW)
        at = pl.multiple_of(at, LANES)
        out_win = pltpu.roll(out_t[:, pl.ds(at, WINDOW)], turn, 1)[:, :LANES]
        ids_win = pltpu.roll(ids_wide[:, pl.ds(at, WINDOW)], turn, 1)[:, :LANES]
        base = (number * group).astype(F32)
        lefts = ([], [])
        terms = split2(out_win)
        for e in range(group):
            mask = (ids_win == base + float(e)).astype(F32)
            mask = jnp.concatenate([mask] * (pairs // 8), axis=0).astype(BF16)
            for left, term in zip(lefts, terms):
                left.append(jnp.concatenate([term[:pairs] * mask, term[pairs:] * mask], axis=1))
        left = jnp.concatenate(lefts[0] + lefts[1], axis=0)
        high, low = split2(in_twice[pl.ds(start, LANES), :])
        right = jnp.concatenate(
            [
                jnp.concatenate([high * lanes, low * lanes], axis=1)
                for lanes in (left_lanes, right_lanes)
            ],
            axis=0,
        )
        res = dot_nn(left, right)
        top = group * pairs
        rows[slot] = (
            (res[:top, :LANES] + res[top:, :LANES]) + (res[:top, LANES:] + res[top:, LANES:])
        )
        to = pl.multiple_of(g * group, group)
        for pair in range(pairs):
            sketch[pl.ds(to, group), pair * LANES:(pair + 1) * LANES] = rows[
                slot, pl.ds(pair, group, stride=pairs), :
            ]

    @pl.loop(0, ex_block // group // slots)
    def _(turn):
        for slot in range(slots):
            one_group(turn * slots + slot, slot)

    values = sketch[...]
    high, low = split2(values)
    high_ref[...] = high
    low_ref[...] = low
    sq = jnp.sum((values * values).reshape(ex_block // 8, 8, -1), axis=0)
    total = sq[:, 0:LANES]
    for k in range(1, values.shape[1] // LANES):
        total = total + sq[:, k * LANES:(k + 1) * LANES]
    sq_ref[...] += total
    b_high, b_low = split2(b_ref[...])
    both = dot_nt(jnp.concatenate([b_high, b_low], axis=0), high)
    count = b_high.shape[0]
    inner_ref[...] = both[:count] + both[count:] + dot_nt(b_high, low)


def build(offs, starts, sources, ids, pick, b, ranks, share):
    tokens = ids.shape[1]
    half_ranks = pick.shape[0]
    queries, comps = b.shape
    ex_block = 256
    group = 8
    whole = lambda i, *_: (0, 0)
    return pl.pallas_call(
        functools.partial(build_kernel, ranks, share, ex_block, len(sources)),
        out_shape=(
            jax.ShapeDtypeStruct((EX_DEV, comps), BF16),
            jax.ShapeDtypeStruct((EX_DEV, comps), BF16),
            jax.ShapeDtypeStruct((queries, EX_DEV), F32),
            jax.ShapeDtypeStruct((8, LANES), F32),
        ),
        grid_spec=pltpu.PrefetchScalarGridSpec(
            num_scalar_prefetch=2,
            grid=(EX_DEV // ex_block,),
            in_specs=[pl.BlockSpec(a.shape, whole) for a in (*sources, ids, pick, b)],
            out_specs=[
                pl.BlockSpec((ex_block, comps), lambda i, *_: (i, 0)),
                pl.BlockSpec((ex_block, comps), lambda i, *_: (i, 0)),
                pl.BlockSpec((queries, ex_block), lambda i, *_: (0, i)),
                pl.BlockSpec((8, LANES), whole),
            ],
            scratch_shapes=[
                pltpu.VMEM((half_ranks, tokens), F32),
                pltpu.VMEM((tokens, LANES), F32),
                pltpu.VMEM((8, tokens), F32),
                pltpu.VMEM((4, group * half_ranks // 2, LANES), F32),
                pltpu.VMEM((ex_block, comps), F32),
            ],
        ),
        compiler_params=pltpu.CompilerParams(vmem_limit_bytes=53 * MIB),
        cost_estimate=pl.CostEstimate(
            flops=12 * EX_DEV * half_ranks * WINDOW * 2 * LANES,
            bytes_accessed=4 * EX_DEV * comps + 4 * tokens * LANES,
            transcendentals=0,
        ),
    )(offs, starts, *sources, ids, pick, b)


def column(values, k):
    return values[:, k:k + 1]


def lanes_of(columns, shape):
    lane = lax.broadcasted_iota(jnp.int32, shape, 1)
    out = jnp.zeros(shape, F32)
    for k, one in enumerate(columns):
        out = jnp.where(lane == k, one, out)
    return out


def begin(first, examples, comps_all, mine, other, s_prev, state):
    total = mine + other
    inner, stats = total[:, :examples], total[:, examples:]
    norm = column(stats, 0)
    if first:
        damping = 0.1 * column(stats, 1) / (examples * comps_all)
        s, length, beta = inner, norm, None
    else:
        beta = norm / column(state, 0)
        s = inner + beta * s_prev
        length = norm + 2.0 * beta * column(stats, 1) + beta * beta * column(state, 1)
        damping = column(state, 2)
    bend = jnp.sum(s * s, axis=1, keepdims=True) / examples + damping * length
    return s, norm, length, damping, beta, norm / bend


def step_kernel(first, planes, examples, comps_all, *refs):
    refs = list(refs)
    take = lambda n: [refs.pop(0) for _ in range(n)]
    mine_ref, other_ref, r_ref = take(3)
    if not first:
        p_ref, x_ref, s_ref, y_ref, state_ref = take(5)
    highs, lows = take(planes), take(planes)
    msg_out, r_out, p_out, x_out, s_out, y_out, state_out = take(7)
    s_two, z_acc, stats_acc, scal = take(4)
    step = pl.program_id(0)
    count = mine_ref.shape[0]

    @pl.when(step == 0)
    def _():
        s, norm, length, damping, beta, alpha = begin(
            first, examples, comps_all, mine_ref[...], other_ref[...],
            None if first else s_ref[...], None if first else state_ref[...],
        )
        s_out[...] = s
        y_out[...] = alpha * s if first else y_ref[...] + alpha * s
        high, low = split2(s)
        s_two[0:count, :] = high
        s_two[count:2 * count, :] = low
        state_out[...] = lanes_of([norm, length, damping], state_out.shape)
        scal[...] = lanes_of([alpha, damping] + ([] if first else [beta]), scal.shape)
        z_acc[...] = jnp.zeros_like(z_acc)
        stats_acc[...] = jnp.zeros_like(stats_acc)

    alpha, damping = scal[:, 0:1], scal[:, 1:2]
    r = r_ref[...]
    if first:
        p = r
        x_out[...] = alpha * p
    else:
        p = r + scal[:, 2:3] * p_ref[...]
        x_out[...] = x_ref[...] + alpha * p
    p_out[...] = p
    q = jnp.zeros(r.shape, F32)
    for k in range(planes):
        part = slice(k * EX_DEV, (k + 1) * EX_DEV)
        both = dot_nn(s_two[:, part], highs[k][...])
        q = q + both[:count] + both[count:] + dot_nn(s_two[0:count, part], lows[k][...])
    r_new = r - alpha * (q / examples + damping * p)
    r_out[...] = r_new
    high, low = split2(r_new)
    stacked = jnp.concatenate([high, low], axis=0)
    for k in range(planes):
        part = slice(k * EX_DEV, (k + 1) * EX_DEV)
        both = dot_nt(stacked, highs[k][...])
        z_acc[:, part] += both[:count] + both[count:] + dot_nt(high, lows[k][...])
    stats_acc[...] += lanes_of(
        [
            jnp.sum(r_new * r_new, axis=1, keepdims=True),
            jnp.sum(r_new * p, axis=1, keepdims=True),
        ],
        stats_acc.shape,
    )

    @pl.when(step == pl.num_programs(0) - 1)
    def _():
        msg_out[:, 0:examples] = z_acc[...]
        msg_out[:, examples:] = stats_acc[...]


def one_step(first, examples, comps_all, mine, other, r, rest, highs, lows):
    planes = len(highs)
    count, comps = r.shape
    block = 512
    whole = lambda i: (0, 0)
    along = lambda i: (0, i)
    full = lambda a: pl.BlockSpec(a.shape, whole)
    piece = pl.BlockSpec((count, block), along)
    in_specs = [full(mine), full(other), piece]
    if not first:
        p, x, s, y, state = rest
        in_specs += [piece, piece, full(s), full(y), full(state)]
    in_specs += [pl.BlockSpec((EX_DEV, block), along)] * (2 * planes)
    wide = jax.ShapeDtypeStruct((count, examples), F32)
    long = jax.ShapeDtypeStruct((count, comps), F32)
    small = jax.ShapeDtypeStruct((count, LANES), F32)
    message = jax.ShapeDtypeStruct((count, examples + LANES), F32)
    return pl.pallas_call(
        functools.partial(step_kernel, first, planes, examples, comps_all),
        out_shape=(message, long, long, long, wide, wide, small),
        grid=(comps // block,),
        in_specs=in_specs,
        out_specs=[full(message), piece, piece, piece, full(wide), full(wide), full(small)],
        scratch_shapes=[
            pltpu.VMEM((2 * count, examples), BF16),
            pltpu.VMEM((count, examples), F32),
            pltpu.VMEM((count, LANES), F32),
            pltpu.VMEM((count, LANES), F32),
        ],
        compiler_params=pltpu.CompilerParams(vmem_limit_bytes=56 * MIB),
        cost_estimate=pl.CostEstimate(
            flops=12 * count * examples * comps,
            bytes_accessed=4 * examples * comps,
            transcendentals=0,
        ),
    )(mine, other, r, *rest, *highs, *lows)


def last_kernel(examples, comps_all, mine_ref, other_ref, r_ref, p_ref, x_ref, s_ref, y_ref, state_ref, x_out, y_out):
    s, _, _, _, beta, alpha = begin(
        False, examples, comps_all, mine_ref[...], other_ref[...], s_ref[...], state_ref[...]
    )
    scale = 1.0 / jnp.sqrt(F32(comps_all))
    y_out[...] = (y_ref[...] + alpha * s) * scale
    x_out[...] = x_ref[...] + alpha * (r_ref[...] + beta * p_ref[...])


def last_step(examples, comps_all, *arrays):
    x, y = arrays[4], arrays[6]
    return pl.pallas_call(
        functools.partial(last_kernel, examples, comps_all),
        out_shape=(jax.ShapeDtypeStruct(x.shape, F32), jax.ShapeDtypeStruct(y.shape, F32)),
        compiler_params=pltpu.CompilerParams(vmem_limit_bytes=24 * MIB),
    )(*arrays)


def place_kernel(where_ref, *refs):
    parts, out_ref, held = refs[:-2], refs[-2], refs[-1]
    parts = parts[:2]
    rows = parts[0].shape[0]
    slot = 0
    for part in parts:
        for k in range(part.shape[0] // rows):
            at = pl.multiple_of(where_ref[1 + slot] * rows, rows)
            held[pl.ds(at, rows), :] = part[k * rows:(k + 1) * rows, :]
            slot += 1
    out_ref[...] = held[...].T


def place(where, own, others, out, shape):
    rows = own.shape[0] + others.shape[0]
    whole = lambda i, where: (0, 0)
    operands = [own, others] + ([] if out is None else [out])
    in_specs = [pl.BlockSpec(own.shape, whole), pl.BlockSpec(others.shape, whole)]
    if out is not None:
        in_specs.append(pl.BlockSpec(memory_space=pl.ANY))
    return pl.pallas_call(
        place_kernel,
        out_shape=jax.ShapeDtypeStruct(shape, F32),
        grid_spec=pltpu.PrefetchScalarGridSpec(
            num_scalar_prefetch=1,
            grid=(1,),
            in_specs=in_specs,
            out_specs=pl.BlockSpec((shape[0], rows), lambda i, where: (0, where[0])),
            scratch_shapes=[pltpu.VMEM((rows, own.shape[1]), F32)],
        ),
        input_output_aliases={} if out is None else {3: 0},
        compiler_params=pltpu.CompilerParams(vmem_limit_bytes=24 * MIB),
    )(where, *operands)


def per_device(n_dp, n_t, activations, out_grads, proj_in, proj_out, example_ids, queries):
    tokens = activations.shape[0]
    ranks = proj_in.shape[1]
    comps_all = proj_in.shape[1] * proj_out.shape[1]
    examples = EX_DEV * n_dp
    n_c = n_t // 2
    bits = n_c.bit_length() - 1
    j = lax.axis_index("tensor")
    i = lax.axis_index("dp")
    chip, core = j // 2, j % 2

    def swap(values, mask):
        return lax.ppermute(values, "tensor", [(a, a ^ mask) for a in range(n_t)])

    def shift(values, by):
        return lax.ppermute(values, "dp", [(a, (a + by) % n_dp) for a in range(n_dp)])

    near_chip = [chip ^ k for k in range(n_c)]

    q_chip = queries.shape[0] // n_c
    slots = [lax.dynamic_slice_in_dim(queries, near_chip[k] * q_chip, q_chip, 0) for k in range(n_c)]
    slots = [slots[0]] + [swap(slots[k], 2 * k) for k in range(1, n_c)]
    b = jnp.concatenate(slots, axis=1)

    group = 8
    bounds = group * jnp.arange(EX_DEV // group, dtype=jnp.int32)
    starts = jnp.sum((example_ids[0][None, :] < bounds[:, None]).astype(F32), axis=1)
    starts = jnp.minimum(starts, F32(tokens - LANES))
    id_rows = tokens // LANES
    extra = jnp.concatenate(
        [
            example_ids.astype(F32).reshape((id_rows, LANES)),
            jnp.pad(starts[None, :], ((0, 7), (0, LANES - EX_DEV // group))),
        ],
        axis=0,
    )

    share = tokens // n_t
    blocks = jnp.stack(near_chip).astype(jnp.int32) * 2
    give = project(blocks + 1 - core, activations, out_grads, proj_in, proj_out, share)
    keep = project(blocks + core, activations, out_grads, proj_in, proj_out, share)
    kept = (keep + swap(give, 1)).reshape((n_c, share, LANES))
    own = kept[0]
    for k in range(1, n_c):
        own = own + swap(kept[k], 2 * k)

    rings = [jnp.concatenate([own, extra], axis=0)]
    for _ in range(n_dp - 1):
        rings.append(shift(rings[-1], 1))

    per = comps_all // ranks // n_t
    wanted = [(near_chip[k] * 2 + core) * per + a + ranks for k in range(n_c) for a in range(per)]
    wanted = jnp.stack(wanted[0::2] + wanted[1::2])
    pick = (wanted[:, None] == jnp.arange(LANES)[None, :]).astype(BF16)

    highs, lows, inners, squares = [], [], [], []
    for away in range(n_dp):
        order = list(range(bits))
        if away % 2:
            order = order[::-1]
        held, ks = rings[away][:share], [0]
        for bit in order[:-1]:
            held = jnp.concatenate([held, swap(held, 2 << bit)], axis=0)
            ks = ks + [k | (1 << bit) for k in ks]
        came = swap(held, 2 << order[-1])
        ks = ks + [k | (1 << order[-1]) for k in ks]
        sources = [held, came, swap(held, 1), swap(came, 1)]
        offs = jnp.stack(
            [near_chip[k] * 2 + which for which in (core, 1 - core) for k in ks]
        ).astype(jnp.int32)
        ids = rings[away][share:share + id_rows].reshape((1, tokens))
        first = rings[away][share + id_rows, :EX_DEV // group].astype(jnp.int32)
        high, low, inner, square = build(offs, first, sources, ids, pick, b, ranks, share)
        highs.append(high)
        lows.append(low)
        inners.append(inner)
        squares.append(square)

    square = jnp.sum(jnp.stack(squares))
    stats = jnp.concatenate(
        [
            jnp.sum(b * b, axis=1, keepdims=True),
            jnp.broadcast_to(square, (q_chip, 1)),
            jnp.zeros((q_chip, LANES - 2), F32),
        ],
        axis=1,
    )
    message = jnp.concatenate(inners + [stats], axis=1)
    r, rest = b, ()
    for step in range(ITERS - 1):
        other = swap(message, 1)
        message, r, p, x, s, y, state = one_step(
            step == 0, examples, comps_all, message, other, r, rest, highs, lows
        )
        rest = (p, x, s, y, state)
    other = swap(message, 1)
    x, y = last_step(examples, comps_all, message, other, r, *rest)

    per_slot = comps_all // n_t
    own_x = x[:, :per_slot]
    others_x = jnp.concatenate(
        [swap(x[:, k * per_slot:(k + 1) * per_slot], 2 * k) for k in range(1, n_c)], axis=0
    )
    out = None
    for away in range(n_dp):
        if away:
            own_x, others_x = shift(own_x, 1), shift(others_x, 1)
        where = jnp.stack([(i - away) % n_dp] + near_chip).astype(jnp.int32)
        out = place(where, own_x, others_x, out, (per_slot, n_dp * n_c * q_chip))

    part_q = q_chip // 2
    mine = lax.dynamic_slice_in_dim(y, core * part_q, part_q, 0)
    by_plane = jnp.zeros((n_dp, part_q, EX_DEV), F32)
    for away in range(n_dp):
        part = mine[:, away * EX_DEV:(away + 1) * EX_DEV]
        if away:
            part = shift(part, -away)
        by_plane = lax.dynamic_update_slice(by_plane, part[None], ((i + away) % n_dp, 0, 0))
    by_chip = jnp.zeros((n_c, part_q, EX_DEV), F32)
    for k in range(n_c):
        part = lax.dynamic_slice_in_dim(by_plane, near_chip[k], 1, 0)
        if k:
            part = swap(part, 2 * k)
        by_chip = lax.dynamic_update_slice(by_chip, part, (near_chip[k], 0, 0))
    n_half = n_c // 2
    give = lax.dynamic_slice_in_dim(by_chip, (1 - core) * n_half, n_half, 0)
    keep = lax.dynamic_slice_in_dim(by_chip, core * n_half, n_half, 0)
    came = swap(give, 1)
    scores = jnp.zeros((n_half, 2, part_q, EX_DEV), F32)
    scores = lax.dynamic_update_slice(scores, keep[:, None], (0, core, 0, 0))
    scores = lax.dynamic_update_slice(scores, came[:, None], (0, 1 - core, 0, 0))
    return (out, scores.reshape((n_half * q_chip, EX_DEV)))


def solution(mesh):
    in_specs = (
        P("dp", "tensor"),
        P("dp", "tensor"),
        P("tensor", None),
        P("tensor", None),
        P("dp", None),
        P("dp", "tensor"),
    )
    out_specs = (P("tensor", None), P("tensor", "dp"))
    body = functools.partial(per_device, mesh.shape["dp"], mesh.shape["tensor"])
    return jax.shard_map(body, mesh=mesh, in_specs=in_specs, out_specs=out_specs, check_vma=False)
```

```python
import functools

import jax
import jax.numpy as jnp
from jax import lax
from jax.experimental import pallas as pl
from jax.experimental.pallas import tpu as pltpu
from jax.sharding import PartitionSpec as P

ITERS = 4
EX_DEV = 512
LANES = 128
WINDOW = 256
F32 = jnp.float32
BF16 = jnp.bfloat16
MIB = 1024 * 1024


def split2(values):
    high = values.astype(BF16)
    low = (values - high.astype(F32)).astype(BF16)
    return high, low


def dot_nn(left, right):
    return lax.dot_general(left, right, (((1,), (0,)), ((), ())), preferred_element_type=F32)


def dot_nt(left, right):
    return lax.dot_general(left, right, (((1,), (1,)), ((), ())), preferred_element_type=F32)


def project_kernel(order_ref, act_ref, grad_ref, wi_ref, wo_ref, out_ref):
    del order_ref
    out_ref[...] = jnp.concatenate(
        [dot_nt(act_ref[...], wi_ref[...]), dot_nt(grad_ref[...], wo_ref[...])], axis=1
    )


def project(order, activations, out_grads, w_in, w_out, block):
    steps = order.shape[0]
    feats, hidden = activations.shape[1], out_grads.shape[1]
    return pl.pallas_call(
        project_kernel,
        out_shape=jax.ShapeDtypeStruct((steps * block, LANES), F32),
        grid_spec=pltpu.PrefetchScalarGridSpec(
            num_scalar_prefetch=1,
            grid=(steps,),
            in_specs=[
                pl.BlockSpec((block, feats), lambda i, order: (order[i], 0)),
                pl.BlockSpec((block, hidden), lambda i, order: (order[i], 0)),
                pl.BlockSpec(w_in.shape, lambda i, order: (0, 0)),
                pl.BlockSpec(w_out.shape, lambda i, order: (0, 0)),
            ],
            out_specs=pl.BlockSpec((block, LANES), lambda i, order: (i, 0)),
        ),
        compiler_params=pltpu.CompilerParams(vmem_limit_bytes=61 * MIB),
        cost_estimate=pl.CostEstimate(
            flops=2 * steps * block * (feats + hidden) * 4 * WINDOW,
            bytes_accessed=2 * steps * block * (feats + hidden),
            transcendentals=0,
        ),
    )(order, activations, out_grads, w_in, w_out)


def build_kernel(ranks, share, ex_block, n_sources, *refs):
    offs_ref, start_ref = refs[:2]
    sources = refs[2:2 + n_sources]
    ids_ref, pick_ref, b_ref = refs[2 + n_sources:5 + n_sources]
    high_ref, low_ref, inner_ref, sq_ref = refs[5 + n_sources:9 + n_sources]
    out_t, in_twice, ids_wide, rows, sketch = refs[9 + n_sources:]
    step = pl.program_id(0)
    half_ranks = pick_ref.shape[0]
    pairs = half_ranks // 2
    tokens = ids_ref.shape[1]

    @pl.when(step == 0)
    def _():
        lane = lax.broadcasted_iota(jnp.int32, (share, LANES), 1)
        block = 0
        for source in sources:
            for k in range(source.shape[0] // share):
                values = source[k * share:(k + 1) * share, :]
                at = pl.multiple_of(offs_ref[block] * share, share)
                block += 1
                high, low = split2(values)
                out_t[:, pl.ds(at, share)] = dot_nt(pick_ref[...], high) + dot_nt(pick_ref[...], low)
                in_twice[pl.ds(at, share), :] = jnp.where(
                    lane < ranks, values, pltpu.roll(values, ranks, 1)
                )
        ids_wide[...] = jnp.broadcast_to(ids_ref[...], ids_wide.shape)
        sq_ref[...] = jnp.zeros_like(sq_ref)

    slots = rows.shape[0]
    group = rows.shape[1] // pairs
    lane = lax.broadcasted_iota(jnp.int32, (LANES, LANES), 1)
    left_lanes = (lane < ranks).astype(F32).astype(BF16)
    right_lanes = (lane >= ranks).astype(F32).astype(BF16)

    def one_group(g, slot):
        number = step * (ex_block // group) + g
        start = start_ref[number]
        at = jnp.minimum(lax.div(start, LANES) * LANES, tokens - WINDOW)
        turn = lax.rem(WINDOW - (start - at), WINDOW)
        at = pl.multiple_of(at, LANES)
        out_win = pltpu.roll(out_t[:, pl.ds(at, WINDOW)], turn, 1)[:, :LANES]
        ids_win = pltpu.roll(ids_wide[:, pl.ds(at, WINDOW)], turn, 1)[:, :LANES]
        base = (number * group).astype(F32)
        lefts = ([], [])
        terms = split2(out_win)
        for e in range(group):
            mask = (ids_win == base + float(e)).astype(F32)
            mask = jnp.concatenate([mask] * (pairs // 8), axis=0).astype(BF16)
            for left, term in zip(lefts, terms):
                left.append(jnp.concatenate([term[:pairs] * mask, term[pairs:] * mask], axis=1))
        left = jnp.concatenate(lefts[0] + lefts[1], axis=0)
        high, low = split2(in_twice[pl.ds(start, LANES), :])
        right = jnp.concatenate(
            [
                jnp.concatenate([high * lanes, low * lanes], axis=1)
                for lanes in (left_lanes, right_lanes)
            ],
            axis=0,
        )
        res = dot_nn(left, right)
        top = group * pairs
        rows[slot] = (
            (res[:top, :LANES] + res[top:, :LANES]) + (res[:top, LANES:] + res[top:, LANES:])
        )
        to = pl.multiple_of(g * group, group)
        for pair in range(pairs):
            sketch[pl.ds(to, group), pair * LANES:(pair + 1) * LANES] = rows[
                slot, pl.ds(pair, group, stride=pairs), :
            ]

    @pl.loop(0, ex_block // group // slots)
    def _(turn):
        for slot in range(slots):
            one_group(turn * slots + slot, slot)

    values = sketch[...]
    high, low = split2(values)
    high_ref[...] = high
    low_ref[...] = low
    sq = jnp.sum((values * values).reshape(ex_block // 8, 8, -1), axis=0)
    total = sq[:, 0:LANES]
    for k in range(1, values.shape[1] // LANES):
        total = total + sq[:, k * LANES:(k + 1) * LANES]
    sq_ref[...] += total
    b_both = jnp.concatenate(split2(b_ref[...]), axis=0)
    count = b_ref.shape[0]
    both = (dot_nt(high, b_both) + dot_nt(low, b_both)).T
    inner_ref[...] = both[:count] + both[count:]


def build(offs, starts, sources, ids, pick, b, ranks, share):
    tokens = ids.shape[1]
    half_ranks = pick.shape[0]
    queries, comps = b.shape
    ex_block = 256
    group = 8
    whole = lambda i, *_: (0, 0)
    return pl.pallas_call(
        functools.partial(build_kernel, ranks, share, ex_block, len(sources)),
        out_shape=(
            jax.ShapeDtypeStruct((EX_DEV, comps), BF16),
            jax.ShapeDtypeStruct((EX_DEV, comps), BF16),
            jax.ShapeDtypeStruct((queries, EX_DEV), F32),
            jax.ShapeDtypeStruct((8, LANES), F32),
        ),
        grid_spec=pltpu.PrefetchScalarGridSpec(
            num_scalar_prefetch=2,
            grid=(EX_DEV // ex_block,),
            in_specs=[pl.BlockSpec(a.shape, whole) for a in (*sources, ids, pick, b)],
            out_specs=[
                pl.BlockSpec((ex_block, comps), lambda i, *_: (i, 0)),
                pl.BlockSpec((ex_block, comps), lambda i, *_: (i, 0)),
                pl.BlockSpec((queries, ex_block), lambda i, *_: (0, i)),
                pl.BlockSpec((8, LANES), whole),
            ],
            scratch_shapes=[
                pltpu.VMEM((half_ranks, tokens), F32),
                pltpu.VMEM((tokens, LANES), F32),
                pltpu.VMEM((8, tokens), F32),
                pltpu.VMEM((4, group * half_ranks // 2, LANES), F32),
                pltpu.VMEM((ex_block, comps), F32),
            ],
        ),
        compiler_params=pltpu.CompilerParams(vmem_limit_bytes=50 * MIB),
        cost_estimate=pl.CostEstimate(
            flops=12 * EX_DEV * half_ranks * WINDOW * 2 * LANES,
            bytes_accessed=4 * EX_DEV * comps + 4 * tokens * LANES,
            transcendentals=0,
        ),
    )(offs, starts, *sources, ids, pick, b)


def column(values, k):
    return values[:, k:k + 1]


def lanes_of(columns, shape):
    lane = lax.broadcasted_iota(jnp.int32, shape, 1)
    out = jnp.zeros(shape, F32)
    for k, one in enumerate(columns):
        out = jnp.where(lane == k, one, out)
    return out


def begin(first, examples, comps_all, mine, other, s_prev, state):
    total = mine + other
    inner, stats = total[:, :examples], total[:, examples:]
    norm = column(stats, 0)
    if first:
        damping = 0.1 * column(stats, 1) / (examples * comps_all)
        s, length, beta = inner, norm, None
    else:
        beta = norm / column(state, 0)
        s = inner + beta * s_prev
        length = norm + 2.0 * beta * column(stats, 1) + beta * beta * column(state, 1)
        damping = column(state, 2)
    bend = jnp.sum(s * s, axis=1, keepdims=True) / examples + damping * length
    return s, norm, length, damping, beta, norm / bend


def step_kernel(first, planes, examples, comps_all, *refs):
    refs = list(refs)
    take = lambda n: [refs.pop(0) for _ in range(n)]
    mine_ref, other_ref, r_ref = take(3)
    if not first:
        p_ref, x_ref, s_ref, y_ref, state_ref = take(5)
    highs, lows = take(planes), take(planes)
    msg_out, r_out, p_out, x_out, s_out, y_out, state_out = take(7)
    s_two, z_acc, stats_acc, scal = take(4)
    step = pl.program_id(0)
    count = mine_ref.shape[0]

    @pl.when(step == 0)
    def _():
        s, norm, length, damping, beta, alpha = begin(
            first, examples, comps_all, mine_ref[...], other_ref[...],
            None if first else s_ref[...], None if first else state_ref[...],
        )
        s_out[...] = s
        y_out[...] = alpha * s if first else y_ref[...] + alpha * s
        high, low = split2(s)
        s_two[0:count, :] = high
        s_two[count:2 * count, :] = low
        state_out[...] = lanes_of([norm, length, damping], state_out.shape)
        scal[...] = lanes_of([alpha, damping] + ([] if first else [beta]), scal.shape)
        z_acc[...] = jnp.zeros_like(z_acc)
        stats_acc[...] = jnp.zeros_like(stats_acc)

    alpha, damping = scal[:, 0:1], scal[:, 1:2]
    r = r_ref[...]
    if first:
        p = r
        x_out[...] = alpha * p
    else:
        p = r + scal[:, 2:3] * p_ref[...]
        x_out[...] = x_ref[...] + alpha * p
    p_out[...] = p
    q = jnp.zeros(r.shape, F32)
    for k in range(planes):
        part = slice(k * EX_DEV, (k + 1) * EX_DEV)
        both = dot_nn(s_two[:, part], highs[k][...])
        q = q + both[:count] + both[count:] + dot_nn(s_two[0:count, part], lows[k][...])
    r_new = r - alpha * (q / examples + damping * p)
    r_out[...] = r_new
    stacked = jnp.concatenate(split2(r_new), axis=0)
    for k in range(planes):
        part = slice(k * EX_DEV, (k + 1) * EX_DEV)
        z_acc[part, :] += dot_nt(highs[k][...], stacked) + dot_nt(lows[k][...], stacked)
    stats_acc[...] += lanes_of(
        [
            jnp.sum(r_new * r_new, axis=1, keepdims=True),
            jnp.sum(r_new * p, axis=1, keepdims=True),
        ],
        stats_acc.shape,
    )

    @pl.when(step == pl.num_programs(0) - 1)
    def _():
        both = z_acc[...].T
        msg_out[:, 0:examples] = both[:count] + both[count:]
        msg_out[:, examples:] = stats_acc[...]


def one_step(first, examples, comps_all, mine, other, r, rest, highs, lows):
    planes = len(highs)
    count, comps = r.shape
    block = 512
    whole = lambda i: (0, 0)
    along = lambda i: (0, i)
    full = lambda a: pl.BlockSpec(a.shape, whole)
    piece = pl.BlockSpec((count, block), along)
    in_specs = [full(mine), full(other), piece]
    if not first:
        p, x, s, y, state = rest
        in_specs += [piece, piece, full(s), full(y), full(state)]
    in_specs += [pl.BlockSpec((EX_DEV, block), along)] * (2 * planes)
    wide = jax.ShapeDtypeStruct((count, examples), F32)
    long = jax.ShapeDtypeStruct((count, comps), F32)
    small = jax.ShapeDtypeStruct((count, LANES), F32)
    message = jax.ShapeDtypeStruct((count, examples + LANES), F32)
    return pl.pallas_call(
        functools.partial(step_kernel, first, planes, examples, comps_all),
        out_shape=(message, long, long, long, wide, wide, small),
        grid=(comps // block,),
        in_specs=in_specs,
        out_specs=[full(message), piece, piece, piece, full(wide), full(wide), full(small)],
        scratch_shapes=[
            pltpu.VMEM((2 * count, examples), BF16),
            pltpu.VMEM((examples, 2 * count), F32),
            pltpu.VMEM((count, LANES), F32),
            pltpu.VMEM((count, LANES), F32),
        ],
        compiler_params=pltpu.CompilerParams(vmem_limit_bytes=56 * MIB),
        cost_estimate=pl.CostEstimate(
            flops=12 * count * examples * comps,
            bytes_accessed=4 * examples * comps,
            transcendentals=0,
        ),
    )(mine, other, r, *rest, *highs, *lows)


def last_kernel(examples, comps_all, mine_ref, other_ref, r_ref, p_ref, x_ref, s_ref, y_ref, state_ref, x_out, y_out):
    s, _, _, _, beta, alpha = begin(
        False, examples, comps_all, mine_ref[...], other_ref[...], s_ref[...], state_ref[...]
    )
    scale = 1.0 / jnp.sqrt(F32(comps_all))
    y_out[...] = (y_ref[...] + alpha * s) * scale
    x_out[...] = x_ref[...] + alpha * (r_ref[...] + beta * p_ref[...])


def last_step(examples, comps_all, *arrays):
    x, y = arrays[4], arrays[6]
    full = lambda a: pl.BlockSpec(a.shape, lambda i: (0, 0))
    return pl.pallas_call(
        functools.partial(last_kernel, examples, comps_all),
        out_shape=(jax.ShapeDtypeStruct(x.shape, F32), jax.ShapeDtypeStruct(y.shape, F32)),
        grid=(1,),
        in_specs=[full(a) for a in arrays],
        out_specs=(full(x), full(y)),
        compiler_params=pltpu.CompilerParams(vmem_limit_bytes=60 * MIB),
    )(*arrays)


def place_kernel(where_ref, *refs):
    parts, out_ref, held = refs[:-2], refs[-2], refs[-1]
    parts = parts[:2]
    rows = parts[0].shape[0]
    slot = 0
    for part in parts:
        for k in range(part.shape[0] // rows):
            at = pl.multiple_of(where_ref[1 + slot] * rows, rows)
            held[pl.ds(at, rows), :] = part[k * rows:(k + 1) * rows, :]
            slot += 1
    out_ref[...] = held[...].T


def place(where, own, others, out, shape):
    rows = own.shape[0] + others.shape[0]
    whole = lambda i, where: (0, 0)
    operands = [own, others] + ([] if out is None else [out])
    in_specs = [pl.BlockSpec(own.shape, whole), pl.BlockSpec(others.shape, whole)]
    if out is not None:
        in_specs.append(pl.BlockSpec(memory_space=pl.ANY))
    return pl.pallas_call(
        place_kernel,
        out_shape=jax.ShapeDtypeStruct(shape, F32),
        grid_spec=pltpu.PrefetchScalarGridSpec(
            num_scalar_prefetch=1,
            grid=(1,),
            in_specs=in_specs,
            out_specs=pl.BlockSpec((shape[0], rows), lambda i, where: (0, where[0])),
            scratch_shapes=[pltpu.VMEM((rows, own.shape[1]), F32)],
        ),
        input_output_aliases={} if out is None else {3: 0},
        compiler_params=pltpu.CompilerParams(vmem_limit_bytes=24 * MIB),
    )(where, *operands)


def per_device(n_dp, n_t, activations, out_grads, proj_in, proj_out, example_ids, queries):
    tokens = activations.shape[0]
    ranks = proj_in.shape[1]
    comps_all = proj_in.shape[1] * proj_out.shape[1]
    examples = EX_DEV * n_dp
    n_c = n_t // 2
    bits = n_c.bit_length() - 1
    j = lax.axis_index("tensor")
    i = lax.axis_index("dp")
    chip, core = j // 2, j % 2

    def swap(values, mask):
        return lax.ppermute(values, "tensor", [(a, a ^ mask) for a in range(n_t)])

    def shift(values, by):
        return lax.ppermute(values, "dp", [(a, (a + by) % n_dp) for a in range(n_dp)])

    def tie(values, token):
        return lax.optimization_barrier((values, token))[0]

    near_chip = [chip ^ k for k in range(n_c)]

    q_chip = queries.shape[0] // n_c
    slots = [lax.dynamic_slice_in_dim(queries, near_chip[k] * q_chip, q_chip, 0) for k in range(n_c)]
    slots = [slots[0]] + [swap(slots[k], 2 * k) for k in range(1, n_c)]
    b = jnp.concatenate(slots, axis=1)

    group = 8
    bounds = group * jnp.arange(EX_DEV // group, dtype=jnp.int32)
    starts = jnp.sum((example_ids[0][None, :] < bounds[:, None]).astype(F32), axis=1)
    starts = jnp.minimum(starts, F32(tokens - LANES))
    id_rows = tokens // LANES
    extra = jnp.concatenate(
        [
            example_ids.astype(F32).reshape((id_rows, LANES)),
            jnp.pad(starts[None, :], ((0, 7), (0, LANES - EX_DEV // group))),
        ],
        axis=0,
    )

    share = tokens // n_t
    blocks = jnp.stack(near_chip).astype(jnp.int32) * 2
    w_in, w_out = proj_in.T, proj_out.T
    give = project(blocks + 1 - core, activations, out_grads, w_in, w_out, share)
    keep = project(tie(blocks + core, slots), activations, out_grads, w_in, w_out, share)
    kept = (keep + swap(give, 1)).reshape((n_c, share, LANES))
    own = kept[0]
    for k in range(1, n_c):
        own = own + swap(kept[k], 2 * k)

    rings = [jnp.concatenate([own, extra], axis=0)]
    for _ in range(n_dp - 1):
        rings.append(shift(rings[-1], 1))

    per = comps_all // ranks // n_t
    wanted = [(near_chip[k] * 2 + core) * per + a + ranks for k in range(n_c) for a in range(per)]
    wanted = jnp.stack(wanted[0::2] + wanted[1::2])
    pick = (wanted[:, None] == jnp.arange(LANES)[None, :]).astype(BF16)

    highs, lows, inners, squares = [], [], [], []
    for away in range(n_dp):
        order = list(range(bits))
        if away % 2:
            order = order[::-1]
        after = lambda values, stage: (
            tie(values, squares[away - bits - 1 + stage]) if away > bits - stage else values
        )
        held, ks = after(rings[away][:share], 0), [0]
        for stage, bit in enumerate(order[:-1]):
            held = jnp.concatenate([held, after(swap(held, 2 << bit), stage + 1)], axis=0)
            ks = ks + [k | (1 << bit) for k in ks]
        came = after(swap(held, 2 << order[-1]), bits)
        ks = ks + [k | (1 << order[-1]) for k in ks]
        sources = [held, came, swap(held, 1), swap(came, 1)]
        offs = jnp.stack(
            [near_chip[k] * 2 + which for which in (core, 1 - core) for k in ks]
        ).astype(jnp.int32)
        ids = rings[away][share:share + id_rows].reshape((1, tokens))
        first = rings[away][share + id_rows, :EX_DEV // group].astype(jnp.int32)
        high, low, inner, square = build(offs, first, sources, ids, pick, b, ranks, share)
        highs.append(high)
        lows.append(low)
        inners.append(inner)
        squares.append(square)

    square = jnp.sum(jnp.stack(squares))
    stats = jnp.concatenate(
        [
            jnp.sum(b * b, axis=1, keepdims=True),
            jnp.broadcast_to(square, (q_chip, 1)),
            jnp.zeros((q_chip, LANES - 2), F32),
        ],
        axis=1,
    )
    message = jnp.concatenate(inners + [stats], axis=1)
    r, rest = b, ()
    for step in range(ITERS - 1):
        other = swap(message, 1)
        message, r, p, x, s, y, state = one_step(
            step == 0, examples, comps_all, message, other, r, rest, highs, lows
        )
        rest = (p, x, s, y, state)
    other = swap(message, 1)
    x, y = last_step(examples, comps_all, message, other, r, *rest)

    per_slot = comps_all // n_t
    own_x = x[:, :per_slot]
    others_x = jnp.concatenate(
        [swap(x[:, k * per_slot:(k + 1) * per_slot], 2 * k) for k in range(1, n_c)], axis=0
    )
    y, others_x = lax.optimization_barrier((y, others_x))
    own_parts = [own_x] + [shift(own_x, away) for away in range(1, n_dp)]
    out = None
    for away in range(n_dp):
        if away == 2:
            others_x = tie(others_x, own_parts)
        if away:
            others_x = shift(others_x, 1)
        where = jnp.stack([(i - away) % n_dp] + near_chip).astype(jnp.int32)
        out = place(where, own_parts[away], others_x, out, (per_slot, n_dp * n_c * q_chip))

    part_q = q_chip // 2
    mine = lax.dynamic_slice_in_dim(y, core * part_q, part_q, 0)
    by_plane = jnp.zeros((n_dp, part_q, EX_DEV), F32)
    for away in range(n_dp):
        part = mine[:, away * EX_DEV:(away + 1) * EX_DEV]
        if away:
            part = shift(part, -away)
        by_plane = lax.dynamic_update_slice(by_plane, part[None], ((i + away) % n_dp, 0, 0))
    by_chip = jnp.zeros((n_c, part_q, EX_DEV), F32)
    for k in range(n_c):
        part = lax.dynamic_slice_in_dim(by_plane, near_chip[k], 1, 0)
        if k:
            part = swap(part, 2 * k)
        by_chip = lax.dynamic_update_slice(by_chip, part, (near_chip[k], 0, 0))
    n_half = n_c // 2
    give = lax.dynamic_slice_in_dim(by_chip, (1 - core) * n_half, n_half, 0)
    keep = lax.dynamic_slice_in_dim(by_chip, core * n_half, n_half, 0)
    came = swap(give, 1)
    scores = jnp.zeros((n_half, 2, part_q, EX_DEV), F32)
    scores = lax.dynamic_update_slice(scores, keep[:, None], (0, core, 0, 0))
    scores = lax.dynamic_update_slice(scores, came[:, None], (0, 1 - core, 0, 0))
    return (out, scores.reshape((n_half * q_chip, EX_DEV)))


def solution(mesh):
    in_specs = (
        P("dp", "tensor"),
        P("dp", "tensor"),
        P("tensor", None),
        P("tensor", None),
        P("dp", None),
        P("dp", "tensor"),
    )
    out_specs = (P("tensor", None), P("tensor", "dp"))
    body = functools.partial(per_device, mesh.shape["dp"], mesh.shape["tensor"])
    return jax.shard_map(body, mesh=mesh, in_specs=in_specs, out_specs=out_specs, check_vma=False)
```

```python
import functools

import jax
import jax.numpy as jnp
from jax import lax
from jax.experimental import pallas as pl
from jax.experimental.pallas import tpu as pltpu
from jax.sharding import PartitionSpec as P

ITERS = 4
EX_DEV = 512
LANES = 128
WINDOW = 256
F32 = jnp.float32
BF16 = jnp.bfloat16
MIB = 1024 * 1024
BUILD = 24
STEP = 24


def split2(values):
    high = values.astype(BF16)
    low = (values - high.astype(F32)).astype(BF16)
    return high, low


def dot_nn(left, right):
    return lax.dot_general(left, right, (((1,), (0,)), ((), ())), preferred_element_type=F32)


def dot_nt(left, right):
    return lax.dot_general(left, right, (((1,), (1,)), ((), ())), preferred_element_type=F32)


def project_kernel(order_ref, act_ref, grad_ref, wi_ref, wo_ref, out_ref):
    del order_ref
    out_ref[...] = jnp.concatenate(
        [dot_nt(act_ref[...], wi_ref[...]), dot_nt(grad_ref[...], wo_ref[...])], axis=1
    )


def project(order, activations, out_grads, w_in, w_out, block):
    steps = order.shape[0]
    feats, hidden = activations.shape[1], out_grads.shape[1]
    return pl.pallas_call(
        project_kernel,
        out_shape=jax.ShapeDtypeStruct((steps * block, LANES), F32),
        grid_spec=pltpu.PrefetchScalarGridSpec(
            num_scalar_prefetch=1,
            grid=(steps,),
            in_specs=[
                pl.BlockSpec((block, feats), lambda i, order: (order[i], 0)),
                pl.BlockSpec((block, hidden), lambda i, order: (order[i], 0)),
                pl.BlockSpec(w_in.shape, lambda i, order: (0, 0)),
                pl.BlockSpec(w_out.shape, lambda i, order: (0, 0)),
            ],
            out_specs=pl.BlockSpec((block, LANES), lambda i, order: (i, 0)),
        ),
        compiler_params=pltpu.CompilerParams(vmem_limit_bytes=61 * MIB),
        cost_estimate=pl.CostEstimate(
            flops=2 * steps * block * (feats + hidden) * 4 * WINDOW,
            bytes_accessed=2 * steps * block * (feats + hidden),
            transcendentals=0,
        ),
    )(order, activations, out_grads, w_in, w_out)


def build_kernel(ranks, share, ex_block, n_sources, *refs):
    offs_ref, start_ref = refs[:2]
    sources = refs[2:2 + n_sources]
    ids_ref, pick_ref, b_ref = refs[2 + n_sources:5 + n_sources]
    high_ref, low_ref, inner_ref, sq_ref = refs[5 + n_sources:9 + n_sources]
    out_t, in_twice, ids_wide, rows, sketch = refs[9 + n_sources:]
    step = pl.program_id(0)
    half_ranks = pick_ref.shape[0]
    pairs = half_ranks // 2
    tokens = ids_ref.shape[1]

    @pl.when(step == 0)
    def _():
        lane = lax.broadcasted_iota(jnp.int32, (share, LANES), 1)
        block = 0
        for source in sources:
            for k in range(source.shape[0] // share):
                values = source[k * share:(k + 1) * share, :]
                at = pl.multiple_of(offs_ref[block] * share, share)
                block += 1
                high, low = split2(values)
                out_t[:, pl.ds(at, share)] = dot_nt(pick_ref[...], high) + dot_nt(pick_ref[...], low)
                in_twice[pl.ds(at, share), :] = jnp.where(
                    lane < ranks, values, pltpu.roll(values, ranks, 1)
                )
        ids_wide[...] = jnp.broadcast_to(ids_ref[...], ids_wide.shape)
        sq_ref[...] = jnp.zeros_like(sq_ref)

    slots = rows.shape[0]
    group = rows.shape[1] // pairs
    lane = lax.broadcasted_iota(jnp.int32, (LANES, LANES), 1)
    left_lanes = (lane < ranks).astype(F32).astype(BF16)
    right_lanes = (lane >= ranks).astype(F32).astype(BF16)

    def one_group(g, slot):
        number = step * (ex_block // group) + g
        start = start_ref[number]
        at = jnp.minimum(lax.div(start, LANES) * LANES, tokens - WINDOW)
        turn = lax.rem(WINDOW - (start - at), WINDOW)
        at = pl.multiple_of(at, LANES)
        out_win = pltpu.roll(out_t[:, pl.ds(at, WINDOW)], turn, 1)[:, :LANES]
        ids_win = pltpu.roll(ids_wide[:, pl.ds(at, WINDOW)], turn, 1)[:, :LANES]
        base = (number * group).astype(F32)
        lefts = ([], [])
        terms = split2(out_win)
        for e in range(group):
            mask = (ids_win == base + float(e)).astype(F32)
            mask = jnp.concatenate([mask] * (pairs // 8), axis=0).astype(BF16)
            for left, term in zip(lefts, terms):
                left.append(jnp.concatenate([term[:pairs] * mask, term[pairs:] * mask], axis=1))
        left = jnp.concatenate(lefts[0] + lefts[1], axis=0)
        high, low = split2(in_twice[pl.ds(start, LANES), :])
        right = jnp.concatenate(
            [
                jnp.concatenate([high * lanes, low * lanes], axis=1)
                for lanes in (left_lanes, right_lanes)
            ],
            axis=0,
        )
        res = dot_nn(left, right)
        top = group * pairs
        rows[slot] = (
            (res[:top, :LANES] + res[top:, :LANES]) + (res[:top, LANES:] + res[top:, LANES:])
        )
        to = pl.multiple_of(g * group, group)
        for pair in range(pairs):
            sketch[pl.ds(to, group), pair * LANES:(pair + 1) * LANES] = rows[
                slot, pl.ds(pair, group, stride=pairs), :
            ]

    @pl.loop(0, ex_block // group // slots)
    def _(turn):
        for slot in range(slots):
            one_group(turn * slots + slot, slot)

    values = sketch[...]
    high, low = split2(values)
    high_ref[...] = high
    low_ref[...] = low
    sq = jnp.sum((values * values).reshape(ex_block // 8, 8, -1), axis=0)
    total = sq[:, 0:LANES]
    for k in range(1, values.shape[1] // LANES):
        total = total + sq[:, k * LANES:(k + 1) * LANES]
    sq_ref[...] += total
    b_both = jnp.concatenate(split2(b_ref[...]), axis=0)
    count = b_ref.shape[0]
    both = (dot_nt(high, b_both) + dot_nt(low, b_both)).T
    inner_ref[...] = both[:count] + both[count:]


def build(offs, starts, sources, ids, pick, b, ranks, share):
    tokens = ids.shape[1]
    half_ranks = pick.shape[0]
    queries, comps = b.shape
    ex_block = 256
    group = 8
    whole = lambda i, *_: (0, 0)
    return pl.pallas_call(
        functools.partial(build_kernel, ranks, share, ex_block, len(sources)),
        out_shape=(
            jax.ShapeDtypeStruct((EX_DEV, comps), BF16),
            jax.ShapeDtypeStruct((EX_DEV, comps), BF16),
            jax.ShapeDtypeStruct((queries, EX_DEV), F32),
            jax.ShapeDtypeStruct((8, LANES), F32),
        ),
        grid_spec=pltpu.PrefetchScalarGridSpec(
            num_scalar_prefetch=2,
            grid=(EX_DEV // ex_block,),
            in_specs=[pl.BlockSpec(a.shape, whole) for a in (*sources, ids, pick, b)],
            out_specs=[
                pl.BlockSpec((ex_block, comps), lambda i, *_: (i, 0)),
                pl.BlockSpec((ex_block, comps), lambda i, *_: (i, 0)),
                pl.BlockSpec((queries, ex_block), lambda i, *_: (0, i)),
                pl.BlockSpec((8, LANES), whole),
            ],
            scratch_shapes=[
                pltpu.VMEM((half_ranks, tokens), F32),
                pltpu.VMEM((tokens, LANES), F32),
                pltpu.VMEM((8, tokens), F32),
                pltpu.VMEM((4, group * half_ranks // 2, LANES), F32),
                pltpu.VMEM((ex_block, comps), F32),
            ],
        ),
        compiler_params=pltpu.CompilerParams(vmem_limit_bytes=BUILD * MIB),
        cost_estimate=pl.CostEstimate(
            flops=12 * EX_DEV * half_ranks * WINDOW * 2 * LANES,
            bytes_accessed=4 * EX_DEV * comps + 4 * tokens * LANES,
            transcendentals=0,
        ),
    )(offs, starts, *sources, ids, pick, b)


def column(values, k):
    return values[:, k:k + 1]


def lanes_of(columns, shape):
    lane = lax.broadcasted_iota(jnp.int32, shape, 1)
    out = jnp.zeros(shape, F32)
    for k, one in enumerate(columns):
        out = jnp.where(lane == k, one, out)
    return out


def begin(first, examples, comps_all, mine, other, s_prev, state):
    total = mine + other
    inner, stats = total[:, :examples], total[:, examples:]
    norm = column(stats, 0)
    if first:
        damping = 0.1 * column(stats, 1) / (examples * comps_all)
        s, length, beta = inner, norm, None
    else:
        beta = norm / column(state, 0)
        s = inner + beta * s_prev
        length = norm + 2.0 * beta * column(stats, 1) + beta * beta * column(state, 1)
        damping = column(state, 2)
    bend = jnp.sum(s * s, axis=1, keepdims=True) / examples + damping * length
    return s, norm, length, damping, beta, norm / bend


def step_kernel(first, planes, examples, comps_all, *refs):
    refs = list(refs)
    take = lambda n: [refs.pop(0) for _ in range(n)]
    mine_ref, other_ref, r_ref = take(3)
    if not first:
        p_ref, x_ref, s_ref, y_ref, state_ref = take(5)
    highs, lows = take(planes), take(planes)
    msg_out, r_out, p_out, x_out, s_out, y_out, state_out = take(7)
    s_two, z_acc, stats_acc, scal = take(4)
    count, comps = r_ref.shape
    s, norm, length, damping, beta, alpha = begin(
        first, examples, comps_all, mine_ref[...], other_ref[...],
        None if first else s_ref[...], None if first else state_ref[...],
    )
    s_out[...] = s
    y_out[...] = alpha * s if first else y_ref[...] + alpha * s
    high, low = split2(s)
    s_two[0:count, :] = high
    s_two[count:2 * count, :] = low
    state_out[...] = lanes_of([norm, length, damping], state_out.shape)
    scal[...] = lanes_of([alpha, damping] + ([] if first else [beta]), scal.shape)
    z_acc[...] = jnp.zeros_like(z_acc)
    stats_acc[...] = jnp.zeros_like(stats_acc)
    block = 512

    @pl.loop(0, comps // block)
    def _(turn):
        at = pl.ds(pl.multiple_of(turn * block, block), block)
        alpha, damping = scal[:, 0:1], scal[:, 1:2]
        r = r_ref[:, at]
        if first:
            p = r
            x_out[:, at] = alpha * p
        else:
            p = r + scal[:, 2:3] * p_ref[:, at]
            x_out[:, at] = x_ref[:, at] + alpha * p
        p_out[:, at] = p
        q = jnp.zeros(r.shape, F32)
        for k in range(planes):
            part = slice(k * EX_DEV, (k + 1) * EX_DEV)
            both = dot_nn(s_two[:, part], highs[k][:, at])
            q = q + both[:count] + both[count:] + dot_nn(s_two[0:count, part], lows[k][:, at])
        r_new = r - alpha * (q / examples + damping * p)
        r_out[:, at] = r_new
        stacked = jnp.concatenate(split2(r_new), axis=0)
        for k in range(planes):
            part = slice(k * EX_DEV, (k + 1) * EX_DEV)
            z_acc[part, :] += dot_nt(highs[k][:, at], stacked) + dot_nt(lows[k][:, at], stacked)
        stats_acc[...] += lanes_of(
            [
                jnp.sum(r_new * r_new, axis=1, keepdims=True),
                jnp.sum(r_new * p, axis=1, keepdims=True),
            ],
            stats_acc.shape,
        )

    both = z_acc[...].T
    msg_out[:, 0:examples] = both[:count] + both[count:]
    msg_out[:, examples:] = stats_acc[...]


def one_step(first, examples, comps_all, mine, other, r, rest, highs, lows):
    planes = len(highs)
    count, comps = r.shape
    wide = jax.ShapeDtypeStruct((count, examples), F32)
    long = jax.ShapeDtypeStruct((count, comps), F32)
    small = jax.ShapeDtypeStruct((count, LANES), F32)
    message = jax.ShapeDtypeStruct((count, examples + LANES), F32)
    return pl.pallas_call(
        functools.partial(step_kernel, first, planes, examples, comps_all),
        out_shape=(message, long, long, long, wide, wide, small),
        scratch_shapes=[
            pltpu.VMEM((2 * count, examples), BF16),
            pltpu.VMEM((examples, 2 * count), F32),
            pltpu.VMEM((count, LANES), F32),
            pltpu.VMEM((count, LANES), F32),
        ],
        compiler_params=pltpu.CompilerParams(vmem_limit_bytes=STEP * MIB),
        cost_estimate=pl.CostEstimate(
            flops=12 * count * examples * comps,
            bytes_accessed=4 * examples * comps,
            transcendentals=0,
        ),
    )(mine, other, r, *rest, *highs, *lows)


def last_kernel(examples, comps_all, mine_ref, other_ref, r_ref, p_ref, x_ref, s_ref, y_ref, state_ref, x_out, y_out):
    s, _, _, _, beta, alpha = begin(
        False, examples, comps_all, mine_ref[...], other_ref[...], s_ref[...], state_ref[...]
    )
    scale = 1.0 / jnp.sqrt(F32(comps_all))
    y_out[...] = (y_ref[...] + alpha * s) * scale
    x_out[...] = x_ref[...] + alpha * (r_ref[...] + beta * p_ref[...])


def last_step(examples, comps_all, *arrays):
    x, y = arrays[4], arrays[6]
    return pl.pallas_call(
        functools.partial(last_kernel, examples, comps_all),
        out_shape=(jax.ShapeDtypeStruct(x.shape, F32), jax.ShapeDtypeStruct(y.shape, F32)),
        compiler_params=pltpu.CompilerParams(vmem_limit_bytes=STEP * MIB),
    )(*arrays)


def place_kernel(where_ref, *refs):
    parts, out_ref, held = refs[:-2], refs[-2], refs[-1]
    parts = parts[:2]
    rows = parts[0].shape[0]
    slot = 0
    for part in parts:
        for k in range(part.shape[0] // rows):
            at = pl.multiple_of(where_ref[1 + slot] * rows, rows)
            held[pl.ds(at, rows), :] = part[k * rows:(k + 1) * rows, :]
            slot += 1
    out_ref[...] = held[...].T


def place(where, own, others, out, shape):
    rows = own.shape[0] + others.shape[0]
    whole = lambda i, where: (0, 0)
    operands = [own, others] + ([] if out is None else [out])
    in_specs = [pl.BlockSpec(own.shape, whole), pl.BlockSpec(others.shape, whole)]
    if out is not None:
        in_specs.append(pl.BlockSpec(memory_space=pl.ANY))
    return pl.pallas_call(
        place_kernel,
        out_shape=jax.ShapeDtypeStruct(shape, F32),
        grid_spec=pltpu.PrefetchScalarGridSpec(
            num_scalar_prefetch=1,
            grid=(1,),
            in_specs=in_specs,
            out_specs=pl.BlockSpec((shape[0], rows), lambda i, where: (0, where[0])),
            scratch_shapes=[pltpu.VMEM((rows, own.shape[1]), F32)],
        ),
        input_output_aliases={} if out is None else {3: 0},
        compiler_params=pltpu.CompilerParams(vmem_limit_bytes=24 * MIB),
    )(where, *operands)


def per_device(n_dp, n_t, activations, out_grads, proj_in, proj_out, example_ids, queries):
    tokens = activations.shape[0]
    ranks = proj_in.shape[1]
    comps_all = proj_in.shape[1] * proj_out.shape[1]
    examples = EX_DEV * n_dp
    n_c = n_t // 2
    j = lax.axis_index("tensor")
    i = lax.axis_index("dp")
    chip, core = j // 2, j % 2

    def swap(values, mask):
        return lax.ppermute(values, "tensor", [(a, a ^ mask) for a in range(n_t)])

    def shift(values, by):
        return lax.ppermute(values, "dp", [(a, (a + by) % n_dp) for a in range(n_dp)])

    def tie(values, token):
        return lax.optimization_barrier((values, token))[0]

    near_chip = [chip ^ k for k in range(n_c)]

    q_chip = queries.shape[0] // n_c
    slots = [lax.dynamic_slice_in_dim(queries, near_chip[k] * q_chip, q_chip, 0) for k in range(n_c)]
    slots = [slots[0]] + [swap(slots[k], 2 * k) for k in range(1, n_c)]
    b = jnp.concatenate(slots, axis=1)

    group = 8
    bounds = group * jnp.arange(EX_DEV // group, dtype=jnp.int32)
    starts = jnp.sum((example_ids[0][None, :] < bounds[:, None]).astype(F32), axis=1)
    starts = jnp.minimum(starts, F32(tokens - LANES))
    id_rows = tokens // LANES
    extra = jnp.concatenate(
        [
            example_ids.astype(F32).reshape((id_rows, LANES)),
            jnp.pad(starts[None, :], ((0, 7), (0, LANES - EX_DEV // group))),
        ],
        axis=0,
    )

    share = tokens // n_t
    blocks = jnp.stack(near_chip).astype(jnp.int32) * 2
    w_in, w_out = proj_in.T, proj_out.T
    give = project(blocks + 1 - core, activations, out_grads, w_in, w_out, share)
    keep = project(tie(blocks + core, slots), activations, out_grads, w_in, w_out, share)
    kept = (keep + swap(give, 1)).reshape((n_c, share, LANES))
    own = kept[0]
    for k in range(1, n_c):
        own = own + swap(kept[k], 2 * k)

    rings = [jnp.concatenate([own, extra], axis=0)]
    for _ in range(n_dp - 1):
        rings.append(shift(rings[-1], 1))

    per = comps_all // ranks // n_t
    wanted = [(near_chip[k] * 2 + core) * per + a + ranks for k in range(n_c) for a in range(per)]
    wanted = jnp.stack(wanted[0::2] + wanted[1::2])
    pick = (wanted[:, None] == jnp.arange(LANES)[None, :]).astype(BF16)

    highs, lows, inners, squares = [], [], [], []
    for away in range(n_dp):
        piece = rings[away][:share]
        near = [piece] + [swap(piece, 2 * k) for k in range(1, n_c)]
        sources = near + [
            swap(part, 1) for part in (tie(near, squares[-1]) if squares else near)
        ]
        offs = jnp.stack(
            [near_chip[k] * 2 + which for which in (core, 1 - core) for k in range(n_c)]
        ).astype(jnp.int32)
        ids = rings[away][share:share + id_rows].reshape((1, tokens))
        first = rings[away][share + id_rows, :EX_DEV // group].astype(jnp.int32)
        high, low, inner, square = build(offs, first, sources, ids, pick, b, ranks, share)
        highs.append(high)
        lows.append(low)
        inners.append(inner)
        squares.append(square)

    square = jnp.sum(jnp.stack(squares))
    stats = jnp.concatenate(
        [
            jnp.sum(b * b, axis=1, keepdims=True),
            jnp.broadcast_to(square, (q_chip, 1)),
            jnp.zeros((q_chip, LANES - 2), F32),
        ],
        axis=1,
    )
    message = jnp.concatenate(inners + [stats], axis=1)
    r, rest = b, ()
    for step in range(ITERS - 1):
        other = swap(message, 1)
        message, r, p, x, s, y, state = one_step(
            step == 0, examples, comps_all, message, other, r, rest, highs, lows
        )
        rest = (p, x, s, y, state)
    other = swap(message, 1)
    x, y = last_step(examples, comps_all, message, other, r, *rest)

    per_slot = comps_all // n_t
    own_x = x[:, :per_slot]
    others_x = jnp.concatenate(
        [swap(x[:, k * per_slot:(k + 1) * per_slot], 2 * k) for k in range(1, n_c)], axis=0
    )
    out = None
    for away in range(n_dp):
        if away:
            own_x = shift(own_x, 1)
            others_x = tie(others_x, own_x)
            if away == 2:
                y = tie(y, others_x)
            others_x = shift(others_x, 1)
        where = jnp.stack([(i - away) % n_dp] + near_chip).astype(jnp.int32)
        out = place(where, own_x, others_x, out, (per_slot, n_dp * n_c * q_chip))

    part_q = q_chip // 2
    mine = lax.dynamic_slice_in_dim(y, core * part_q, part_q, 0)
    by_plane = jnp.zeros((n_dp, part_q, EX_DEV), F32)
    for away in range(n_dp):
        part = mine[:, away * EX_DEV:(away + 1) * EX_DEV]
        if away:
            part = shift(part, -away)
        by_plane = lax.dynamic_update_slice(by_plane, part[None], ((i + away) % n_dp, 0, 0))
    by_chip = jnp.zeros((n_c, part_q, EX_DEV), F32)
    for k in range(n_c):
        part = lax.dynamic_slice_in_dim(by_plane, near_chip[k], 1, 0)
        if k:
            part = swap(part, 2 * k)
        by_chip = lax.dynamic_update_slice(by_chip, part, (near_chip[k], 0, 0))
    n_half = n_c // 2
    give = lax.dynamic_slice_in_dim(by_chip, (1 - core) * n_half, n_half, 0)
    keep = lax.dynamic_slice_in_dim(by_chip, core * n_half, n_half, 0)
    came = swap(give, 1)
    scores = jnp.zeros((n_half, 2, part_q, EX_DEV), F32)
    scores = lax.dynamic_update_slice(scores, keep[:, None], (0, core, 0, 0))
    scores = lax.dynamic_update_slice(scores, came[:, None], (0, 1 - core, 0, 0))
    return (out, scores.reshape((n_half * q_chip, EX_DEV)))


def solution(mesh):
    in_specs = (
        P("dp", "tensor"),
        P("dp", "tensor"),
        P("tensor", None),
        P("tensor", None),
        P("dp", None),
        P("dp", "tensor"),
    )
    out_specs = (P("tensor", None), P("tensor", "dp"))
    body = functools.partial(per_device, mesh.shape["dp"], mesh.shape["tensor"])
    return jax.shard_map(body, mesh=mesh, in_specs=in_specs, out_specs=out_specs, check_vma=False)
```

```python
import functools

import jax
import jax.numpy as jnp
from jax import lax
from jax.experimental import pallas as pl
from jax.experimental.pallas import tpu as pltpu
from jax.sharding import PartitionSpec as P

ITERS = 4
EX_DEV = 512
LANES = 128
WINDOW = 256
PARTS = 4
F32 = jnp.float32
BF16 = jnp.bfloat16
MIB = 1024 * 1024
BUILD = 24
STEP = 24


def split2(values):
    high = values.astype(BF16)
    low = (values - high.astype(F32)).astype(BF16)
    return high, low


def dot_nn(left, right):
    return lax.dot_general(left, right, (((1,), (0,)), ((), ())), preferred_element_type=F32)


def dot_nt(left, right):
    return lax.dot_general(left, right, (((1,), (1,)), ((), ())), preferred_element_type=F32)


def project_kernel(order_ref, *refs):
    del order_ref
    acts, grads = refs[:PARTS], refs[PARTS:2 * PARTS]
    wi_ref, wo_ref, out_ref = refs[2 * PARTS:]
    rows = acts[0].shape[0]
    for part, (act_ref, grad_ref) in enumerate(zip(acts, grads)):
        out_ref[part * rows:(part + 1) * rows, :] = jnp.concatenate(
            [dot_nt(act_ref[...], wi_ref[...]), dot_nt(grad_ref[...], wo_ref[...])], axis=1
        )


def project(order, activations, out_grads, w_in, w_out, block):
    steps = order.shape[0]
    feats, hidden = activations.shape[1], out_grads.shape[1]
    rows = block // PARTS

    def parts(width):
        return [
            pl.BlockSpec((rows, width), lambda i, order, part=part: (order[i] * PARTS + part, 0))
            for part in range(PARTS)
        ]

    return pl.pallas_call(
        project_kernel,
        out_shape=jax.ShapeDtypeStruct((steps * block, LANES), F32),
        grid_spec=pltpu.PrefetchScalarGridSpec(
            num_scalar_prefetch=1,
            grid=(steps,),
            in_specs=parts(feats) + parts(hidden) + [
                pl.BlockSpec(w_in.shape, lambda i, order: (0, 0)),
                pl.BlockSpec(w_out.shape, lambda i, order: (0, 0)),
            ],
            out_specs=pl.BlockSpec((block, LANES), lambda i, order: (i, 0)),
        ),
        compiler_params=pltpu.CompilerParams(vmem_limit_bytes=61 * MIB),
        cost_estimate=pl.CostEstimate(
            flops=2 * steps * block * (feats + hidden) * 4 * WINDOW,
            bytes_accessed=2 * steps * block * (feats + hidden),
            transcendentals=0,
        ),
    )(order, *[activations] * PARTS, *[out_grads] * PARTS, w_in, w_out)


def build_kernel(ranks, share, ex_block, n_sources, *refs):
    offs_ref, start_ref = refs[:2]
    sources = refs[2:2 + n_sources]
    ids_ref, pick_ref, b_ref = refs[2 + n_sources:5 + n_sources]
    high_ref, low_ref, inner_ref, sq_ref = refs[5 + n_sources:9 + n_sources]
    out_t, in_twice, ids_wide, rows, sketch = refs[9 + n_sources:]
    step = pl.program_id(0)
    half_ranks = pick_ref.shape[0]
    pairs = half_ranks // 2
    tokens = ids_ref.shape[1]

    @pl.when(step == 0)
    def _():
        lane = lax.broadcasted_iota(jnp.int32, (share, LANES), 1)
        block = 0
        for source in sources:
            for k in range(source.shape[0] // share):
                values = source[k * share:(k + 1) * share, :]
                at = pl.multiple_of(offs_ref[block] * share, share)
                block += 1
                high, low = split2(values)
                out_t[:, pl.ds(at, share)] = dot_nt(pick_ref[...], high) + dot_nt(pick_ref[...], low)
                in_twice[pl.ds(at, share), :] = jnp.where(
                    lane < ranks, values, pltpu.roll(values, ranks, 1)
                )
        ids_wide[...] = jnp.broadcast_to(ids_ref[...], ids_wide.shape)
        sq_ref[...] = jnp.zeros_like(sq_ref)

    slots = rows.shape[0]
    group = rows.shape[1] // pairs
    lane = lax.broadcasted_iota(jnp.int32, (LANES, LANES), 1)
    left_lanes = (lane < ranks).astype(F32).astype(BF16)
    right_lanes = (lane >= ranks).astype(F32).astype(BF16)

    def one_group(g, slot):
        number = step * (ex_block // group) + g
        start = start_ref[number]
        at = jnp.minimum(lax.div(start, LANES) * LANES, tokens - WINDOW)
        turn = lax.rem(WINDOW - (start - at), WINDOW)
        at = pl.multiple_of(at, LANES)
        out_win = pltpu.roll(out_t[:, pl.ds(at, WINDOW)], turn, 1)[:, :LANES]
        ids_win = pltpu.roll(ids_wide[:, pl.ds(at, WINDOW)], turn, 1)[:, :LANES]
        base = (number * group).astype(F32)
        lefts = ([], [])
        terms = split2(out_win)
        for e in range(group):
            mask = (ids_win == base + float(e)).astype(F32)
            mask = jnp.concatenate([mask] * (pairs // 8), axis=0).astype(BF16)
            for left, term in zip(lefts, terms):
                left.append(jnp.concatenate([term[:pairs] * mask, term[pairs:] * mask], axis=1))
        left = jnp.concatenate(lefts[0] + lefts[1], axis=0)
        high, low = split2(in_twice[pl.ds(start, LANES), :])
        right = jnp.concatenate(
            [
                jnp.concatenate([high * lanes, low * lanes], axis=1)
                for lanes in (left_lanes, right_lanes)
            ],
            axis=0,
        )
        res = dot_nn(left, right)
        top = group * pairs
        rows[slot] = (
            (res[:top, :LANES] + res[top:, :LANES]) + (res[:top, LANES:] + res[top:, LANES:])
        )
        to = pl.multiple_of(g * group, group)
        for pair in range(pairs):
            sketch[pl.ds(to, group), pair * LANES:(pair + 1) * LANES] = rows[
                slot, pl.ds(pair, group, stride=pairs), :
            ]

    @pl.loop(0, ex_block // group // slots)
    def _(turn):
        for slot in range(slots):
            one_group(turn * slots + slot, slot)

    values = sketch[...]
    high, low = split2(values)
    high_ref[...] = high
    low_ref[...] = low
    sq = jnp.sum((values * values).reshape(ex_block // 8, 8, -1), axis=0)
    total = sq[:, 0:LANES]
    for k in range(1, values.shape[1] // LANES):
        total = total + sq[:, k * LANES:(k + 1) * LANES]
    sq_ref[...] += total
    b_both = jnp.concatenate(split2(b_ref[...]), axis=0)
    count = b_ref.shape[0]
    both = (dot_nt(high, b_both) + dot_nt(low, b_both)).T
    inner_ref[...] = both[:count] + both[count:]


def build(offs, starts, sources, ids, pick, b, ranks, share):
    tokens = ids.shape[1]
    half_ranks = pick.shape[0]
    queries, comps = b.shape
    ex_block = 256
    group = 8
    whole = lambda i, *_: (0, 0)
    return pl.pallas_call(
        functools.partial(build_kernel, ranks, share, ex_block, len(sources)),
        out_shape=(
            jax.ShapeDtypeStruct((EX_DEV, comps), BF16),
            jax.ShapeDtypeStruct((EX_DEV, comps), BF16),
            jax.ShapeDtypeStruct((queries, EX_DEV), F32),
            jax.ShapeDtypeStruct((8, LANES), F32),
        ),
        grid_spec=pltpu.PrefetchScalarGridSpec(
            num_scalar_prefetch=2,
            grid=(EX_DEV // ex_block,),
            in_specs=[pl.BlockSpec(a.shape, whole) for a in (*sources, ids, pick, b)],
            out_specs=[
                pl.BlockSpec((ex_block, comps), lambda i, *_: (i, 0)),
                pl.BlockSpec((ex_block, comps), lambda i, *_: (i, 0)),
                pl.BlockSpec((queries, ex_block), lambda i, *_: (0, i)),
                pl.BlockSpec((8, LANES), whole),
            ],
            scratch_shapes=[
                pltpu.VMEM((half_ranks, tokens), F32),
                pltpu.VMEM((tokens, LANES), F32),
                pltpu.VMEM((8, tokens), F32),
                pltpu.VMEM((4, group * half_ranks // 2, LANES), F32),
                pltpu.VMEM((ex_block, comps), F32),
            ],
        ),
        compiler_params=pltpu.CompilerParams(vmem_limit_bytes=BUILD * MIB),
        cost_estimate=pl.CostEstimate(
            flops=12 * EX_DEV * half_ranks * WINDOW * 2 * LANES,
            bytes_accessed=4 * EX_DEV * comps + 4 * tokens * LANES,
            transcendentals=0,
        ),
    )(offs, starts, *sources, ids, pick, b)


def join_kernel(planes, *refs):
    inners, squares, b_ref, out_ref = refs[:planes], refs[planes:2 * planes], refs[-2], refs[-1]
    for k, inner in enumerate(inners):
        out_ref[:, k * EX_DEV:(k + 1) * EX_DEV] = inner[...]
    total = squares[0][...]
    for square in squares[1:]:
        total = total + square[...]
    total = jnp.sum(jnp.sum(total, axis=1, keepdims=True), axis=0, keepdims=True)
    b = b_ref[...]
    norm = jnp.sum(b * b, axis=1, keepdims=True)
    shape = (b.shape[0], LANES)
    out_ref[:, planes * EX_DEV:] = lanes_of([norm, total], shape)


def join(inners, squares, b):
    planes = len(inners)
    return pl.pallas_call(
        functools.partial(join_kernel, planes),
        out_shape=jax.ShapeDtypeStruct((b.shape[0], planes * EX_DEV + LANES), F32),
        compiler_params=pltpu.CompilerParams(vmem_limit_bytes=STEP * MIB),
    )(*inners, *squares, b)


def column(values, k):
    return values[:, k:k + 1]


def lanes_of(columns, shape):
    lane = lax.broadcasted_iota(jnp.int32, shape, 1)
    out = jnp.zeros(shape, F32)
    for k, one in enumerate(columns):
        out = jnp.where(lane == k, one, out)
    return out


def begin(first, examples, comps_all, mine, other, s_prev, state):
    total = mine + other
    inner, stats = total[:, :examples], total[:, examples:]
    norm = column(stats, 0)
    if first:
        damping = 0.1 * column(stats, 1) / (examples * comps_all)
        s, length, beta = inner, norm, None
    else:
        beta = norm / column(state, 0)
        s = inner + beta * s_prev
        length = norm + 2.0 * beta * column(stats, 1) + beta * beta * column(state, 1)
        damping = column(state, 2)
    bend = jnp.sum(s * s, axis=1, keepdims=True) / examples + damping * length
    return s, norm, length, damping, beta, norm / bend


def step_kernel(first, planes, examples, comps_all, *refs):
    refs = list(refs)
    take = lambda n: [refs.pop(0) for _ in range(n)]
    mine_ref, other_ref, r_ref = take(3)
    if not first:
        p_ref, x_ref, s_ref, y_ref, state_ref = take(5)
    highs, lows = take(planes), take(planes)
    msg_out, r_out, p_out, x_out, s_out, y_out, state_out = take(7)
    s_two, z_acc, stats_acc, scal = take(4)
    count, comps = r_ref.shape
    s, norm, length, damping, beta, alpha = begin(
        first, examples, comps_all, mine_ref[...], other_ref[...],
        None if first else s_ref[...], None if first else state_ref[...],
    )
    s_out[...] = s
    y_out[...] = alpha * s if first else y_ref[...] + alpha * s
    high, low = split2(s)
    s_two[0:count, :] = high
    s_two[count:2 * count, :] = low
    state_out[...] = lanes_of([norm, length, damping], state_out.shape)
    scal[...] = lanes_of([alpha, damping] + ([] if first else [beta]), scal.shape)
    z_acc[...] = jnp.zeros_like(z_acc)
    stats_acc[...] = jnp.zeros_like(stats_acc)
    block = 512

    @pl.loop(0, comps // block)
    def _(turn):
        at = pl.ds(pl.multiple_of(turn * block, block), block)
        alpha, damping = scal[:, 0:1], scal[:, 1:2]
        r = r_ref[:, at]
        if first:
            p = r
            x_out[:, at] = alpha * p
        else:
            p = r + scal[:, 2:3] * p_ref[:, at]
            x_out[:, at] = x_ref[:, at] + alpha * p
        p_out[:, at] = p
        q = jnp.zeros(r.shape, F32)
        for k in range(planes):
            part = slice(k * EX_DEV, (k + 1) * EX_DEV)
            both = dot_nn(s_two[:, part], highs[k][:, at])
            q = q + both[:count] + both[count:] + dot_nn(s_two[0:count, part], lows[k][:, at])
        r_new = r - alpha * (q / examples + damping * p)
        r_out[:, at] = r_new
        stacked = jnp.concatenate(split2(r_new), axis=0)
        for k in range(planes):
            part = slice(k * EX_DEV, (k + 1) * EX_DEV)
            z_acc[part, :] += dot_nt(highs[k][:, at], stacked) + dot_nt(lows[k][:, at], stacked)
        stats_acc[...] += lanes_of(
            [
                jnp.sum(r_new * r_new, axis=1, keepdims=True),
                jnp.sum(r_new * p, axis=1, keepdims=True),
            ],
            stats_acc.shape,
        )

    both = z_acc[...].T
    msg_out[:, 0:examples] = both[:count] + both[count:]
    msg_out[:, examples:] = stats_acc[...]


def one_step(first, examples, comps_all, mine, other, r, rest, highs, lows):
    planes = len(highs)
    count, comps = r.shape
    wide = jax.ShapeDtypeStruct((count, examples), F32)
    long = jax.ShapeDtypeStruct((count, comps), F32)
    small = jax.ShapeDtypeStruct((count, LANES), F32)
    message = jax.ShapeDtypeStruct((count, examples + LANES), F32)
    return pl.pallas_call(
        functools.partial(step_kernel, first, planes, examples, comps_all),
        out_shape=(message, long, long, long, wide, wide, small),
        scratch_shapes=[
            pltpu.VMEM((2 * count, examples), BF16),
            pltpu.VMEM((examples, 2 * count), F32),
            pltpu.VMEM((count, LANES), F32),
            pltpu.VMEM((count, LANES), F32),
        ],
        compiler_params=pltpu.CompilerParams(vmem_limit_bytes=STEP * MIB),
        cost_estimate=pl.CostEstimate(
            flops=12 * count * examples * comps,
            bytes_accessed=4 * examples * comps,
            transcendentals=0,
        ),
    )(mine, other, r, *rest, *highs, *lows)


def last_kernel(examples, comps_all, mine_ref, other_ref, r_ref, p_ref, x_ref, s_ref, y_ref, state_ref, x_out, y_out):
    s, _, _, _, beta, alpha = begin(
        False, examples, comps_all, mine_ref[...], other_ref[...], s_ref[...], state_ref[...]
    )
    scale = 1.0 / jnp.sqrt(F32(comps_all))
    y_out[...] = (y_ref[...] + alpha * s) * scale
    x_out[...] = x_ref[...] + alpha * (r_ref[...] + beta * p_ref[...])


def last_step(examples, comps_all, *arrays):
    x, y = arrays[4], arrays[6]
    return pl.pallas_call(
        functools.partial(last_kernel, examples, comps_all),
        out_shape=(jax.ShapeDtypeStruct(x.shape, F32), jax.ShapeDtypeStruct(y.shape, F32)),
        compiler_params=pltpu.CompilerParams(vmem_limit_bytes=STEP * MIB),
    )(*arrays)


def place_kernel(where_ref, *refs):
    parts, out_ref, held = refs[:-2], refs[-2], refs[-1]
    parts = parts[:2]
    rows = parts[0].shape[0]
    slot = 0
    for part in parts:
        for k in range(part.shape[0] // rows):
            at = pl.multiple_of(where_ref[1 + slot] * rows, rows)
            held[pl.ds(at, rows), :] = part[k * rows:(k + 1) * rows, :]
            slot += 1
    out_ref[...] = held[...].T


def place(where, own, others, out, shape):
    rows = own.shape[0] + others.shape[0]
    whole = lambda i, where: (0, 0)
    operands = [own, others] + ([] if out is None else [out])
    in_specs = [pl.BlockSpec(own.shape, whole), pl.BlockSpec(others.shape, whole)]
    if out is not None:
        in_specs.append(pl.BlockSpec(memory_space=pl.ANY))
    return pl.pallas_call(
        place_kernel,
        out_shape=jax.ShapeDtypeStruct(shape, F32),
        grid_spec=pltpu.PrefetchScalarGridSpec(
            num_scalar_prefetch=1,
            grid=(1,),
            in_specs=in_specs,
            out_specs=pl.BlockSpec((shape[0], rows), lambda i, where: (0, where[0])),
            scratch_shapes=[pltpu.VMEM((rows, own.shape[1]), F32)],
        ),
        input_output_aliases={} if out is None else {3: 0},
        compiler_params=pltpu.CompilerParams(vmem_limit_bytes=24 * MIB),
    )(where, *operands)


def per_device(n_dp, n_t, activations, out_grads, proj_in, proj_out, example_ids, queries):
    tokens = activations.shape[0]
    ranks = proj_in.shape[1]
    comps_all = proj_in.shape[1] * proj_out.shape[1]
    examples = EX_DEV * n_dp
    n_c = n_t // 2
    j = lax.axis_index("tensor")
    i = lax.axis_index("dp")
    chip, core = j // 2, j % 2

    def swap(values, mask):
        return lax.ppermute(values, "tensor", [(a, a ^ mask) for a in range(n_t)])

    def shift(values, by):
        return lax.ppermute(values, "dp", [(a, (a + by) % n_dp) for a in range(n_dp)])

    def tie(values, token):
        return lax.optimization_barrier((values, token))[0]

    near_chip = [chip ^ k for k in range(n_c)]

    q_chip = queries.shape[0] // n_c
    slots = [lax.dynamic_slice_in_dim(queries, near_chip[k] * q_chip, q_chip, 0) for k in range(n_c)]
    slots = [slots[0]] + [swap(slots[k], 2 * k) for k in range(1, n_c)]
    b = jnp.concatenate(slots, axis=1)

    group = 8
    bounds = group * jnp.arange(EX_DEV // group, dtype=jnp.int32)
    starts = jnp.sum((example_ids[0][None, :] < bounds[:, None]).astype(F32), axis=1)
    starts = jnp.minimum(starts, F32(tokens - LANES))
    id_rows = tokens // LANES
    extra = jnp.concatenate(
        [
            example_ids.astype(F32).reshape((id_rows, LANES)),
            jnp.pad(starts[None, :], ((0, 7), (0, LANES - EX_DEV // group))),
        ],
        axis=0,
    )
    extras = [extra] + [shift(extra, away) for away in range(1, n_dp)]
    plane_ids = [one[:id_rows].reshape((1, tokens)) for one in extras]
    firsts = [one[id_rows, :EX_DEV // group].astype(jnp.int32) for one in extras]

    share = tokens // n_t
    blocks = jnp.stack(near_chip).astype(jnp.int32) * 2
    w_in, w_out = proj_in.T, proj_out.T
    give = project(blocks + 1 - core, activations, out_grads, w_in, w_out, share)
    keep = project(blocks + core, activations, out_grads, w_in, w_out, share)
    kept = (keep + swap(give, 1)).reshape((n_c, share, LANES))
    own = kept[0]
    for k in range(1, n_c):
        own = own + swap(kept[k], 2 * k)

    rings = [own]
    for _ in range(n_dp - 1):
        rings.append(shift(rings[-1], 1))

    per = comps_all // ranks // n_t
    wanted = [(near_chip[k] * 2 + core) * per + a + ranks for k in range(n_c) for a in range(per)]
    wanted = jnp.stack(wanted[0::2] + wanted[1::2])
    pick = (wanted[:, None] == jnp.arange(LANES)[None, :]).astype(BF16)

    offs = jnp.stack(
        [near_chip[k] * 2 + which for which in (core, 1 - core) for k in range(n_c)]
    ).astype(jnp.int32)
    offs, pick, b, plane_ids, firsts = lax.optimization_barrier((offs, pick, b, plane_ids, firsts))

    highs, lows, inners, squares = [], [], [], []
    for away in range(n_dp):
        piece = rings[away]
        near = [piece] + [swap(piece, 2 * k) for k in range(1, n_c)]
        sources = near + [
            swap(part, 1) for part in (tie(near, squares[-1]) if squares else near)
        ]
        high, low, inner, square = build(
            offs, firsts[away], sources, plane_ids[away], pick, b, ranks, share
        )
        highs.append(high)
        lows.append(low)
        inners.append(inner)
        squares.append(square)

    message = join(inners, squares, b)
    r, rest = b, ()
    for step in range(ITERS - 1):
        other = swap(message, 1)
        message, r, p, x, s, y, state = one_step(
            step == 0, examples, comps_all, message, other, r, rest, highs, lows
        )
        rest = (p, x, s, y, state)
    other = swap(message, 1)
    x, y = last_step(examples, comps_all, message, other, r, *rest)

    n_half = n_c // 2
    per_slot = comps_all // n_t

    def send(values, to):
        pairs = [
            (di * n_t + 2 * c + c // n_half, to(di, c, c // n_half))
            for di in range(n_dp) for c in range(n_c)
        ]
        return lax.ppermute(values, ("dp", "tensor"), pairs)

    others_x = jnp.concatenate(
        [swap(x[:, k * per_slot:(k + 1) * per_slot], 2 * k) for k in range(1, n_c)], axis=0
    )
    own_x = x[:, :per_slot]
    by_plane = jnp.zeros((n_dp, q_chip, EX_DEV), F32)
    for away in range(n_dp):
        part = y[:, away * EX_DEV:(away + 1) * EX_DEV]
        if away:
            part = send(part, lambda di, c, h: ((di - away) % n_dp) * n_t + 2 * c + h)
        by_plane = lax.dynamic_update_slice(by_plane, part[None], ((i + away) % n_dp, 0, 0))
    by_chip = jnp.zeros((n_c, q_chip, EX_DEV), F32)
    for k in range(n_c):
        part = lax.dynamic_slice_in_dim(by_plane, near_chip[k], 1, 0)
        if k:
            part = send(part, lambda di, c, h: di * n_t + 2 * (c ^ k) + h)
        by_chip = lax.dynamic_update_slice(by_chip, part, (near_chip[k], 0, 0))
    scores = lax.dynamic_slice_in_dim(by_chip, core * n_half, n_half, 0)

    out = None
    for away in range(n_dp):
        if away:
            own_x = shift(own_x, 1)
            others_x = tie(others_x, (own_x, by_plane if away == 1 else scores))
            others_x = shift(others_x, 1)
        where = jnp.stack([(i - away) % n_dp] + near_chip).astype(jnp.int32)
        out = place(where, own_x, others_x, out, (per_slot, n_dp * n_c * q_chip))
    return (out, scores.reshape((n_half * q_chip, EX_DEV)))


def solution(mesh):
    in_specs = (
        P("dp", "tensor"),
        P("dp", "tensor"),
        P("tensor", None),
        P("tensor", None),
        P("dp", None),
        P("dp", "tensor"),
    )
    out_specs = (P("tensor", None), P("tensor", "dp"))
    body = functools.partial(per_device, mesh.shape["dp"], mesh.shape["tensor"])
    return jax.shard_map(body, mesh=mesh, in_specs=in_specs, out_specs=out_specs, check_vma=False)
```

```python
import functools

import jax
import jax.numpy as jnp
from jax import lax
from jax.experimental import pallas as pl
from jax.experimental.pallas import tpu as pltpu
from jax.sharding import PartitionSpec as P

ITERS = 4
EX_DEV = 512
LANES = 128
WINDOW = 256
PARTS = 4
F32 = jnp.float32
BF16 = jnp.bfloat16
MIB = 1024 * 1024
BUILD = 24
STEP = 24


def split2(values):
    high = values.astype(BF16)
    low = (values - high.astype(F32)).astype(BF16)
    return high, low


def dot_nn(left, right):
    return lax.dot_general(left, right, (((1,), (0,)), ((), ())), preferred_element_type=F32)


def dot_nt(left, right):
    return lax.dot_general(left, right, (((1,), (1,)), ((), ())), preferred_element_type=F32)


def project_kernel(order_ref, *refs):
    del order_ref
    acts, grads = refs[:PARTS], refs[PARTS:2 * PARTS]
    wi_ref, wo_ref, out_ref = refs[2 * PARTS:]
    rows = acts[0].shape[0]
    for part, (act_ref, grad_ref) in enumerate(zip(acts, grads)):
        out_ref[part * rows:(part + 1) * rows, :] = jnp.concatenate(
            [dot_nt(act_ref[...], wi_ref[...]), dot_nt(grad_ref[...], wo_ref[...])], axis=1
        )


def project(order, activations, out_grads, w_in, w_out, block):
    steps = order.shape[0]
    feats, hidden = activations.shape[1], out_grads.shape[1]
    rows = block // PARTS

    def parts(width):
        return [
            pl.BlockSpec((rows, width), lambda i, order, part=part: (order[i] * PARTS + part, 0))
            for part in range(PARTS)
        ]

    return pl.pallas_call(
        project_kernel,
        out_shape=jax.ShapeDtypeStruct((steps * block, LANES), F32),
        grid_spec=pltpu.PrefetchScalarGridSpec(
            num_scalar_prefetch=1,
            grid=(steps,),
            in_specs=parts(feats) + parts(hidden) + [
                pl.BlockSpec(w_in.shape, lambda i, order: (0, 0)),
                pl.BlockSpec(w_out.shape, lambda i, order: (0, 0)),
            ],
            out_specs=pl.BlockSpec((block, LANES), lambda i, order: (i, 0)),
        ),
        compiler_params=pltpu.CompilerParams(vmem_limit_bytes=61 * MIB),
        cost_estimate=pl.CostEstimate(
            flops=2 * steps * block * (feats + hidden) * 4 * WINDOW,
            bytes_accessed=2 * steps * block * (feats + hidden),
            transcendentals=0,
        ),
    )(order, *[activations] * PARTS, *[out_grads] * PARTS, w_in, w_out)


def build_kernel(ranks, share, ex_block, n_sources, *refs):
    offs_ref, start_ref = refs[:2]
    sources = refs[2:2 + n_sources]
    ids_ref, pick_ref = refs[2 + n_sources:4 + n_sources]
    high_ref, low_ref, sq_ref = refs[4 + n_sources:7 + n_sources]
    out_t, in_twice, ids_wide, rows, sketch = refs[7 + n_sources:]
    step = pl.program_id(0)
    half_ranks = pick_ref.shape[0]
    pairs = half_ranks // 2
    tokens = ids_ref.shape[1]

    @pl.when(step == 0)
    def _():
        lane = lax.broadcasted_iota(jnp.int32, (share, LANES), 1)
        block = 0
        for source in sources:
            for k in range(source.shape[0] // share):
                values = source[k * share:(k + 1) * share, :]
                at = pl.multiple_of(offs_ref[block] * share, share)
                block += 1
                high, low = split2(values)
                out_t[:, pl.ds(at, share)] = dot_nt(pick_ref[...], high) + dot_nt(pick_ref[...], low)
                in_twice[pl.ds(at, share), :] = jnp.where(
                    lane < ranks, values, pltpu.roll(values, ranks, 1)
                )
        ids_wide[...] = jnp.broadcast_to(ids_ref[...], ids_wide.shape)
        sq_ref[...] = jnp.zeros_like(sq_ref)

    slots = rows.shape[0]
    group = rows.shape[1] // pairs
    lane = lax.broadcasted_iota(jnp.int32, (LANES, LANES), 1)
    left_lanes = (lane < ranks).astype(F32).astype(BF16)
    right_lanes = (lane >= ranks).astype(F32).astype(BF16)

    def one_group(g, slot):
        number = step * (ex_block // group) + g
        start = start_ref[number]
        at = jnp.minimum(lax.div(start, LANES) * LANES, tokens - WINDOW)
        turn = lax.rem(WINDOW - (start - at), WINDOW)
        at = pl.multiple_of(at, LANES)
        out_win = pltpu.roll(out_t[:, pl.ds(at, WINDOW)], turn, 1)[:, :LANES]
        ids_win = pltpu.roll(ids_wide[:, pl.ds(at, WINDOW)], turn, 1)[:, :LANES]
        base = (number * group).astype(F32)
        lefts = ([], [])
        terms = split2(out_win)
        for e in range(group):
            mask = (ids_win == base + float(e)).astype(F32)
            mask = jnp.concatenate([mask] * (pairs // 8), axis=0).astype(BF16)
            for left, term in zip(lefts, terms):
                left.append(jnp.concatenate([term[:pairs] * mask, term[pairs:] * mask], axis=1))
        left = jnp.concatenate(lefts[0] + lefts[1], axis=0)
        high, low = split2(in_twice[pl.ds(start, LANES), :])
        right = jnp.concatenate(
            [
                jnp.concatenate([high * lanes, low * lanes], axis=1)
                for lanes in (left_lanes, right_lanes)
            ],
            axis=0,
        )
        res = dot_nn(left, right)
        top = group * pairs
        rows[slot] = (
            (res[:top, :LANES] + res[top:, :LANES]) + (res[:top, LANES:] + res[top:, LANES:])
        )
        to = pl.multiple_of(g * group, group)
        for pair in range(pairs):
            sketch[pl.ds(to, group), pair * LANES:(pair + 1) * LANES] = rows[
                slot, pl.ds(pair, group, stride=pairs), :
            ]

    @pl.loop(0, ex_block // group // slots)
    def _(turn):
        for slot in range(slots):
            one_group(turn * slots + slot, slot)

    values = sketch[...]
    high, low = split2(values)
    high_ref[...] = high
    low_ref[...] = low
    sq = jnp.sum((values * values).reshape(ex_block // 8, 8, -1), axis=0)
    total = sq[:, 0:LANES]
    for k in range(1, values.shape[1] // LANES):
        total = total + sq[:, k * LANES:(k + 1) * LANES]
    sq_ref[...] += total


def build(offs, starts, sources, ids, pick, ranks, share, comps):
    tokens = ids.shape[1]
    half_ranks = pick.shape[0]
    ex_block = 256
    group = 8
    whole = lambda i, *_: (0, 0)
    return pl.pallas_call(
        functools.partial(build_kernel, ranks, share, ex_block, len(sources)),
        out_shape=(
            jax.ShapeDtypeStruct((EX_DEV, comps), BF16),
            jax.ShapeDtypeStruct((EX_DEV, comps), BF16),
            jax.ShapeDtypeStruct((8, LANES), F32),
        ),
        grid_spec=pltpu.PrefetchScalarGridSpec(
            num_scalar_prefetch=2,
            grid=(EX_DEV // ex_block,),
            in_specs=[pl.BlockSpec(a.shape, whole) for a in (*sources, ids, pick)],
            out_specs=[
                pl.BlockSpec((ex_block, comps), lambda i, *_: (i, 0)),
                pl.BlockSpec((ex_block, comps), lambda i, *_: (i, 0)),
                pl.BlockSpec((8, LANES), whole),
            ],
            scratch_shapes=[
                pltpu.VMEM((half_ranks, tokens), F32),
                pltpu.VMEM((tokens, LANES), F32),
                pltpu.VMEM((8, tokens), F32),
                pltpu.VMEM((4, group * half_ranks // 2, LANES), F32),
                pltpu.VMEM((ex_block, comps), F32),
            ],
        ),
        compiler_params=pltpu.CompilerParams(vmem_limit_bytes=BUILD * MIB),
        cost_estimate=pl.CostEstimate(
            flops=12 * EX_DEV * half_ranks * WINDOW * 2 * LANES,
            bytes_accessed=4 * EX_DEV * comps + 4 * tokens * LANES,
            transcendentals=0,
        ),
    )(offs, starts, *sources, ids, pick)


def join_kernel(planes, *refs):
    highs, lows, squares = refs[:planes], refs[planes:2 * planes], refs[2 * planes:3 * planes]
    slots, out_ref, b_ref = refs[3 * planes:-2], refs[-2], refs[-1]
    width = slots[0].shape[1]
    for k, slot in enumerate(slots):
        b_ref[:, k * width:(k + 1) * width] = slot[...]
    b = b_ref[...]
    count = b.shape[0]
    b_both = jnp.concatenate(split2(b), axis=0)
    for k in range(planes):
        both = (dot_nt(highs[k][...], b_both) + dot_nt(lows[k][...], b_both)).T
        out_ref[:, k * EX_DEV:(k + 1) * EX_DEV] = both[:count] + both[count:]
    total = squares[0][...]
    for square in squares[1:]:
        total = total + square[...]
    total = jnp.sum(jnp.sum(total, axis=1, keepdims=True), axis=0, keepdims=True)
    norm = jnp.sum(b * b, axis=1, keepdims=True)
    out_ref[:, planes * EX_DEV:] = lanes_of([norm, total], (count, LANES))


def join(highs, lows, squares, slots):
    planes = len(highs)
    count, comps = slots[0].shape[0], highs[0].shape[1]
    return pl.pallas_call(
        functools.partial(join_kernel, planes),
        out_shape=(
            jax.ShapeDtypeStruct((count, planes * EX_DEV + LANES), F32),
            jax.ShapeDtypeStruct((count, comps), F32),
        ),
        compiler_params=pltpu.CompilerParams(vmem_limit_bytes=STEP * MIB),
        cost_estimate=pl.CostEstimate(
            flops=6 * planes * EX_DEV * count * comps,
            bytes_accessed=4 * planes * EX_DEV * comps,
            transcendentals=0,
        ),
    )(*highs, *lows, *squares, *slots)


def column(values, k):
    return values[:, k:k + 1]


def lanes_of(columns, shape):
    lane = lax.broadcasted_iota(jnp.int32, shape, 1)
    out = jnp.zeros(shape, F32)
    for k, one in enumerate(columns):
        out = jnp.where(lane == k, one, out)
    return out


def begin(first, examples, comps_all, mine, other, s_prev, state):
    total = mine + other
    inner, stats = total[:, :examples], total[:, examples:]
    norm = column(stats, 0)
    if first:
        damping = 0.1 * column(stats, 1) / (examples * comps_all)
        s, length, beta = inner, norm, None
    else:
        beta = norm / column(state, 0)
        s = inner + beta * s_prev
        length = norm + 2.0 * beta * column(stats, 1) + beta * beta * column(state, 1)
        damping = column(state, 2)
    bend = jnp.sum(s * s, axis=1, keepdims=True) / examples + damping * length
    return s, norm, length, damping, beta, norm / bend


def step_kernel(first, planes, examples, comps_all, *refs):
    refs = list(refs)
    take = lambda n: [refs.pop(0) for _ in range(n)]
    mine_ref, other_ref, r_ref = take(3)
    if not first:
        p_ref, x_ref, s_ref, y_ref, state_ref = take(5)
    highs, lows = take(planes), take(planes)
    msg_out, r_out, p_out, x_out, s_out, y_out, state_out = take(7)
    s_two, z_acc, stats_acc, scal = take(4)
    count, comps = r_ref.shape
    s, norm, length, damping, beta, alpha = begin(
        first, examples, comps_all, mine_ref[...], other_ref[...],
        None if first else s_ref[...], None if first else state_ref[...],
    )
    s_out[...] = s
    y_out[...] = alpha * s if first else y_ref[...] + alpha * s
    high, low = split2(s)
    s_two[0:count, :] = high
    s_two[count:2 * count, :] = low
    state_out[...] = lanes_of([norm, length, damping], state_out.shape)
    scal[...] = lanes_of([alpha, damping] + ([] if first else [beta]), scal.shape)
    z_acc[...] = jnp.zeros_like(z_acc)
    stats_acc[...] = jnp.zeros_like(stats_acc)
    block = 512

    @pl.loop(0, comps // block)
    def _(turn):
        at = pl.ds(pl.multiple_of(turn * block, block), block)
        alpha, damping = scal[:, 0:1], scal[:, 1:2]
        r = r_ref[:, at]
        if first:
            p = r
            x_out[:, at] = alpha * p
        else:
            p = r + scal[:, 2:3] * p_ref[:, at]
            x_out[:, at] = x_ref[:, at] + alpha * p
        p_out[:, at] = p
        q = jnp.zeros(r.shape, F32)
        for k in range(planes):
            part = slice(k * EX_DEV, (k + 1) * EX_DEV)
            both = dot_nn(s_two[:, part], highs[k][:, at])
            q = q + both[:count] + both[count:] + dot_nn(s_two[0:count, part], lows[k][:, at])
        r_new = r - alpha * (q / examples + damping * p)
        r_out[:, at] = r_new
        stacked = jnp.concatenate(split2(r_new), axis=0)
        for k in range(planes):
            part = slice(k * EX_DEV, (k + 1) * EX_DEV)
            z_acc[part, :] += dot_nt(highs[k][:, at], stacked) + dot_nt(lows[k][:, at], stacked)
        stats_acc[...] += lanes_of(
            [
                jnp.sum(r_new * r_new, axis=1, keepdims=True),
                jnp.sum(r_new * p, axis=1, keepdims=True),
            ],
            stats_acc.shape,
        )

    both = z_acc[...].T
    msg_out[:, 0:examples] = both[:count] + both[count:]
    msg_out[:, examples:] = stats_acc[...]


def one_step(first, examples, comps_all, mine, other, r, rest, highs, lows):
    planes = len(highs)
    count, comps = r.shape
    wide = jax.ShapeDtypeStruct((count, examples), F32)
    long = jax.ShapeDtypeStruct((count, comps), F32)
    small = jax.ShapeDtypeStruct((count, LANES), F32)
    message = jax.ShapeDtypeStruct((count, examples + LANES), F32)
    return pl.pallas_call(
        functools.partial(step_kernel, first, planes, examples, comps_all),
        out_shape=(message, long, long, long, wide, wide, small),
        scratch_shapes=[
            pltpu.VMEM((2 * count, examples), BF16),
            pltpu.VMEM((examples, 2 * count), F32),
            pltpu.VMEM((count, LANES), F32),
            pltpu.VMEM((count, LANES), F32),
        ],
        compiler_params=pltpu.CompilerParams(vmem_limit_bytes=STEP * MIB),
        cost_estimate=pl.CostEstimate(
            flops=12 * count * examples * comps,
            bytes_accessed=4 * examples * comps,
            transcendentals=0,
        ),
    )(mine, other, r, *rest, *highs, *lows)


def last_kernel(examples, comps_all, mine_ref, other_ref, r_ref, p_ref, x_ref, s_ref, y_ref, state_ref, x_out, y_out):
    s, _, _, _, beta, alpha = begin(
        False, examples, comps_all, mine_ref[...], other_ref[...], s_ref[...], state_ref[...]
    )
    scale = 1.0 / jnp.sqrt(F32(comps_all))
    y_out[...] = (y_ref[...] + alpha * s) * scale
    x_out[...] = x_ref[...] + alpha * (r_ref[...] + beta * p_ref[...])


def last_step(examples, comps_all, *arrays):
    x, y = arrays[4], arrays[6]
    return pl.pallas_call(
        functools.partial(last_kernel, examples, comps_all),
        out_shape=(jax.ShapeDtypeStruct(x.shape, F32), jax.ShapeDtypeStruct(y.shape, F32)),
        compiler_params=pltpu.CompilerParams(vmem_limit_bytes=STEP * MIB),
    )(*arrays)


def place_kernel(slots, where_ref, part_ref, *refs):
    out_ref, held = refs[-2:]
    rows = part_ref.shape[0] // slots
    for k in range(slots):
        at = pl.multiple_of(where_ref[1 + k] * rows, rows)
        held[pl.ds(at, rows), :] = part_ref[k * rows:(k + 1) * rows, :]
    out_ref[...] = held[...].T


def place(where, part, out, shape):
    operands, in_specs = [part], [pl.BlockSpec(part.shape, lambda i, where: (0, 0))]
    if out is not None:
        operands.append(out)
        in_specs.append(pl.BlockSpec(memory_space=pl.ANY))
    return pl.pallas_call(
        functools.partial(place_kernel, where.shape[0] - 1),
        out_shape=jax.ShapeDtypeStruct(shape, F32),
        grid_spec=pltpu.PrefetchScalarGridSpec(
            num_scalar_prefetch=1,
            grid=(1,),
            in_specs=in_specs,
            out_specs=pl.BlockSpec((shape[0], part.shape[0]), lambda i, where: (0, where[0])),
            scratch_shapes=[pltpu.VMEM(part.shape, F32)],
        ),
        input_output_aliases={} if out is None else {2: 0},
        compiler_params=pltpu.CompilerParams(vmem_limit_bytes=24 * MIB),
    )(where, *operands)


def per_device(n_dp, n_t, activations, out_grads, proj_in, proj_out, example_ids, queries):
    tokens = activations.shape[0]
    ranks = proj_in.shape[1]
    comps_all = proj_in.shape[1] * proj_out.shape[1]
    examples = EX_DEV * n_dp
    n_c = n_t // 2
    j = lax.axis_index("tensor")
    i = lax.axis_index("dp")
    chip, core = j // 2, j % 2

    def swap(values, mask):
        return lax.ppermute(values, "tensor", [(a, a ^ mask) for a in range(n_t)])

    def shift(values, by):
        return lax.ppermute(values, "dp", [(a, (a + by) % n_dp) for a in range(n_dp)])

    def tie(values, token):
        return lax.optimization_barrier((values, token))[0]

    near_chip = [chip ^ k for k in range(n_c)]

    q_chip = queries.shape[0] // n_c
    slots = [lax.dynamic_slice_in_dim(queries, near_chip[k] * q_chip, q_chip, 0) for k in range(n_c)]

    group = 8
    bounds = group * jnp.arange(EX_DEV // group, dtype=jnp.int32)
    starts = jnp.sum((example_ids[0][None, :] < bounds[:, None]).astype(F32), axis=1)
    starts = jnp.minimum(starts, F32(tokens - LANES))
    id_rows = tokens // LANES
    extra = jnp.concatenate(
        [
            example_ids.astype(F32).reshape((id_rows, LANES)),
            jnp.pad(starts[None, :], ((0, 7), (0, LANES - EX_DEV // group))),
        ],
        axis=0,
    )

    share = tokens // n_t
    blocks = jnp.stack(near_chip).astype(jnp.int32) * 2
    w_in, w_out = proj_in.T, proj_out.T
    give = project(blocks + 1 - core, activations, out_grads, w_in, w_out, share)
    keep = project(blocks + core, activations, out_grads, w_in, w_out, share)
    extra = tie(extra, give)
    extras = [extra] + [shift(extra, away) for away in range(1, n_dp)]
    plane_ids = [one[:id_rows].reshape((1, tokens)) for one in extras]
    firsts = [one[id_rows, :EX_DEV // group].astype(jnp.int32) for one in extras]
    kept = (keep + swap(give, 1)).reshape((n_c, share, LANES))
    own = kept[0]
    for k in range(1, n_c):
        own = own + swap(kept[k], 2 * k)

    rings = [own]
    for _ in range(n_dp - 1):
        rings.append(shift(rings[-1], 1))

    per = comps_all // ranks // n_t
    wanted = [(near_chip[k] * 2 + core) * per + a + ranks for k in range(n_c) for a in range(per)]
    wanted = jnp.stack(wanted[0::2] + wanted[1::2])
    pick = (wanted[:, None] == jnp.arange(LANES)[None, :]).astype(BF16)

    offs = jnp.stack(
        [near_chip[k] * 2 + which for which in (core, 1 - core) for k in range(n_c)]
    ).astype(jnp.int32)
    offs, pick, plane_ids, firsts, slots = lax.optimization_barrier(
        (offs, pick, plane_ids, firsts, slots)
    )

    highs, lows, squares = [], [], []
    for away in range(n_dp):
        piece = rings[away]
        near = [piece] + [swap(piece, 2 * k) for k in range(1, n_c)]
        sources = near + [
            swap(part, 1) for part in (tie(near, squares[-1]) if squares else near)
        ]
        high, low, square = build(
            offs, firsts[away], sources, plane_ids[away], pick, ranks, share, comps_all // 2
        )
        highs.append(high)
        lows.append(low)
        squares.append(square)

    slots = [slots[0]] + [swap(slots[k], 2 * k) for k in range(1, n_c)]
    message, b = join(highs, lows, squares, slots)
    r, rest = b, ()
    for step in range(ITERS - 1):
        other = swap(message, 1)
        message, r, p, x, s, y, state = one_step(
            step == 0, examples, comps_all, message, other, r, rest, highs, lows
        )
        rest = (p, x, s, y, state)
    other = swap(message, 1)
    x, y = last_step(examples, comps_all, message, other, r, *rest)

    n_half = n_c // 2
    per_slot = comps_all // n_t

    def send(values, to):
        pairs = [
            (di * n_t + 2 * c + c // n_half, to(di, c, c // n_half))
            for di in range(n_dp) for c in range(n_c)
        ]
        return lax.ppermute(values, ("dp", "tensor"), pairs)

    ring = [x[:, k * per_slot:(k + 1) * per_slot] for k in range(n_c)]
    ring = jnp.concatenate([ring[0]] + [swap(ring[k], 2 * k) for k in range(1, n_c)], axis=0)
    y = tie(y, ring)
    by_plane = jnp.zeros((n_dp, q_chip, EX_DEV), F32)
    for away in range(n_dp):
        part = y[:, away * EX_DEV:(away + 1) * EX_DEV]
        if away:
            part = send(part, lambda di, c, h: ((di - away) % n_dp) * n_t + 2 * c + h)
        by_plane = lax.dynamic_update_slice(by_plane, part[None], ((i + away) % n_dp, 0, 0))
    by_chip = jnp.zeros((n_c, q_chip, EX_DEV), F32)
    for k in range(n_c):
        part = lax.dynamic_slice_in_dim(by_plane, near_chip[k], 1, 0)
        if k:
            part = send(part, lambda di, c, h: di * n_t + 2 * (c ^ k) + h)
        by_chip = lax.dynamic_update_slice(by_chip, part, (near_chip[k], 0, 0))
    scores = lax.dynamic_slice_in_dim(by_chip, core * n_half, n_half, 0)

    outs = [None]
    for away in range(n_dp):
        if away:
            before = [[], [by_plane, outs[-2]], [scores, outs[-2]]][min(away - 1, 2)]
            ring = shift(tie(ring, before) if before else ring, 1)
        where = jnp.stack([(i - away) % n_dp] + near_chip).astype(jnp.int32)
        outs.append(place(where, ring, outs[-1], (per_slot, n_dp * n_c * q_chip)))
    return (outs[-1], scores.reshape((n_half * q_chip, EX_DEV)))


def solution(mesh):
    in_specs = (
        P("dp", "tensor"),
        P("dp", "tensor"),
        P("tensor", None),
        P("tensor", None),
        P("dp", None),
        P("dp", "tensor"),
    )
    out_specs = (P("tensor", None), P("tensor", "dp"))
    body = functools.partial(per_device, mesh.shape["dp"], mesh.shape["tensor"])
    return jax.shard_map(body, mesh=mesh, in_specs=in_specs, out_specs=out_specs, check_vma=False)
```

```python
import functools

import jax
import jax.numpy as jnp
from jax import lax
from jax.experimental import pallas as pl
from jax.experimental.pallas import tpu as pltpu
from jax.sharding import PartitionSpec as P

ITERS = 4
EX_DEV = 512
LANES = 128
WINDOW = 256
PARTS = 2
F32 = jnp.float32
BF16 = jnp.bfloat16
MIB = 1024 * 1024
BUILD = 24
STEP = 24


def split2(values):
    high = values.astype(BF16)
    low = (values - high.astype(F32)).astype(BF16)
    return high, low


def dot_nn(left, right):
    return lax.dot_general(left, right, (((1,), (0,)), ((), ())), preferred_element_type=F32)


def dot_nt(left, right):
    return lax.dot_general(left, right, (((1,), (1,)), ((), ())), preferred_element_type=F32)


def project_kernel(order_ref, act_ref, grad_ref, wi_ref, wo_ref, *outs):
    del order_ref
    values = jnp.concatenate(
        [dot_nt(act_ref[...], wi_ref[...]), dot_nt(grad_ref[...], wo_ref[...])], axis=1
    )
    for which, out_ref in enumerate(outs):
        @pl.when(pl.program_id(0) // PARTS == which)
        def _():
            out_ref[...] = values


def project(order, activations, out_grads, w_in, w_out, block):
    feats, hidden = activations.shape[1], out_grads.shape[1]
    rows = block // PARTS
    at = lambda i, order: (order[i // PARTS] * PARTS + i % PARTS, 0)
    return pl.pallas_call(
        project_kernel,
        out_shape=(jax.ShapeDtypeStruct((block, LANES), F32),) * 2,
        grid_spec=pltpu.PrefetchScalarGridSpec(
            num_scalar_prefetch=1,
            grid=(2 * PARTS,),
            in_specs=[
                pl.BlockSpec((rows, feats), at),
                pl.BlockSpec((rows, hidden), at),
                pl.BlockSpec(w_in.shape, lambda i, order: (0, 0)),
                pl.BlockSpec(w_out.shape, lambda i, order: (0, 0)),
            ],
            out_specs=[
                pl.BlockSpec((rows, LANES), lambda i, order: (jnp.minimum(i, PARTS - 1), 0)),
                pl.BlockSpec((rows, LANES), lambda i, order: (jnp.maximum(i - PARTS, 0), 0)),
            ],
        ),
        compiler_params=pltpu.CompilerParams(vmem_limit_bytes=61 * MIB),
        cost_estimate=pl.CostEstimate(
            flops=4 * block * (feats + hidden) * 4 * WINDOW,
            bytes_accessed=4 * block * (feats + hidden),
            transcendentals=0,
        ),
    )(order, activations, out_grads, w_in, w_out)


def build_kernel(ranks, share, ex_block, n_sources, *refs):
    offs_ref, start_ref = refs[:2]
    sources = refs[2:2 + n_sources]
    ids_ref, pick_ref = refs[2 + n_sources:4 + n_sources]
    high_ref, low_ref, sq_ref = refs[4 + n_sources:7 + n_sources]
    out_t, in_twice, ids_wide, rows, sketch = refs[7 + n_sources:]
    step = pl.program_id(0)
    half_ranks = pick_ref.shape[0]
    pairs = half_ranks // 2
    tokens = ids_ref.shape[1]

    @pl.when(step == 0)
    def _():
        lane = lax.broadcasted_iota(jnp.int32, (share, LANES), 1)
        block = 0
        for source in sources:
            for k in range(source.shape[0] // share):
                values = source[k * share:(k + 1) * share, :]
                at = pl.multiple_of(offs_ref[block] * share, share)
                block += 1
                high, low = split2(values)
                out_t[:, pl.ds(at, share)] = dot_nt(pick_ref[...], high) + dot_nt(pick_ref[...], low)
                in_twice[pl.ds(at, share), :] = jnp.where(
                    lane < ranks, values, pltpu.roll(values, ranks, 1)
                )
        ids_wide[...] = jnp.broadcast_to(ids_ref[...], ids_wide.shape)
        sq_ref[...] = jnp.zeros_like(sq_ref)

    slots = rows.shape[0]
    group = rows.shape[1] // pairs
    lane = lax.broadcasted_iota(jnp.int32, (LANES, LANES), 1)
    left_lanes = (lane < ranks).astype(F32).astype(BF16)
    right_lanes = (lane >= ranks).astype(F32).astype(BF16)

    def one_group(g, slot):
        number = step * (ex_block // group) + g
        start = start_ref[number]
        at = jnp.minimum(lax.div(start, LANES) * LANES, tokens - WINDOW)
        turn = lax.rem(WINDOW - (start - at), WINDOW)
        at = pl.multiple_of(at, LANES)
        out_win = pltpu.roll(out_t[:, pl.ds(at, WINDOW)], turn, 1)[:, :LANES]
        ids_win = pltpu.roll(ids_wide[:, pl.ds(at, WINDOW)], turn, 1)[:, :LANES]
        base = (number * group).astype(F32)
        lefts = ([], [])
        terms = split2(out_win)
        for e in range(group):
            mask = (ids_win == base + float(e)).astype(F32)
            mask = jnp.concatenate([mask] * (pairs // 8), axis=0).astype(BF16)
            for left, term in zip(lefts, terms):
                left.append(jnp.concatenate([term[:pairs] * mask, term[pairs:] * mask], axis=1))
        left = jnp.concatenate(lefts[0] + lefts[1], axis=0)
        high, low = split2(in_twice[pl.ds(start, LANES), :])
        right = jnp.concatenate(
            [
                jnp.concatenate([high * lanes, low * lanes], axis=1)
                for lanes in (left_lanes, right_lanes)
            ],
            axis=0,
        )
        res = dot_nn(left, right)
        top = group * pairs
        rows[slot] = (
            (res[:top, :LANES] + res[top:, :LANES]) + (res[:top, LANES:] + res[top:, LANES:])
        )
        to = pl.multiple_of(g * group, group)
        for pair in range(pairs):
            sketch[pl.ds(to, group), pair * LANES:(pair + 1) * LANES] = rows[
                slot, pl.ds(pair, group, stride=pairs), :
            ]

    @pl.loop(0, ex_block // group // slots)
    def _(turn):
        for slot in range(slots):
            one_group(turn * slots + slot, slot)

    values = sketch[...]
    high, low = split2(values)
    high_ref[...] = high
    low_ref[...] = low
    sq = jnp.sum((values * values).reshape(ex_block // 8, 8, -1), axis=0)
    total = sq[:, 0:LANES]
    for k in range(1, values.shape[1] // LANES):
        total = total + sq[:, k * LANES:(k + 1) * LANES]
    sq_ref[...] += total


def build(offs, starts, sources, ids, pick, ranks, share, comps):
    tokens = ids.shape[1]
    half_ranks = pick.shape[0]
    ex_block = 256
    group = 8
    whole = lambda i, *_: (0, 0)
    return pl.pallas_call(
        functools.partial(build_kernel, ranks, share, ex_block, len(sources)),
        out_shape=(
            jax.ShapeDtypeStruct((EX_DEV, comps), BF16),
            jax.ShapeDtypeStruct((EX_DEV, comps), BF16),
            jax.ShapeDtypeStruct((8, LANES), F32),
        ),
        grid_spec=pltpu.PrefetchScalarGridSpec(
            num_scalar_prefetch=2,
            grid=(EX_DEV // ex_block,),
            in_specs=[pl.BlockSpec(a.shape, whole) for a in (*sources, ids, pick)],
            out_specs=[
                pl.BlockSpec((ex_block, comps), lambda i, *_: (i, 0)),
                pl.BlockSpec((ex_block, comps), lambda i, *_: (i, 0)),
                pl.BlockSpec((8, LANES), whole),
            ],
            scratch_shapes=[
                pltpu.VMEM((half_ranks, tokens), F32),
                pltpu.VMEM((tokens, LANES), F32),
                pltpu.VMEM((8, tokens), F32),
                pltpu.VMEM((4, group * half_ranks // 2, LANES), F32),
                pltpu.VMEM((ex_block, comps), F32),
            ],
        ),
        compiler_params=pltpu.CompilerParams(vmem_limit_bytes=BUILD * MIB),
        cost_estimate=pl.CostEstimate(
            flops=12 * EX_DEV * half_ranks * WINDOW * 2 * LANES,
            bytes_accessed=4 * EX_DEV * comps + 4 * tokens * LANES,
            transcendentals=0,
        ),
    )(offs, starts, *sources, ids, pick)


def join_kernel(planes, *refs):
    highs, lows, squares = refs[:planes], refs[planes:2 * planes], refs[2 * planes:3 * planes]
    slots, out_ref, b_ref = refs[3 * planes:-2], refs[-2], refs[-1]
    width = slots[0].shape[1]
    for k, slot in enumerate(slots):
        b_ref[:, k * width:(k + 1) * width] = slot[...]
    b = b_ref[...]
    count = b.shape[0]
    b_both = jnp.concatenate(split2(b), axis=0)
    for k in range(planes):
        both = (dot_nt(highs[k][...], b_both) + dot_nt(lows[k][...], b_both)).T
        out_ref[:, k * EX_DEV:(k + 1) * EX_DEV] = both[:count] + both[count:]
    total = squares[0][...]
    for square in squares[1:]:
        total = total + square[...]
    total = jnp.sum(jnp.sum(total, axis=1, keepdims=True), axis=0, keepdims=True)
    norm = jnp.sum(b * b, axis=1, keepdims=True)
    out_ref[:, planes * EX_DEV:] = lanes_of([norm, total], (count, LANES))


def join(highs, lows, squares, slots):
    planes = len(highs)
    count, comps = slots[0].shape[0], highs[0].shape[1]
    return pl.pallas_call(
        functools.partial(join_kernel, planes),
        out_shape=(
            jax.ShapeDtypeStruct((count, planes * EX_DEV + LANES), F32),
            jax.ShapeDtypeStruct((count, comps), F32),
        ),
        compiler_params=pltpu.CompilerParams(vmem_limit_bytes=STEP * MIB),
        cost_estimate=pl.CostEstimate(
            flops=6 * planes * EX_DEV * count * comps,
            bytes_accessed=4 * planes * EX_DEV * comps,
            transcendentals=0,
        ),
    )(*highs, *lows, *squares, *slots)


def column(values, k):
    return values[:, k:k + 1]


def lanes_of(columns, shape):
    lane = lax.broadcasted_iota(jnp.int32, shape, 1)
    out = jnp.zeros(shape, F32)
    for k, one in enumerate(columns):
        out = jnp.where(lane == k, one, out)
    return out


def begin(first, examples, comps_all, mine, other, s_prev, state):
    total = mine + other
    inner, stats = total[:, :examples], total[:, examples:]
    norm = column(stats, 0)
    if first:
        damping = 0.1 * column(stats, 1) / (examples * comps_all)
        s, length, beta = inner, norm, None
    else:
        beta = norm / column(state, 0)
        s = inner + beta * s_prev
        length = norm + 2.0 * beta * column(stats, 1) + beta * beta * column(state, 1)
        damping = column(state, 2)
    bend = jnp.sum(s * s, axis=1, keepdims=True) / examples + damping * length
    return s, norm, length, damping, beta, norm / bend


def step_kernel(first, planes, examples, comps_all, *refs):
    refs = list(refs)
    take = lambda n: [refs.pop(0) for _ in range(n)]
    mine_ref, other_ref, r_ref = take(3)
    if not first:
        p_ref, x_ref, s_ref, y_ref, state_ref = take(5)
    highs, lows = take(planes), take(planes)
    msg_out, r_out, p_out, x_out, s_out, y_out, state_out = take(7)
    s_two, z_acc, stats_acc, scal = take(4)
    count, comps = r_ref.shape
    s, norm, length, damping, beta, alpha = begin(
        first, examples, comps_all, mine_ref[...], other_ref[...],
        None if first else s_ref[...], None if first else state_ref[...],
    )
    s_out[...] = s
    y_out[...] = alpha * s if first else y_ref[...] + alpha * s
    high, low = split2(s)
    s_two[0:count, :] = high
    s_two[count:2 * count, :] = low
    state_out[...] = lanes_of([norm, length, damping], state_out.shape)
    scal[...] = lanes_of([alpha, damping] + ([] if first else [beta]), scal.shape)
    z_acc[...] = jnp.zeros_like(z_acc)
    stats_acc[...] = jnp.zeros_like(stats_acc)
    block = 512

    @pl.loop(0, comps // block)
    def _(turn):
        at = pl.ds(pl.multiple_of(turn * block, block), block)
        alpha, damping = scal[:, 0:1], scal[:, 1:2]
        r = r_ref[:, at]
        if first:
            p = r
            x_out[:, at] = alpha * p
        else:
            p = r + scal[:, 2:3] * p_ref[:, at]
            x_out[:, at] = x_ref[:, at] + alpha * p
        p_out[:, at] = p
        q = jnp.zeros(r.shape, F32)
        for k in range(planes):
            part = slice(k * EX_DEV, (k + 1) * EX_DEV)
            both = dot_nn(s_two[:, part], highs[k][:, at])
            q = q + both[:count] + both[count:] + dot_nn(s_two[0:count, part], lows[k][:, at])
        r_new = r - alpha * (q / examples + damping * p)
        r_out[:, at] = r_new
        stacked = jnp.concatenate(split2(r_new), axis=0)
        for k in range(planes):
            part = slice(k * EX_DEV, (k + 1) * EX_DEV)
            z_acc[part, :] += dot_nt(highs[k][:, at], stacked) + dot_nt(lows[k][:, at], stacked)
        stats_acc[...] += lanes_of(
            [
                jnp.sum(r_new * r_new, axis=1, keepdims=True),
                jnp.sum(r_new * p, axis=1, keepdims=True),
            ],
            stats_acc.shape,
        )

    both = z_acc[...].T
    msg_out[:, 0:examples] = both[:count] + both[count:]
    msg_out[:, examples:] = stats_acc[...]


def one_step(first, examples, comps_all, mine, other, r, rest, highs, lows):
    planes = len(highs)
    count, comps = r.shape
    wide = jax.ShapeDtypeStruct((count, examples), F32)
    long = jax.ShapeDtypeStruct((count, comps), F32)
    small = jax.ShapeDtypeStruct((count, LANES), F32)
    message = jax.ShapeDtypeStruct((count, examples + LANES), F32)
    return pl.pallas_call(
        functools.partial(step_kernel, first, planes, examples, comps_all),
        out_shape=(message, long, long, long, wide, wide, small),
        scratch_shapes=[
            pltpu.VMEM((2 * count, examples), BF16),
            pltpu.VMEM((examples, 2 * count), F32),
            pltpu.VMEM((count, LANES), F32),
            pltpu.VMEM((count, LANES), F32),
        ],
        compiler_params=pltpu.CompilerParams(vmem_limit_bytes=STEP * MIB),
        cost_estimate=pl.CostEstimate(
            flops=12 * count * examples * comps,
            bytes_accessed=4 * examples * comps,
            transcendentals=0,
        ),
    )(mine, other, r, *rest, *highs, *lows)


def last_kernel(examples, comps_all, mine_ref, other_ref, r_ref, p_ref, x_ref, s_ref, y_ref, state_ref, x_out, y_out):
    s, _, _, _, beta, alpha = begin(
        False, examples, comps_all, mine_ref[...], other_ref[...], s_ref[...], state_ref[...]
    )
    scale = 1.0 / jnp.sqrt(F32(comps_all))
    y_out[...] = (y_ref[...] + alpha * s) * scale
    x_out[...] = x_ref[...] + alpha * (r_ref[...] + beta * p_ref[...])


def last_step(examples, comps_all, *arrays):
    x, y = arrays[4], arrays[6]
    return pl.pallas_call(
        functools.partial(last_kernel, examples, comps_all),
        out_shape=(jax.ShapeDtypeStruct(x.shape, F32), jax.ShapeDtypeStruct(y.shape, F32)),
        compiler_params=pltpu.CompilerParams(vmem_limit_bytes=STEP * MIB),
    )(*arrays)


def arrange_kernel(count, origin_ref, *refs):
    parts, outs, held = refs[:count], refs[count:-1], refs[-1]
    rows = parts[0].shape[0]
    for k, part in enumerate(parts):
        held[k * rows:(k + 1) * rows, :] = part[...]
    for k, out in enumerate(outs):
        out[...] = held[pl.ds(pl.multiple_of(origin_ref[k] * rows, rows), rows), :]


def arrange(origin, parts):
    rows, columns = parts[0].shape
    whole = pl.BlockSpec((rows, columns), lambda i, origin: (0, 0))
    return pl.pallas_call(
        functools.partial(arrange_kernel, len(parts)),
        out_shape=(jax.ShapeDtypeStruct((rows, columns), F32),) * origin.shape[0],
        grid_spec=pltpu.PrefetchScalarGridSpec(
            num_scalar_prefetch=1,
            grid=(1,),
            in_specs=[whole] * len(parts),
            out_specs=[whole] * origin.shape[0],
            scratch_shapes=[pltpu.VMEM((len(parts) * rows, columns), F32)],
        ),
        compiler_params=pltpu.CompilerParams(vmem_limit_bytes=8 * MIB),
    )(origin, *parts)


def place_kernel(slots, planes, where_ref, *refs):
    rings, out_ref, held = refs[:planes], refs[planes], refs[planes + 1]
    rows = rings[0].shape[0] // slots
    step = pl.program_id(0)
    for away, ring in enumerate(rings):
        to = pl.multiple_of(where_ref[slots + away] * rows, rows)
        k = where_ref[step]
        held[pl.ds(to, rows), :] = ring[pl.ds(pl.multiple_of(k * rows, rows), rows), :]
    out_ref[...] = held[...].T


def place(where, rings, slots):
    planes = len(rings)
    rows, comps = rings[0].shape[0] // slots * planes, rings[0].shape[1]
    whole = pl.BlockSpec(rings[0].shape, lambda i, where: (0, 0))
    return pl.pallas_call(
        functools.partial(place_kernel, slots, planes),
        out_shape=jax.ShapeDtypeStruct((comps, slots * rows), F32),
        grid_spec=pltpu.PrefetchScalarGridSpec(
            num_scalar_prefetch=1,
            grid=(slots,),
            in_specs=[whole] * planes,
            out_specs=pl.BlockSpec((comps, rows), lambda i, where: (0, i)),
            scratch_shapes=[pltpu.VMEM((rows, comps), F32)],
        ),
        compiler_params=pltpu.CompilerParams(vmem_limit_bytes=24 * MIB),
    )(where, *rings)


def per_device(n_dp, n_t, activations, out_grads, proj_in, proj_out, example_ids, queries):
    tokens = activations.shape[0]
    ranks = proj_in.shape[1]
    comps_all = proj_in.shape[1] * proj_out.shape[1]
    examples = EX_DEV * n_dp
    n_c = n_t // 2
    j = lax.axis_index("tensor")
    i = lax.axis_index("dp")
    chip, core = j // 2, j % 2

    def swap(values, mask):
        return lax.ppermute(values, "tensor", [(a, a ^ mask) for a in range(n_t)])

    def shift(values, by):
        return lax.ppermute(values, "dp", [(a, (a + by) % n_dp) for a in range(n_dp)])

    def tie(values, token):
        return lax.optimization_barrier((values, token))[0]

    near_chip = [chip ^ k for k in range(n_c)]

    q_chip = queries.shape[0] // n_dp
    parts = [
        lax.dynamic_slice_in_dim(queries, (i + away) % n_dp * q_chip, q_chip, 0) for away in range(n_dp)
    ]
    origin = jnp.stack([(i - near_chip[k]) % n_dp for k in range(n_c)]).astype(jnp.int32)

    group = 8
    bounds = group * jnp.arange(EX_DEV // group, dtype=jnp.int32)
    starts = jnp.sum((example_ids[0][None, :] < bounds[:, None]).astype(F32), axis=1)
    starts = jnp.minimum(starts, F32(tokens - LANES))
    id_rows = tokens // LANES
    extra = jnp.concatenate(
        [
            example_ids.astype(F32).reshape((id_rows, LANES)),
            jnp.pad(starts[None, :], ((0, 7), (0, LANES - EX_DEV // group))),
        ],
        axis=0,
    )

    share = tokens // n_t
    w_in, w_out = proj_in.T, proj_out.T
    own, came = None, []
    for k in reversed(range(n_c)):
        order = jnp.stack([near_chip[k] * 2 + 1 - core, near_chip[k] * 2 + core]).astype(jnp.int32)
        if k < n_c - 1:
            order = tie(order, [give] if k else [came[:-2], part])
        give, keep = project(order, activations, out_grads, w_in, w_out, share)
        part = keep + swap(give, 1)
        if k == n_c - 1:
            first_give = give
        if k:
            came.append(swap(part, 2 * k))
        else:
            own = part
    for part in came:
        own = own + part
    extra = tie(extra, first_give)
    extras = [extra] + [shift(extra, away) for away in range(1, n_dp)]
    plane_ids = [one[:id_rows].reshape((1, tokens)) for one in extras]
    firsts = [one[id_rows, :EX_DEV // group].astype(jnp.int32) for one in extras]

    rings = [own]
    for _ in range(n_dp - 1):
        rings.append(shift(rings[-1], 1))

    per = comps_all // ranks // n_t
    wanted = [(near_chip[k] * 2 + core) * per + a + ranks for k in range(n_c) for a in range(per)]
    wanted = jnp.stack(wanted[0::2] + wanted[1::2])
    pick = (wanted[:, None] == jnp.arange(LANES)[None, :]).astype(BF16)

    offs = jnp.stack(
        [near_chip[k] * 2 + which for which in (core, 1 - core) for k in range(n_c)]
    ).astype(jnp.int32)
    offs, pick, plane_ids, firsts, parts, origin = lax.optimization_barrier(
        (offs, pick, plane_ids, firsts, parts, origin)
    )

    highs, lows, squares = [], [], []
    for away in range(n_dp):
        piece = rings[away]
        near = [piece] + [swap(piece, 2 * k) for k in range(1, n_c)]
        sources = near + [
            swap(part, 1) for part in (tie(near, squares[-1]) if squares else near)
        ]
        high, low, square = build(
            offs, firsts[away], sources, plane_ids[away], pick, ranks, share, comps_all // 2
        )
        highs.append(high)
        lows.append(low)
        squares.append(square)

    slots = arrange(origin, [parts[0]] + [shift(parts[away], away) for away in range(1, n_dp)])
    slots = [slots[0]] + [swap(slots[k], 2 * k) for k in range(1, n_c)]
    message, b = join(highs, lows, squares, slots)
    r, rest = b, ()
    for step in range(ITERS - 1):
        other = swap(message, 1)
        message, r, p, x, s, y, state = one_step(
            step == 0, examples, comps_all, message, other, r, rest, highs, lows
        )
        rest = (p, x, s, y, state)
    other = swap(message, 1)
    x, y = last_step(examples, comps_all, message, other, r, *rest)

    n_half = n_dp // 2
    per_slot = comps_all // n_t

    def send(values, by):
        pairs = [
            (a * n_t + 2 * c + a // n_half, (a + by) % n_dp * n_t + 2 * c + a // n_half)
            for a in range(n_dp) for c in range(n_c)
        ]
        return lax.ppermute(values, ("dp", "tensor"), pairs)

    by_plane = jnp.zeros((n_dp, q_chip, EX_DEV), F32)
    for away in range(n_dp):
        part = y[:, away * EX_DEV:(away + 1) * EX_DEV]
        if away:
            part = send(part, -away)
        by_plane = lax.dynamic_update_slice(by_plane, part[None], ((i + away) % n_dp, 0, 0))
    scores = lax.dynamic_slice_in_dim(by_plane, core * n_half, n_half, 0)

    ring = [x[:, k * per_slot:(k + 1) * per_slot] for k in range(n_c)]
    ring = jnp.concatenate([ring[0]] + [swap(ring[k], 2 * k) for k in range(1, n_c)], axis=0)
    rings = [ring]
    for away in range(1, n_dp):
        rings.append(shift(tie(rings[-1], scores) if away == 2 else rings[-1], 1))
    where = jnp.stack(
        [chip ^ c for c in range(n_c)] + [(i - away) % n_dp for away in range(n_dp)]
    ).astype(jnp.int32)
    out = place(where, rings, n_c)
    return (out, scores.reshape((n_half * q_chip, EX_DEV)))


def solution(mesh):
    in_specs = (
        P("dp", "tensor"),
        P("dp", "tensor"),
        P("tensor", None),
        P("tensor", None),
        P("dp", None),
        P("dp", "tensor"),
    )
    out_specs = (P("tensor", None), P("tensor", "dp"))
    body = functools.partial(per_device, mesh.shape["dp"], mesh.shape["tensor"])
    return jax.shard_map(body, mesh=mesh, in_specs=in_specs, out_specs=out_specs, check_vma=False)
```

```python
import functools

import jax
import jax.numpy as jnp
from jax import lax
from jax.experimental import pallas as pl
from jax.experimental.pallas import tpu as pltpu
from jax.sharding import PartitionSpec as P

ITERS = 4
EX_DEV = 512
LANES = 128
WINDOW = 256
PARTS = 4
F32 = jnp.float32
BF16 = jnp.bfloat16
MIB = 1024 * 1024
BUILD = 24
STEP = 24


def split2(values):
    high = values.astype(BF16)
    low = (values - high.astype(F32)).astype(BF16)
    return high, low


def dot_nn(left, right):
    return lax.dot_general(left, right, (((1,), (0,)), ((), ())), preferred_element_type=F32)


def dot_nt(left, right):
    return lax.dot_general(left, right, (((1,), (1,)), ((), ())), preferred_element_type=F32)


def project_kernel(order_ref, *refs):
    del order_ref
    acts, grads = refs[:PARTS], refs[PARTS:2 * PARTS]
    wi_ref, wo_ref, out_ref = refs[2 * PARTS:]
    rows = acts[0].shape[0]
    for part, (act_ref, grad_ref) in enumerate(zip(acts, grads)):
        out_ref[part * rows:(part + 1) * rows, :] = jnp.concatenate(
            [dot_nt(act_ref[...], wi_ref[...]), dot_nt(grad_ref[...], wo_ref[...])], axis=1
        )


def project(order, activations, out_grads, w_in, w_out, block):
    steps = order.shape[0]
    feats, hidden = activations.shape[1], out_grads.shape[1]
    rows = block // PARTS

    def parts(width):
        return [
            pl.BlockSpec((rows, width), lambda i, order, part=part: (order[i] * PARTS + part, 0))
            for part in range(PARTS)
        ]

    return pl.pallas_call(
        project_kernel,
        out_shape=jax.ShapeDtypeStruct((steps * block, LANES), F32),
        grid_spec=pltpu.PrefetchScalarGridSpec(
            num_scalar_prefetch=1,
            grid=(steps,),
            in_specs=parts(feats) + parts(hidden) + [
                pl.BlockSpec(w_in.shape, lambda i, order: (0, 0)),
                pl.BlockSpec(w_out.shape, lambda i, order: (0, 0)),
            ],
            out_specs=pl.BlockSpec((block, LANES), lambda i, order: (i, 0)),
        ),
        compiler_params=pltpu.CompilerParams(vmem_limit_bytes=61 * MIB),
        cost_estimate=pl.CostEstimate(
            flops=2 * steps * block * (feats + hidden) * 4 * WINDOW,
            bytes_accessed=2 * steps * block * (feats + hidden),
            transcendentals=0,
        ),
    )(order, *[activations] * PARTS, *[out_grads] * PARTS, w_in, w_out)


def build_kernel(ranks, share, ex_block, n_sources, *refs):
    offs_ref, start_ref = refs[:2]
    sources = refs[2:2 + n_sources]
    ids_ref, pick_ref = refs[2 + n_sources:4 + n_sources]
    high_ref, low_ref, sq_ref = refs[4 + n_sources:7 + n_sources]
    out_t, in_twice, ids_wide, rows, sketch = refs[7 + n_sources:]
    step = pl.program_id(0)
    half_ranks = pick_ref.shape[0]
    pairs = half_ranks // 2
    tokens = ids_ref.shape[1]

    @pl.when(step == 0)
    def _():
        lane = lax.broadcasted_iota(jnp.int32, (share, LANES), 1)
        block = 0
        for source in sources:
            for k in range(source.shape[0] // share):
                values = source[k * share:(k + 1) * share, :]
                at = pl.multiple_of(offs_ref[block] * share, share)
                block += 1
                high, low = split2(values)
                out_t[:, pl.ds(at, share)] = dot_nt(pick_ref[...], high) + dot_nt(pick_ref[...], low)
                in_twice[pl.ds(at, share), :] = jnp.where(
                    lane < ranks, values, pltpu.roll(values, ranks, 1)
                )
        ids_wide[...] = jnp.broadcast_to(ids_ref[...], ids_wide.shape)
        sq_ref[...] = jnp.zeros_like(sq_ref)

    slots = rows.shape[0]
    group = rows.shape[1] // pairs
    lane = lax.broadcasted_iota(jnp.int32, (LANES, LANES), 1)
    left_lanes = (lane < ranks).astype(F32).astype(BF16)
    right_lanes = (lane >= ranks).astype(F32).astype(BF16)

    def one_group(g, slot):
        number = step * (ex_block // group) + g
        start = start_ref[number]
        at = jnp.minimum(lax.div(start, LANES) * LANES, tokens - WINDOW)
        turn = lax.rem(WINDOW - (start - at), WINDOW)
        at = pl.multiple_of(at, LANES)
        out_win = pltpu.roll(out_t[:, pl.ds(at, WINDOW)], turn, 1)[:, :LANES]
        ids_win = pltpu.roll(ids_wide[:, pl.ds(at, WINDOW)], turn, 1)[:, :LANES]
        base = (number * group).astype(F32)
        lefts = ([], [])
        terms = split2(out_win)
        for e in range(group):
            mask = (ids_win == base + float(e)).astype(F32)
            mask = jnp.concatenate([mask] * (pairs // 8), axis=0).astype(BF16)
            for left, term in zip(lefts, terms):
                left.append(jnp.concatenate([term[:pairs] * mask, term[pairs:] * mask], axis=1))
        left = jnp.concatenate(lefts[0] + lefts[1], axis=0)
        high, low = split2(in_twice[pl.ds(start, LANES), :])
        right = jnp.concatenate(
            [
                jnp.concatenate([high * lanes, low * lanes], axis=1)
                for lanes in (left_lanes, right_lanes)
            ],
            axis=0,
        )
        res = dot_nn(left, right)
        top = group * pairs
        rows[slot] = (
            (res[:top, :LANES] + res[top:, :LANES]) + (res[:top, LANES:] + res[top:, LANES:])
        )
        to = pl.multiple_of(g * group, group)
        for pair in range(pairs):
            sketch[pl.ds(to, group), pair * LANES:(pair + 1) * LANES] = rows[
                slot, pl.ds(pair, group, stride=pairs), :
            ]

    @pl.loop(0, ex_block // group // slots)
    def _(turn):
        for slot in range(slots):
            one_group(turn * slots + slot, slot)

    values = sketch[...]
    high, low = split2(values)
    high_ref[...] = high
    low_ref[...] = low
    sq = jnp.sum((values * values).reshape(ex_block // 8, 8, -1), axis=0)
    total = sq[:, 0:LANES]
    for k in range(1, values.shape[1] // LANES):
        total = total + sq[:, k * LANES:(k + 1) * LANES]
    sq_ref[...] += total


def build(offs, starts, sources, ids, pick, ranks, share, comps):
    tokens = ids.shape[1]
    half_ranks = pick.shape[0]
    ex_block = 256
    group = 8
    whole = lambda i, *_: (0, 0)
    return pl.pallas_call(
        functools.partial(build_kernel, ranks, share, ex_block, len(sources)),
        out_shape=(
            jax.ShapeDtypeStruct((EX_DEV, comps), BF16),
            jax.ShapeDtypeStruct((EX_DEV, comps), BF16),
            jax.ShapeDtypeStruct((8, LANES), F32),
        ),
        grid_spec=pltpu.PrefetchScalarGridSpec(
            num_scalar_prefetch=2,
            grid=(EX_DEV // ex_block,),
            in_specs=[pl.BlockSpec(a.shape, whole) for a in (*sources, ids, pick)],
            out_specs=[
                pl.BlockSpec((ex_block, comps), lambda i, *_: (i, 0)),
                pl.BlockSpec((ex_block, comps), lambda i, *_: (i, 0)),
                pl.BlockSpec((8, LANES), whole),
            ],
            scratch_shapes=[
                pltpu.VMEM((half_ranks, tokens), F32),
                pltpu.VMEM((tokens, LANES), F32),
                pltpu.VMEM((8, tokens), F32),
                pltpu.VMEM((4, group * half_ranks // 2, LANES), F32),
                pltpu.VMEM((ex_block, comps), F32),
            ],
        ),
        compiler_params=pltpu.CompilerParams(vmem_limit_bytes=BUILD * MIB),
        cost_estimate=pl.CostEstimate(
            flops=12 * EX_DEV * half_ranks * WINDOW * 2 * LANES,
            bytes_accessed=4 * EX_DEV * comps + 4 * tokens * LANES,
            transcendentals=0,
        ),
    )(offs, starts, *sources, ids, pick)


def join_kernel(planes, *refs):
    highs, lows, squares = refs[:planes], refs[planes:2 * planes], refs[2 * planes:3 * planes]
    slots, out_ref, b_ref = refs[3 * planes:-2], refs[-2], refs[-1]
    width = slots[0].shape[1]
    for k, slot in enumerate(slots):
        b_ref[:, k * width:(k + 1) * width] = slot[...]
    b = b_ref[...]
    count = b.shape[0]
    b_both = jnp.concatenate(split2(b), axis=0)
    for k in range(planes):
        both = (dot_nt(highs[k][...], b_both) + dot_nt(lows[k][...], b_both)).T
        out_ref[:, k * EX_DEV:(k + 1) * EX_DEV] = both[:count] + both[count:]
    total = squares[0][...]
    for square in squares[1:]:
        total = total + square[...]
    total = jnp.sum(jnp.sum(total, axis=1, keepdims=True), axis=0, keepdims=True)
    norm = jnp.sum(b * b, axis=1, keepdims=True)
    out_ref[:, planes * EX_DEV:] = lanes_of([norm, total], (count, LANES))


def join(highs, lows, squares, slots):
    planes = len(highs)
    count, comps = slots[0].shape[0], highs[0].shape[1]
    return pl.pallas_call(
        functools.partial(join_kernel, planes),
        out_shape=(
            jax.ShapeDtypeStruct((count, planes * EX_DEV + LANES), F32),
            jax.ShapeDtypeStruct((count, comps), F32),
        ),
        compiler_params=pltpu.CompilerParams(vmem_limit_bytes=STEP * MIB),
        cost_estimate=pl.CostEstimate(
            flops=6 * planes * EX_DEV * count * comps,
            bytes_accessed=4 * planes * EX_DEV * comps,
            transcendentals=0,
        ),
    )(*highs, *lows, *squares, *slots)


def column(values, k):
    return values[:, k:k + 1]


def lanes_of(columns, shape):
    lane = lax.broadcasted_iota(jnp.int32, shape, 1)
    out = jnp.zeros(shape, F32)
    for k, one in enumerate(columns):
        out = jnp.where(lane == k, one, out)
    return out


def begin(first, examples, comps_all, mine, other, s_prev, state):
    total = mine + other
    inner, stats = total[:, :examples], total[:, examples:]
    norm = column(stats, 0)
    if first:
        damping = 0.1 * column(stats, 1) / (examples * comps_all)
        s, length, beta = inner, norm, None
    else:
        beta = norm / column(state, 0)
        s = inner + beta * s_prev
        length = norm + 2.0 * beta * column(stats, 1) + beta * beta * column(state, 1)
        damping = column(state, 2)
    bend = jnp.sum(s * s, axis=1, keepdims=True) / examples + damping * length
    return s, norm, length, damping, beta, norm / bend


def step_kernel(first, planes, examples, comps_all, *refs):
    refs = list(refs)
    take = lambda n: [refs.pop(0) for _ in range(n)]
    mine_ref, other_ref, r_ref = take(3)
    if not first:
        p_ref, x_ref, s_ref, y_ref, state_ref = take(5)
    highs, lows = take(planes), take(planes)
    msg_out, r_out, p_out, x_out, s_out, y_out, state_out = take(7)
    s_two, z_acc, stats_acc, scal = take(4)
    count, comps = r_ref.shape
    s, norm, length, damping, beta, alpha = begin(
        first, examples, comps_all, mine_ref[...], other_ref[...],
        None if first else s_ref[...], None if first else state_ref[...],
    )
    s_out[...] = s
    y_out[...] = alpha * s if first else y_ref[...] + alpha * s
    high, low = split2(s)
    s_two[0:count, :] = high
    s_two[count:2 * count, :] = low
    state_out[...] = lanes_of([norm, length, damping], state_out.shape)
    scal[...] = lanes_of([alpha, damping] + ([] if first else [beta]), scal.shape)
    z_acc[...] = jnp.zeros_like(z_acc)
    stats_acc[...] = jnp.zeros_like(stats_acc)
    block = 512

    @pl.loop(0, comps // block)
    def _(turn):
        at = pl.ds(pl.multiple_of(turn * block, block), block)
        alpha, damping = scal[:, 0:1], scal[:, 1:2]
        r = r_ref[:, at]
        if first:
            p = r
            x_out[:, at] = alpha * p
        else:
            p = r + scal[:, 2:3] * p_ref[:, at]
            x_out[:, at] = x_ref[:, at] + alpha * p
        p_out[:, at] = p
        q = jnp.zeros(r.shape, F32)
        for k in range(planes):
            part = slice(k * EX_DEV, (k + 1) * EX_DEV)
            both = dot_nn(s_two[:, part], highs[k][:, at])
            q = q + both[:count] + both[count:] + dot_nn(s_two[0:count, part], lows[k][:, at])
        r_new = r - alpha * (q / examples + damping * p)
        r_out[:, at] = r_new
        stacked = jnp.concatenate(split2(r_new), axis=0)
        for k in range(planes):
            part = slice(k * EX_DEV, (k + 1) * EX_DEV)
            z_acc[part, :] += dot_nt(highs[k][:, at], stacked) + dot_nt(lows[k][:, at], stacked)
        stats_acc[...] += lanes_of(
            [
                jnp.sum(r_new * r_new, axis=1, keepdims=True),
                jnp.sum(r_new * p, axis=1, keepdims=True),
            ],
            stats_acc.shape,
        )

    both = z_acc[...].T
    msg_out[:, 0:examples] = both[:count] + both[count:]
    msg_out[:, examples:] = stats_acc[...]


def one_step(first, examples, comps_all, mine, other, r, rest, highs, lows):
    planes = len(highs)
    count, comps = r.shape
    wide = jax.ShapeDtypeStruct((count, examples), F32)
    long = jax.ShapeDtypeStruct((count, comps), F32)
    small = jax.ShapeDtypeStruct((count, LANES), F32)
    message = jax.ShapeDtypeStruct((count, examples + LANES), F32)
    return pl.pallas_call(
        functools.partial(step_kernel, first, planes, examples, comps_all),
        out_shape=(message, long, long, long, wide, wide, small),
        scratch_shapes=[
            pltpu.VMEM((2 * count, examples), BF16),
            pltpu.VMEM((examples, 2 * count), F32),
            pltpu.VMEM((count, LANES), F32),
            pltpu.VMEM((count, LANES), F32),
        ],
        compiler_params=pltpu.CompilerParams(vmem_limit_bytes=STEP * MIB),
        cost_estimate=pl.CostEstimate(
            flops=12 * count * examples * comps,
            bytes_accessed=4 * examples * comps,
            transcendentals=0,
        ),
    )(mine, other, r, *rest, *highs, *lows)


def last_kernel(examples, comps_all, mine_ref, other_ref, r_ref, p_ref, x_ref, s_ref, y_ref, state_ref, x_out, y_out):
    s, _, _, _, beta, alpha = begin(
        False, examples, comps_all, mine_ref[...], other_ref[...], s_ref[...], state_ref[...]
    )
    scale = 1.0 / jnp.sqrt(F32(comps_all))
    y_out[...] = (y_ref[...] + alpha * s) * scale
    x_out[...] = x_ref[...] + alpha * (r_ref[...] + beta * p_ref[...])


def last_step(examples, comps_all, *arrays):
    x, y = arrays[4], arrays[6]
    return pl.pallas_call(
        functools.partial(last_kernel, examples, comps_all),
        out_shape=(jax.ShapeDtypeStruct(x.shape, F32), jax.ShapeDtypeStruct(y.shape, F32)),
        compiler_params=pltpu.CompilerParams(vmem_limit_bytes=STEP * MIB),
    )(*arrays)


def arrange_kernel(count, origin_ref, *refs):
    parts, outs, held = refs[:count], refs[count:-1], refs[-1]
    rows = parts[0].shape[0]
    for k, part in enumerate(parts):
        held[k * rows:(k + 1) * rows, :] = part[...]
    for k, out in enumerate(outs):
        out[...] = held[pl.ds(pl.multiple_of(origin_ref[k] * rows, rows), rows), :]


def arrange(origin, parts):
    rows, columns = parts[0].shape
    whole = pl.BlockSpec((rows, columns), lambda i, origin: (0, 0))
    return pl.pallas_call(
        functools.partial(arrange_kernel, len(parts)),
        out_shape=(jax.ShapeDtypeStruct((rows, columns), F32),) * origin.shape[0],
        grid_spec=pltpu.PrefetchScalarGridSpec(
            num_scalar_prefetch=1,
            grid=(1,),
            in_specs=[whole] * len(parts),
            out_specs=[whole] * origin.shape[0],
            scratch_shapes=[pltpu.VMEM((len(parts) * rows, columns), F32)],
        ),
        compiler_params=pltpu.CompilerParams(vmem_limit_bytes=8 * MIB),
    )(origin, *parts)


def place_kernel(slots, count, where_ref, *refs):
    arrays, out_ref, held = refs[:count], refs[count], refs[count + 1]
    rows = arrays[0].shape[0] // slots
    k = where_ref[pl.program_id(0)]
    for number, array in enumerate(arrays):
        to = where_ref[slots + number]

        @pl.when(to >= 0)
        def _():
            held[pl.ds(pl.multiple_of(to * rows, rows), rows), :] = array[
                pl.ds(pl.multiple_of(k * rows, rows), rows), :
            ]

    out_ref[...] = held[...].T


def place(where, arrays, slots, planes):
    rows, comps = arrays[0].shape[0] // slots * planes, arrays[0].shape[1]
    whole = pl.BlockSpec(arrays[0].shape, lambda i, where: (0, 0))
    return pl.pallas_call(
        functools.partial(place_kernel, slots, len(arrays)),
        out_shape=jax.ShapeDtypeStruct((comps, slots * rows), F32),
        grid_spec=pltpu.PrefetchScalarGridSpec(
            num_scalar_prefetch=1,
            grid=(slots,),
            in_specs=[whole] * len(arrays),
            out_specs=pl.BlockSpec((comps, rows), lambda i, where: (0, i)),
            scratch_shapes=[pltpu.VMEM((rows, comps), F32)],
        ),
        compiler_params=pltpu.CompilerParams(vmem_limit_bytes=24 * MIB),
    )(where, *arrays)


def per_device(n_dp, n_t, activations, out_grads, proj_in, proj_out, example_ids, queries):
    tokens = activations.shape[0]
    ranks = proj_in.shape[1]
    comps_all = proj_in.shape[1] * proj_out.shape[1]
    examples = EX_DEV * n_dp
    n_c = n_t // 2
    j = lax.axis_index("tensor")
    i = lax.axis_index("dp")
    chip, core = j // 2, j % 2

    def swap(values, mask):
        return lax.ppermute(values, "tensor", [(a, a ^ mask) for a in range(n_t)])

    def shift(values, by):
        return lax.ppermute(values, "dp", [(a, (a + by) % n_dp) for a in range(n_dp)])

    def tie(values, token):
        return lax.optimization_barrier((values, token))[0]

    near_chip = [chip ^ k for k in range(n_c)]

    q_chip = queries.shape[0] // n_dp
    parts = [
        lax.dynamic_slice_in_dim(queries, (i + away) % n_dp * q_chip, q_chip, 0) for away in range(n_dp)
    ]
    origin = jnp.stack([(i - near_chip[k]) % n_dp for k in range(n_c)]).astype(jnp.int32)

    group = 8
    bounds = group * jnp.arange(EX_DEV // group, dtype=jnp.int32)
    starts = jnp.sum((example_ids[0][None, :] < bounds[:, None]).astype(F32), axis=1)
    starts = jnp.minimum(starts, F32(tokens - LANES))
    id_rows = tokens // LANES
    extra = jnp.concatenate(
        [
            example_ids.astype(F32).reshape((id_rows, LANES)),
            jnp.pad(starts[None, :], ((0, 7), (0, LANES - EX_DEV // group))),
        ],
        axis=0,
    )

    share = tokens // n_t
    blocks = jnp.stack(near_chip).astype(jnp.int32) * 2
    w_in, w_out = proj_in.T, proj_out.T
    give = project(blocks + 1 - core, activations, out_grads, w_in, w_out, share)
    keep = project(blocks + core, activations, out_grads, w_in, w_out, share)
    extra = tie(extra, give)
    extras = [extra] + [shift(extra, away) for away in range(1, n_dp)]
    plane_ids = [one[:id_rows].reshape((1, tokens)) for one in extras]
    firsts = [one[id_rows, :EX_DEV // group].astype(jnp.int32) for one in extras]
    kept = (keep + swap(give, 1)).reshape((n_c, share, LANES))
    own = kept[0]
    for k in range(1, n_c):
        own = own + swap(kept[k], 2 * k)

    rings = [own]
    for _ in range(n_dp - 1):
        rings.append(shift(rings[-1], 1))

    per = comps_all // ranks // n_t
    wanted = [(near_chip[k] * 2 + core) * per + a + ranks for k in range(n_c) for a in range(per)]
    wanted = jnp.stack(wanted[0::2] + wanted[1::2])
    pick = (wanted[:, None] == jnp.arange(LANES)[None, :]).astype(BF16)

    offs = jnp.stack(
        [near_chip[k] * 2 + which for which in (core, 1 - core) for k in range(n_c)]
    ).astype(jnp.int32)
    offs, pick, plane_ids, firsts, parts, origin = lax.optimization_barrier(
        (offs, pick, plane_ids, firsts, parts, origin)
    )

    highs, lows, squares = [], [], []
    for away in range(n_dp):
        if away == n_dp // 2:
            slots = arrange(origin, [parts[0]] + [shift(parts[k], k) for k in range(1, n_dp)])
            pick = tie(pick, slots)
        piece = rings[away]
        near = [piece] + [swap(piece, 2 * k) for k in range(1, n_c)]
        sources = near + [
            swap(part, 1) for part in (tie(near, squares[-1]) if squares else near)
        ]
        high, low, square = build(
            offs, firsts[away], sources, plane_ids[away], pick, ranks, share, comps_all // 2
        )
        highs.append(high)
        lows.append(low)
        squares.append(square)

    slots = [slots[0]] + [swap(slots[k], 2 * k) for k in range(1, n_c)]
    message, b = join(highs, lows, squares, slots)
    r, rest = b, ()
    for step in range(ITERS - 1):
        other = swap(message, 1)
        message, r, p, x, s, y, state = one_step(
            step == 0, examples, comps_all, message, other, r, rest, highs, lows
        )
        rest = (p, x, s, y, state)
    other = swap(message, 1)
    x, y = last_step(examples, comps_all, message, other, r, *rest)

    n_half = n_dp // 2
    per_slot = comps_all // n_t

    def send(values, by):
        pairs = [
            (a * n_t + 2 * c + a // n_half, (a + by) % n_dp * n_t + 2 * c + a // n_half)
            for a in range(n_dp) for c in range(n_c)
        ]
        return lax.ppermute(values, ("dp", "tensor"), pairs)

    by_plane = jnp.zeros((n_dp, q_chip, EX_DEV), F32)
    for away in range(n_dp):
        part = y[:, away * EX_DEV:(away + 1) * EX_DEV]
        if away:
            part = send(part, -away)
        by_plane = lax.dynamic_update_slice(by_plane, part[None], ((i + away) % n_dp, 0, 0))
    scores = lax.dynamic_slice_in_dim(by_plane, core * n_half, n_half, 0)

    ring = [x[:, k * per_slot:(k + 1) * per_slot] for k in range(n_c)]
    ring = jnp.concatenate([ring[0]] + [swap(ring[k], 2 * k) for k in range(1, n_c)], axis=0)
    arrays, places = [ring], [i]
    ups = downs = ring
    for away in range(1, n_dp):
        if away == 2:
            ups, downs = tie((ups, downs), scores)
        ups = lax.ppermute(ups, "dp", [(a, a + 1) for a in range(away - 1, n_dp - 1)])
        downs = lax.ppermute(downs, "dp", [(a, a - 1) for a in range(1, n_dp - away + 1)])
        arrays += [ups, downs]
        places += [jnp.maximum(i - away, -1), jnp.where(i + away < n_dp, i + away, -1)]
    where = jnp.stack([chip ^ c for c in range(n_c)] + places).astype(jnp.int32)
    out = place(where, arrays, n_c, n_dp)
    return (out, scores.reshape((n_half * q_chip, EX_DEV)))


def solution(mesh):
    in_specs = (
        P("dp", "tensor"),
        P("dp", "tensor"),
        P("tensor", None),
        P("tensor", None),
        P("dp", None),
        P("dp", "tensor"),
    )
    out_specs = (P("tensor", None), P("tensor", "dp"))
    body = functools.partial(per_device, mesh.shape["dp"], mesh.shape["tensor"])
    return jax.shard_map(body, mesh=mesh, in_specs=in_specs, out_specs=out_specs, check_vma=False)
```

```python
import functools

import jax
import jax.numpy as jnp
from jax import lax
from jax.experimental import pallas as pl
from jax.experimental.pallas import tpu as pltpu
from jax.sharding import PartitionSpec as P

ITERS = 4
EX_DEV = 512
LANES = 128
WINDOW = 256
PARTS = 4
F32 = jnp.float32
BF16 = jnp.bfloat16
MIB = 1024 * 1024
BUILD = 24
STEP = 24


def split2(values):
    high = values.astype(BF16)
    low = (values - high.astype(F32)).astype(BF16)
    return high, low


def dot_nn(left, right):
    return lax.dot_general(left, right, (((1,), (0,)), ((), ())), preferred_element_type=F32)


def dot_nt(left, right):
    return lax.dot_general(left, right, (((1,), (1,)), ((), ())), preferred_element_type=F32)


def project_kernel(order_ref, *refs):
    del order_ref
    acts, grads = refs[:PARTS], refs[PARTS:2 * PARTS]
    wi_ref, wo_ref, out_ref = refs[2 * PARTS:]
    rows = acts[0].shape[0]
    for part, (act_ref, grad_ref) in enumerate(zip(acts, grads)):
        out_ref[part * rows:(part + 1) * rows, :] = jnp.concatenate(
            [dot_nt(act_ref[...], wi_ref[...]), dot_nt(grad_ref[...], wo_ref[...])], axis=1
        )


def project(order, activations, out_grads, w_in, w_out, block):
    steps = order.shape[0]
    feats, hidden = activations.shape[1], out_grads.shape[1]
    rows = block // PARTS

    def parts(width):
        return [
            pl.BlockSpec((rows, width), lambda i, order, part=part: (order[i] * PARTS + part, 0))
            for part in range(PARTS)
        ]

    return pl.pallas_call(
        project_kernel,
        out_shape=jax.ShapeDtypeStruct((steps * block, LANES), F32),
        grid_spec=pltpu.PrefetchScalarGridSpec(
            num_scalar_prefetch=1,
            grid=(steps,),
            in_specs=parts(feats) + parts(hidden) + [
                pl.BlockSpec(w_in.shape, lambda i, order: (0, 0)),
                pl.BlockSpec(w_out.shape, lambda i, order: (0, 0)),
            ],
            out_specs=pl.BlockSpec((block, LANES), lambda i, order: (i, 0)),
        ),
        compiler_params=pltpu.CompilerParams(vmem_limit_bytes=61 * MIB),
        cost_estimate=pl.CostEstimate(
            flops=2 * steps * block * (feats + hidden) * 4 * WINDOW,
            bytes_accessed=2 * steps * block * (feats + hidden),
            transcendentals=0,
        ),
    )(order, *[activations] * PARTS, *[out_grads] * PARTS, w_in, w_out)


def build_kernel(ranks, share, ex_block, n_sources, *refs):
    offs_ref, start_ref = refs[:2]
    sources = refs[2:2 + n_sources]
    ids_ref, pick_ref = refs[2 + n_sources:4 + n_sources]
    high_ref, low_ref, sq_ref = refs[4 + n_sources:7 + n_sources]
    out_t, in_twice, ids_wide, rows, sketch = refs[7 + n_sources:]
    step = pl.program_id(0)
    half_ranks = pick_ref.shape[0]
    pairs = half_ranks // 2
    tokens = ids_ref.shape[1]

    @pl.when(step == 0)
    def _():
        lane = lax.broadcasted_iota(jnp.int32, (share, LANES), 1)
        block = 0
        for source in sources:
            for k in range(source.shape[0] // share):
                values = source[k * share:(k + 1) * share, :]
                at = pl.multiple_of(offs_ref[block] * share, share)
                block += 1
                high, low = split2(values)
                out_t[:, pl.ds(at, share)] = dot_nt(pick_ref[...], high) + dot_nt(pick_ref[...], low)
                in_twice[pl.ds(at, share), :] = jnp.where(
                    lane < ranks, values, pltpu.roll(values, ranks, 1)
                )
        ids_wide[...] = jnp.broadcast_to(ids_ref[...], ids_wide.shape)
        sq_ref[...] = jnp.zeros_like(sq_ref)

    slots = rows.shape[0]
    group = rows.shape[1] // pairs
    lane = lax.broadcasted_iota(jnp.int32, (LANES, LANES), 1)
    left_lanes = (lane < ranks).astype(F32).astype(BF16)
    right_lanes = (lane >= ranks).astype(F32).astype(BF16)

    def one_group(g, slot):
        number = step * (ex_block // group) + g
        start = start_ref[number]
        at = jnp.minimum(lax.div(start, LANES) * LANES, tokens - WINDOW)
        turn = lax.rem(WINDOW - (start - at), WINDOW)
        at = pl.multiple_of(at, LANES)
        out_win = pltpu.roll(out_t[:, pl.ds(at, WINDOW)], turn, 1)[:, :LANES]
        ids_win = pltpu.roll(ids_wide[:, pl.ds(at, WINDOW)], turn, 1)[:, :LANES]
        base = (number * group).astype(F32)
        lefts = ([], [])
        terms = split2(out_win)
        for e in range(group):
            mask = (ids_win == base + float(e)).astype(F32)
            mask = jnp.concatenate([mask] * (pairs // 8), axis=0).astype(BF16)
            for left, term in zip(lefts, terms):
                left.append(jnp.concatenate([term[:pairs] * mask, term[pairs:] * mask], axis=1))
        left = jnp.concatenate(lefts[0] + lefts[1], axis=0)
        high, low = split2(in_twice[pl.ds(start, LANES), :])
        right = jnp.concatenate(
            [
                jnp.concatenate([high * lanes, low * lanes], axis=1)
                for lanes in (left_lanes, right_lanes)
            ],
            axis=0,
        )
        res = dot_nn(left, right)
        top = group * pairs
        rows[slot] = (
            (res[:top, :LANES] + res[top:, :LANES]) + (res[:top, LANES:] + res[top:, LANES:])
        )
        to = pl.multiple_of(g * group, group)
        for pair in range(pairs):
            sketch[pl.ds(to, group), pair * LANES:(pair + 1) * LANES] = rows[
                slot, pl.ds(pair, group, stride=pairs), :
            ]

    @pl.loop(0, ex_block // group // slots)
    def _(turn):
        for slot in range(slots):
            one_group(turn * slots + slot, slot)

    values = sketch[...]
    high, low = split2(values)
    high_ref[...] = high
    low_ref[...] = low
    sq = jnp.sum((values * values).reshape(ex_block // 8, 8, -1), axis=0)
    total = sq[:, 0:LANES]
    for k in range(1, values.shape[1] // LANES):
        total = total + sq[:, k * LANES:(k + 1) * LANES]
    sq_ref[...] += total


def build(offs, starts, sources, ids, pick, ranks, share, comps):
    tokens = ids.shape[1]
    half_ranks = pick.shape[0]
    ex_block = 256
    group = 8
    whole = lambda i, *_: (0, 0)
    return pl.pallas_call(
        functools.partial(build_kernel, ranks, share, ex_block, len(sources)),
        out_shape=(
            jax.ShapeDtypeStruct((EX_DEV, comps), BF16),
            jax.ShapeDtypeStruct((EX_DEV, comps), BF16),
            jax.ShapeDtypeStruct((8, LANES), F32),
        ),
        grid_spec=pltpu.PrefetchScalarGridSpec(
            num_scalar_prefetch=2,
            grid=(EX_DEV // ex_block,),
            in_specs=[pl.BlockSpec(a.shape, whole) for a in (*sources, ids, pick)],
            out_specs=[
                pl.BlockSpec((ex_block, comps), lambda i, *_: (i, 0)),
                pl.BlockSpec((ex_block, comps), lambda i, *_: (i, 0)),
                pl.BlockSpec((8, LANES), whole),
            ],
            scratch_shapes=[
                pltpu.VMEM((half_ranks, tokens), F32),
                pltpu.VMEM((tokens, LANES), F32),
                pltpu.VMEM((8, tokens), F32),
                pltpu.VMEM((4, group * half_ranks // 2, LANES), F32),
                pltpu.VMEM((ex_block, comps), F32),
            ],
        ),
        compiler_params=pltpu.CompilerParams(vmem_limit_bytes=BUILD * MIB),
        cost_estimate=pl.CostEstimate(
            flops=12 * EX_DEV * half_ranks * WINDOW * 2 * LANES,
            bytes_accessed=4 * EX_DEV * comps + 4 * tokens * LANES,
            transcendentals=0,
        ),
    )(offs, starts, *sources, ids, pick)


def join_kernel(planes, *refs):
    highs, lows, squares = refs[:planes], refs[planes:2 * planes], refs[2 * planes:3 * planes]
    slots, out_ref, b_ref = refs[3 * planes:-2], refs[-2], refs[-1]
    width = slots[0].shape[1]
    for k, slot in enumerate(slots):
        b_ref[:, k * width:(k + 1) * width] = slot[...]
    b = b_ref[...]
    count = b.shape[0]
    b_both = jnp.concatenate(split2(b), axis=0)
    for k in range(planes):
        both = (dot_nt(highs[k][...], b_both) + dot_nt(lows[k][...], b_both)).T
        out_ref[:, k * EX_DEV:(k + 1) * EX_DEV] = both[:count] + both[count:]
    total = squares[0][...]
    for square in squares[1:]:
        total = total + square[...]
    total = jnp.sum(jnp.sum(total, axis=1, keepdims=True), axis=0, keepdims=True)
    norm = jnp.sum(b * b, axis=1, keepdims=True)
    out_ref[:, planes * EX_DEV:] = lanes_of([norm, total], (count, LANES))


def join(highs, lows, squares, slots):
    planes = len(highs)
    count, comps = slots[0].shape[0], highs[0].shape[1]
    return pl.pallas_call(
        functools.partial(join_kernel, planes),
        out_shape=(
            jax.ShapeDtypeStruct((count, planes * EX_DEV + LANES), F32),
            jax.ShapeDtypeStruct((count, comps), F32),
        ),
        compiler_params=pltpu.CompilerParams(vmem_limit_bytes=STEP * MIB),
        cost_estimate=pl.CostEstimate(
            flops=6 * planes * EX_DEV * count * comps,
            bytes_accessed=4 * planes * EX_DEV * comps,
            transcendentals=0,
        ),
    )(*highs, *lows, *squares, *slots)


def column(values, k):
    return values[:, k:k + 1]


def lanes_of(columns, shape):
    lane = lax.broadcasted_iota(jnp.int32, shape, 1)
    out = jnp.zeros(shape, F32)
    for k, one in enumerate(columns):
        out = jnp.where(lane == k, one, out)
    return out


def begin(first, examples, comps_all, mine, other, s_prev, state):
    total = mine + other
    inner, stats = total[:, :examples], total[:, examples:]
    norm = column(stats, 0)
    if first:
        damping = 0.1 * column(stats, 1) / (examples * comps_all)
        s, length, beta = inner, norm, None
    else:
        beta = norm / column(state, 0)
        s = inner + beta * s_prev
        length = norm + 2.0 * beta * column(stats, 1) + beta * beta * column(state, 1)
        damping = column(state, 2)
    bend = jnp.sum(s * s, axis=1, keepdims=True) / examples + damping * length
    return s, norm, length, damping, beta, norm / bend


def step_kernel(first, planes, examples, comps_all, *refs):
    refs = list(refs)
    take = lambda n: [refs.pop(0) for _ in range(n)]
    mine_ref, other_ref, r_ref = take(3)
    if not first:
        p_ref, x_ref, s_ref, y_ref, state_ref = take(5)
    highs, lows = take(planes), take(planes)
    msg_out, r_out, p_out, x_out, s_out, y_out, state_out = take(7)
    s_two, z_acc, stats_acc, scal = take(4)
    count, comps = r_ref.shape
    s, norm, length, damping, beta, alpha = begin(
        first, examples, comps_all, mine_ref[...], other_ref[...],
        None if first else s_ref[...], None if first else state_ref[...],
    )
    s_out[...] = s
    y_out[...] = alpha * s if first else y_ref[...] + alpha * s
    high, low = split2(s)
    s_two[0:count, :] = high
    s_two[count:2 * count, :] = low
    state_out[...] = lanes_of([norm, length, damping], state_out.shape)
    scal[...] = lanes_of([alpha, damping] + ([] if first else [beta]), scal.shape)
    z_acc[...] = jnp.zeros_like(z_acc)
    stats_acc[...] = jnp.zeros_like(stats_acc)
    block = 512

    @pl.loop(0, comps // block)
    def _(turn):
        at = pl.ds(pl.multiple_of(turn * block, block), block)
        alpha, damping = scal[:, 0:1], scal[:, 1:2]
        r = r_ref[:, at]
        if first:
            p = r
            x_out[:, at] = alpha * p
        else:
            p = r + scal[:, 2:3] * p_ref[:, at]
            x_out[:, at] = x_ref[:, at] + alpha * p
        p_out[:, at] = p
        q = jnp.zeros(r.shape, F32)
        for k in range(planes):
            part = slice(k * EX_DEV, (k + 1) * EX_DEV)
            both = dot_nn(s_two[:, part], highs[k][:, at])
            q = q + both[:count] + both[count:] + dot_nn(s_two[0:count, part], lows[k][:, at])
        r_new = r - alpha * (q / examples + damping * p)
        r_out[:, at] = r_new
        stacked = jnp.concatenate(split2(r_new), axis=0)
        for k in range(planes):
            part = slice(k * EX_DEV, (k + 1) * EX_DEV)
            z_acc[part, :] += dot_nt(highs[k][:, at], stacked) + dot_nt(lows[k][:, at], stacked)
        stats_acc[...] += lanes_of(
            [
                jnp.sum(r_new * r_new, axis=1, keepdims=True),
                jnp.sum(r_new * p, axis=1, keepdims=True),
            ],
            stats_acc.shape,
        )

    both = z_acc[...].T
    msg_out[:, 0:examples] = both[:count] + both[count:]
    msg_out[:, examples:] = stats_acc[...]


def one_step(first, examples, comps_all, mine, other, r, rest, highs, lows):
    planes = len(highs)
    count, comps = r.shape
    wide = jax.ShapeDtypeStruct((count, examples), F32)
    long = jax.ShapeDtypeStruct((count, comps), F32)
    small = jax.ShapeDtypeStruct((count, LANES), F32)
    message = jax.ShapeDtypeStruct((count, examples + LANES), F32)
    return pl.pallas_call(
        functools.partial(step_kernel, first, planes, examples, comps_all),
        out_shape=(message, long, long, long, wide, wide, small),
        scratch_shapes=[
            pltpu.VMEM((2 * count, examples), BF16),
            pltpu.VMEM((examples, 2 * count), F32),
            pltpu.VMEM((count, LANES), F32),
            pltpu.VMEM((count, LANES), F32),
        ],
        compiler_params=pltpu.CompilerParams(vmem_limit_bytes=STEP * MIB),
        cost_estimate=pl.CostEstimate(
            flops=12 * count * examples * comps,
            bytes_accessed=4 * examples * comps,
            transcendentals=0,
        ),
    )(mine, other, r, *rest, *highs, *lows)


def last_kernel(examples, comps_all, mine_ref, other_ref, r_ref, p_ref, x_ref, s_ref, y_ref, state_ref, x_out, y_out):
    s, _, _, _, beta, alpha = begin(
        False, examples, comps_all, mine_ref[...], other_ref[...], s_ref[...], state_ref[...]
    )
    scale = 1.0 / jnp.sqrt(F32(comps_all))
    y_out[...] = (y_ref[...] + alpha * s) * scale
    x_out[...] = x_ref[...] + alpha * (r_ref[...] + beta * p_ref[...])


def last_step(examples, comps_all, *arrays):
    x, y = arrays[4], arrays[6]
    return pl.pallas_call(
        functools.partial(last_kernel, examples, comps_all),
        out_shape=(jax.ShapeDtypeStruct(x.shape, F32), jax.ShapeDtypeStruct(y.shape, F32)),
        compiler_params=pltpu.CompilerParams(vmem_limit_bytes=STEP * MIB),
    )(*arrays)


def arrange_kernel(count, origin_ref, *refs):
    parts, outs, held = refs[:count], refs[count:-1], refs[-1]
    rows = parts[0].shape[0]
    for k, part in enumerate(parts):
        held[k * rows:(k + 1) * rows, :] = part[...]
    for k, out in enumerate(outs):
        out[...] = held[pl.ds(pl.multiple_of(origin_ref[k] * rows, rows), rows), :]


def arrange(origin, parts):
    rows, columns = parts[0].shape
    whole = pl.BlockSpec((rows, columns), lambda i, origin: (0, 0))
    return pl.pallas_call(
        functools.partial(arrange_kernel, len(parts)),
        out_shape=(jax.ShapeDtypeStruct((rows, columns), F32),) * origin.shape[0],
        grid_spec=pltpu.PrefetchScalarGridSpec(
            num_scalar_prefetch=1,
            grid=(1,),
            in_specs=[whole] * len(parts),
            out_specs=[whole] * origin.shape[0],
            scratch_shapes=[pltpu.VMEM((len(parts) * rows, columns), F32)],
        ),
        compiler_params=pltpu.CompilerParams(vmem_limit_bytes=8 * MIB),
    )(origin, *parts)


def place_kernel(slots, count, where_ref, *refs):
    arrays, out_ref, held = refs[:count], refs[count], refs[count + 1]
    rows = arrays[0].shape[0] // slots
    k = where_ref[pl.program_id(0)]
    for number, array in enumerate(arrays):
        to = where_ref[slots + number]
        held[pl.ds(pl.multiple_of(to * rows, rows), rows), :] = array[
            pl.ds(pl.multiple_of(k * rows, rows), rows), :
        ]
    out_ref[...] = held[...].T


def place(where, arrays, slots, planes):
    rows, comps = arrays[0].shape[0] // slots * planes, arrays[0].shape[1]
    whole = pl.BlockSpec(arrays[0].shape, lambda i, where: (0, 0))
    return pl.pallas_call(
        functools.partial(place_kernel, slots, len(arrays)),
        out_shape=jax.ShapeDtypeStruct((comps, slots * rows), F32),
        grid_spec=pltpu.PrefetchScalarGridSpec(
            num_scalar_prefetch=1,
            grid=(slots,),
            in_specs=[whole] * len(arrays),
            out_specs=pl.BlockSpec((comps, rows), lambda i, where: (0, i)),
            scratch_shapes=[pltpu.VMEM((rows, comps), F32)],
        ),
        compiler_params=pltpu.CompilerParams(vmem_limit_bytes=24 * MIB),
    )(where, *arrays)


def per_device(n_dp, n_t, activations, out_grads, proj_in, proj_out, example_ids, queries):
    tokens = activations.shape[0]
    ranks = proj_in.shape[1]
    comps_all = proj_in.shape[1] * proj_out.shape[1]
    examples = EX_DEV * n_dp
    n_c = n_t // 2
    j = lax.axis_index("tensor")
    i = lax.axis_index("dp")
    chip, core = j // 2, j % 2

    def swap(values, mask):
        return lax.ppermute(values, "tensor", [(a, a ^ mask) for a in range(n_t)])

    def shift(values, by):
        return lax.ppermute(values, "dp", [(a, (a + by) % n_dp) for a in range(n_dp)])

    def tie(values, token):
        return lax.optimization_barrier((values, token))[0]

    near_chip = [chip ^ k for k in range(n_c)]

    q_chip = queries.shape[0] // n_dp
    parts = [
        lax.dynamic_slice_in_dim(queries, (i + away) % n_dp * q_chip, q_chip, 0) for away in range(n_dp)
    ]
    origin = jnp.stack([(i - near_chip[k]) % n_dp for k in range(n_c)]).astype(jnp.int32)

    group = 8
    bounds = group * jnp.arange(EX_DEV // group, dtype=jnp.int32)
    starts = jnp.sum((example_ids[0][None, :] < bounds[:, None]).astype(F32), axis=1)
    starts = jnp.minimum(starts, F32(tokens - LANES))
    id_rows = tokens // LANES
    extra = jnp.concatenate(
        [
            example_ids.astype(F32).reshape((id_rows, LANES)),
            jnp.pad(starts[None, :], ((0, 7), (0, LANES - EX_DEV // group))),
        ],
        axis=0,
    )

    share = tokens // n_t
    blocks = jnp.stack(near_chip).astype(jnp.int32) * 2
    w_in, w_out = proj_in.T, proj_out.T
    give = project(blocks + 1 - core, activations, out_grads, w_in, w_out, share)
    keep = project(blocks + core, activations, out_grads, w_in, w_out, share)
    kept = (keep + swap(give, 1)).reshape((n_c, share, LANES))
    kept, extra, parts = lax.optimization_barrier((kept, extra, parts))
    extras = [extra] + [shift(extra, away) for away in range(1, n_dp)]
    plane_ids = [one[:id_rows].reshape((1, tokens)) for one in extras]
    firsts = [one[id_rows, :EX_DEV // group].astype(jnp.int32) for one in extras]
    own = kept[0]
    for k in range(1, n_c):
        own = own + swap(kept[k], 2 * k)

    parts = [parts[0]] + [shift(parts[k], k) for k in range(1, n_dp)]
    own, parts, plane_ids, firsts = lax.optimization_barrier((own, parts, plane_ids, firsts))

    rings = [own]
    for _ in range(n_dp - 1):
        rings.append(shift(rings[-1], 1))

    per = comps_all // ranks // n_t
    wanted = [(near_chip[k] * 2 + core) * per + a + ranks for k in range(n_c) for a in range(per)]
    wanted = jnp.stack(wanted[0::2] + wanted[1::2])
    pick = (wanted[:, None] == jnp.arange(LANES)[None, :]).astype(BF16)

    offs = jnp.stack(
        [near_chip[k] * 2 + which for which in (core, 1 - core) for k in range(n_c)]
    ).astype(jnp.int32)
    offs, pick, plane_ids, firsts, slots = lax.optimization_barrier(
        (offs, pick, plane_ids, firsts, arrange(origin, parts))
    )

    highs, lows, squares = [], [], []
    for away in range(n_dp):
        piece = rings[away]
        near = [piece] + [swap(piece, 2 * k) for k in range(1, n_c)]
        sources = near + [
            swap(part, 1) for part in (tie(near, squares[-1]) if squares else near)
        ]
        high, low, square = build(
            offs, firsts[away], sources, plane_ids[away], pick, ranks, share, comps_all // 2
        )
        highs.append(high)
        lows.append(low)
        squares.append(square)

    slots = [slots[0]] + [swap(slots[k], 2 * k) for k in range(1, n_c)]
    message, b = join(highs, lows, squares, slots)
    r, rest = b, ()
    for step in range(ITERS - 1):
        other = swap(message, 1)
        message, r, p, x, s, y, state = one_step(
            step == 0, examples, comps_all, message, other, r, rest, highs, lows
        )
        rest = (p, x, s, y, state)
    other = swap(message, 1)
    x, y = last_step(examples, comps_all, message, other, r, *rest)

    n_half = n_dp // 2
    per_slot = comps_all // n_t

    def send(values, by):
        pairs = [
            (a * n_t + 2 * c + a // n_half, (a + by) % n_dp * n_t + 2 * c + a // n_half)
            for a in range(n_dp) for c in range(n_c)
        ]
        return lax.ppermute(values, ("dp", "tensor"), pairs)

    by_plane = jnp.zeros((n_dp, q_chip, EX_DEV), F32)
    for away in range(n_dp):
        part = y[:, away * EX_DEV:(away + 1) * EX_DEV]
        if away:
            part = send(part, -away)
        by_plane = lax.dynamic_update_slice(by_plane, part[None], ((i + away) % n_dp, 0, 0))
    scores = lax.dynamic_slice_in_dim(by_plane, core * n_half, n_half, 0)

    ring = [x[:, k * per_slot:(k + 1) * per_slot] for k in range(n_c)]
    ring = jnp.concatenate([ring[0]] + [swap(ring[k], 2 * k) for k in range(1, n_c)], axis=0)
    arrays, places = [ring], [i]
    for away in range(1, n_dp):
        ring = shift(tie(ring, scores) if away == 2 else ring, 1)
        arrays.append(ring)
        places.append((i - away) % n_dp)
    where = jnp.stack([chip ^ c for c in range(n_c)] + places).astype(jnp.int32)
    out = place(where, arrays, n_c, n_dp)
    return (out, scores.reshape((n_half * q_chip, EX_DEV)))


def solution(mesh):
    in_specs = (
        P("dp", "tensor"),
        P("dp", "tensor"),
        P("tensor", None),
        P("tensor", None),
        P("dp", None),
        P("dp", "tensor"),
    )
    out_specs = (P("tensor", None), P("tensor", "dp"))
    body = functools.partial(per_device, mesh.shape["dp"], mesh.shape["tensor"])
    return jax.shard_map(body, mesh=mesh, in_specs=in_specs, out_specs=out_specs, check_vma=False)
```

```python
import functools

import jax
import jax.numpy as jnp
from jax import lax
from jax.experimental import pallas as pl
from jax.experimental.pallas import tpu as pltpu
from jax.sharding import PartitionSpec as P

ITERS = 4
EX_DEV = 512
LANES = 128
WINDOW = 256
PARTS = 4
F32 = jnp.float32
BF16 = jnp.bfloat16
MIB = 1024 * 1024
BUILD = 24
STEP = 24


def split2(values):
    high = values.astype(BF16)
    low = (values - high.astype(F32)).astype(BF16)
    return high, low


def dot_nn(left, right):
    return lax.dot_general(left, right, (((1,), (0,)), ((), ())), preferred_element_type=F32)


def dot_nt(left, right):
    return lax.dot_general(left, right, (((1,), (1,)), ((), ())), preferred_element_type=F32)


def project_kernel(order_ref, *refs):
    del order_ref
    acts, grads = refs[:PARTS], refs[PARTS:2 * PARTS]
    wi_ref, wo_ref, out_ref = refs[2 * PARTS:]
    rows = acts[0].shape[0]
    for part, (act_ref, grad_ref) in enumerate(zip(acts, grads)):
        out_ref[part * rows:(part + 1) * rows, :] = jnp.concatenate(
            [dot_nt(act_ref[...], wi_ref[...]), dot_nt(grad_ref[...], wo_ref[...])], axis=1
        )


def project(order, activations, out_grads, w_in, w_out, block):
    steps = order.shape[0]
    feats, hidden = activations.shape[1], out_grads.shape[1]
    rows = block // PARTS

    def parts(width):
        return [
            pl.BlockSpec((rows, width), lambda i, order, part=part: (order[i] * PARTS + part, 0))
            for part in range(PARTS)
        ]

    return pl.pallas_call(
        project_kernel,
        out_shape=jax.ShapeDtypeStruct((steps * block, LANES), F32),
        grid_spec=pltpu.PrefetchScalarGridSpec(
            num_scalar_prefetch=1,
            grid=(steps,),
            in_specs=parts(feats) + parts(hidden) + [
                pl.BlockSpec(w_in.shape, lambda i, order: (0, 0)),
                pl.BlockSpec(w_out.shape, lambda i, order: (0, 0)),
            ],
            out_specs=pl.BlockSpec((block, LANES), lambda i, order: (i, 0)),
        ),
        compiler_params=pltpu.CompilerParams(vmem_limit_bytes=61 * MIB),
        cost_estimate=pl.CostEstimate(
            flops=2 * steps * block * (feats + hidden) * 4 * WINDOW,
            bytes_accessed=2 * steps * block * (feats + hidden),
            transcendentals=0,
        ),
    )(order, *[activations] * PARTS, *[out_grads] * PARTS, w_in, w_out)


def build_kernel(ranks, share, ex_block, n_sources, *refs):
    offs_ref, start_ref = refs[:2]
    sources = refs[2:2 + n_sources]
    ids_ref, pick_ref = refs[2 + n_sources:4 + n_sources]
    high_ref, low_ref, sq_ref = refs[4 + n_sources:7 + n_sources]
    out_t, in_twice, ids_wide, rows, sketch = refs[7 + n_sources:]
    step = pl.program_id(0)
    half_ranks = pick_ref.shape[0]
    pairs = half_ranks // 2
    tokens = ids_ref.shape[1]

    @pl.when(step == 0)
    def _():
        lane = lax.broadcasted_iota(jnp.int32, (share, LANES), 1)
        block = 0
        for source in sources:
            for k in range(source.shape[0] // share):
                values = source[k * share:(k + 1) * share, :]
                at = pl.multiple_of(offs_ref[block] * share, share)
                block += 1
                high, low = split2(values)
                out_t[:, pl.ds(at, share)] = dot_nt(pick_ref[...], high) + dot_nt(pick_ref[...], low)
                in_twice[pl.ds(at, share), :] = jnp.where(
                    lane < ranks, values, pltpu.roll(values, ranks, 1)
                )
        ids_wide[...] = jnp.broadcast_to(ids_ref[...], ids_wide.shape)
        sq_ref[...] = jnp.zeros_like(sq_ref)

    slots = rows.shape[0]
    group = rows.shape[1] // pairs
    lane = lax.broadcasted_iota(jnp.int32, (LANES, LANES), 1)
    left_lanes = (lane < ranks).astype(F32).astype(BF16)
    right_lanes = (lane >= ranks).astype(F32).astype(BF16)

    def one_group(g, slot):
        number = step * (ex_block // group) + g
        start = start_ref[number]
        at = jnp.minimum(lax.div(start, LANES) * LANES, tokens - WINDOW)
        turn = lax.rem(WINDOW - (start - at), WINDOW)
        at = pl.multiple_of(at, LANES)
        out_win = pltpu.roll(out_t[:, pl.ds(at, WINDOW)], turn, 1)[:, :LANES]
        ids_win = pltpu.roll(ids_wide[:, pl.ds(at, WINDOW)], turn, 1)[:, :LANES]
        base = (number * group).astype(F32)
        lefts = ([], [])
        terms = split2(out_win)
        for e in range(group):
            mask = (ids_win == base + float(e)).astype(F32)
            mask = jnp.concatenate([mask] * (pairs // 8), axis=0).astype(BF16)
            for left, term in zip(lefts, terms):
                left.append(jnp.concatenate([term[:pairs] * mask, term[pairs:] * mask], axis=1))
        left = jnp.concatenate(lefts[0] + lefts[1], axis=0)
        high, low = split2(in_twice[pl.ds(start, LANES), :])
        right = jnp.concatenate(
            [
                jnp.concatenate([high * lanes, low * lanes], axis=1)
                for lanes in (left_lanes, right_lanes)
            ],
            axis=0,
        )
        res = dot_nn(left, right)
        top = group * pairs
        rows[slot] = (
            (res[:top, :LANES] + res[top:, :LANES]) + (res[:top, LANES:] + res[top:, LANES:])
        )
        to = pl.multiple_of(g * group, group)
        for pair in range(pairs):
            sketch[pl.ds(to, group), pair * LANES:(pair + 1) * LANES] = rows[
                slot, pl.ds(pair, group, stride=pairs), :
            ]

    @pl.loop(0, ex_block // group // slots)
    def _(turn):
        for slot in range(slots):
            one_group(turn * slots + slot, slot)

    values = sketch[...]
    high, low = split2(values)
    high_ref[...] = high
    low_ref[...] = low
    sq = jnp.sum((values * values).reshape(ex_block // 8, 8, -1), axis=0)
    total = sq[:, 0:LANES]
    for k in range(1, values.shape[1] // LANES):
        total = total + sq[:, k * LANES:(k + 1) * LANES]
    sq_ref[...] += total


def build(offs, starts, sources, ids, pick, ranks, share, comps):
    tokens = ids.shape[1]
    half_ranks = pick.shape[0]
    ex_block = 256
    group = 8
    whole = lambda i, *_: (0, 0)
    return pl.pallas_call(
        functools.partial(build_kernel, ranks, share, ex_block, len(sources)),
        out_shape=(
            jax.ShapeDtypeStruct((EX_DEV, comps), BF16),
            jax.ShapeDtypeStruct((EX_DEV, comps), BF16),
            jax.ShapeDtypeStruct((8, LANES), F32),
        ),
        grid_spec=pltpu.PrefetchScalarGridSpec(
            num_scalar_prefetch=2,
            grid=(EX_DEV // ex_block,),
            in_specs=[pl.BlockSpec(a.shape, whole) for a in (*sources, ids, pick)],
            out_specs=[
                pl.BlockSpec((ex_block, comps), lambda i, *_: (i, 0)),
                pl.BlockSpec((ex_block, comps), lambda i, *_: (i, 0)),
                pl.BlockSpec((8, LANES), whole),
            ],
            scratch_shapes=[
                pltpu.VMEM((half_ranks, tokens), F32),
                pltpu.VMEM((tokens, LANES), F32),
                pltpu.VMEM((8, tokens), F32),
                pltpu.VMEM((4, group * half_ranks // 2, LANES), F32),
                pltpu.VMEM((ex_block, comps), F32),
            ],
        ),
        compiler_params=pltpu.CompilerParams(vmem_limit_bytes=BUILD * MIB),
        cost_estimate=pl.CostEstimate(
            flops=12 * EX_DEV * half_ranks * WINDOW * 2 * LANES,
            bytes_accessed=4 * EX_DEV * comps + 4 * tokens * LANES,
            transcendentals=0,
        ),
    )(offs, starts, *sources, ids, pick)


def join_kernel(planes, *refs):
    highs, lows, squares = refs[:planes], refs[planes:2 * planes], refs[2 * planes:3 * planes]
    slots, out_ref, b_ref = refs[3 * planes:-2], refs[-2], refs[-1]
    width = slots[0].shape[1]
    for k, slot in enumerate(slots):
        b_ref[:, k * width:(k + 1) * width] = slot[...]
    b = b_ref[...]
    count = b.shape[0]
    b_both = jnp.concatenate(split2(b), axis=0)
    for k in range(planes):
        both = (dot_nt(highs[k][...], b_both) + dot_nt(lows[k][...], b_both)).T
        out_ref[:, k * EX_DEV:(k + 1) * EX_DEV] = both[:count] + both[count:]
    total = squares[0][...]
    for square in squares[1:]:
        total = total + square[...]
    total = jnp.sum(jnp.sum(total, axis=1, keepdims=True), axis=0, keepdims=True)
    norm = jnp.sum(b * b, axis=1, keepdims=True)
    out_ref[:, planes * EX_DEV:] = lanes_of([norm, total], (count, LANES))


def join(highs, lows, squares, slots):
    planes = len(highs)
    count, comps = slots[0].shape[0], highs[0].shape[1]
    return pl.pallas_call(
        functools.partial(join_kernel, planes),
        out_shape=(
            jax.ShapeDtypeStruct((count, planes * EX_DEV + LANES), F32),
            jax.ShapeDtypeStruct((count, comps), F32),
        ),
        compiler_params=pltpu.CompilerParams(vmem_limit_bytes=STEP * MIB),
        cost_estimate=pl.CostEstimate(
            flops=6 * planes * EX_DEV * count * comps,
            bytes_accessed=4 * planes * EX_DEV * comps,
            transcendentals=0,
        ),
    )(*highs, *lows, *squares, *slots)


def column(values, k):
    return values[:, k:k + 1]


def lanes_of(columns, shape):
    lane = lax.broadcasted_iota(jnp.int32, shape, 1)
    out = jnp.zeros(shape, F32)
    for k, one in enumerate(columns):
        out = jnp.where(lane == k, one, out)
    return out


def begin(first, examples, comps_all, mine, other, s_prev, state):
    total = mine + other
    inner, stats = total[:, :examples], total[:, examples:]
    norm = column(stats, 0)
    if first:
        damping = 0.1 * column(stats, 1) / (examples * comps_all)
        s, length, beta = inner, norm, None
    else:
        beta = norm / column(state, 0)
        s = inner + beta * s_prev
        length = norm + 2.0 * beta * column(stats, 1) + beta * beta * column(state, 1)
        damping = column(state, 2)
    bend = jnp.sum(s * s, axis=1, keepdims=True) / examples + damping * length
    return s, norm, length, damping, beta, norm / bend


def step_kernel(first, planes, examples, comps_all, *refs):
    refs = list(refs)
    take = lambda n: [refs.pop(0) for _ in range(n)]
    mine_ref, other_ref, r_ref = take(3)
    if not first:
        p_ref, x_ref, s_ref, y_ref, state_ref = take(5)
    highs, lows = take(planes), take(planes)
    msg_out, r_out, p_out, x_out, s_out, y_out, state_out = take(7)
    s_two, z_acc, stats_acc, scal = take(4)
    count, comps = r_ref.shape
    s, norm, length, damping, beta, alpha = begin(
        first, examples, comps_all, mine_ref[...], other_ref[...],
        None if first else s_ref[...], None if first else state_ref[...],
    )
    s_out[...] = s
    y_out[...] = alpha * s if first else y_ref[...] + alpha * s
    high, low = split2(s)
    s_two[0:count, :] = high
    s_two[count:2 * count, :] = low
    state_out[...] = lanes_of([norm, length, damping], state_out.shape)
    scal[...] = lanes_of([alpha, damping] + ([] if first else [beta]), scal.shape)
    z_acc[...] = jnp.zeros_like(z_acc)
    stats_acc[...] = jnp.zeros_like(stats_acc)
    block = 512

    @pl.loop(0, comps // block)
    def _(turn):
        at = pl.ds(pl.multiple_of(turn * block, block), block)
        alpha, damping = scal[:, 0:1], scal[:, 1:2]
        r = r_ref[:, at]
        if first:
            p = r
            x_out[:, at] = alpha * p
        else:
            p = r + scal[:, 2:3] * p_ref[:, at]
            x_out[:, at] = x_ref[:, at] + alpha * p
        p_out[:, at] = p
        q = jnp.zeros(r.shape, F32)
        for k in range(planes):
            part = slice(k * EX_DEV, (k + 1) * EX_DEV)
            both = dot_nn(s_two[:, part], highs[k][:, at])
            q = q + both[:count] + both[count:] + dot_nn(s_two[0:count, part], lows[k][:, at])
        r_new = r - alpha * (q / examples + damping * p)
        r_out[:, at] = r_new
        stacked = jnp.concatenate(split2(r_new), axis=0)
        for k in range(planes):
            part = slice(k * EX_DEV, (k + 1) * EX_DEV)
            z_acc[part, :] += dot_nt(highs[k][:, at], stacked) + dot_nt(lows[k][:, at], stacked)
        stats_acc[...] += lanes_of(
            [
                jnp.sum(r_new * r_new, axis=1, keepdims=True),
                jnp.sum(r_new * p, axis=1, keepdims=True),
            ],
            stats_acc.shape,
        )

    both = z_acc[...].T
    msg_out[:, 0:examples] = both[:count] + both[count:]
    msg_out[:, examples:] = stats_acc[...]


def one_step(first, examples, comps_all, mine, other, r, rest, highs, lows):
    planes = len(highs)
    count, comps = r.shape
    wide = jax.ShapeDtypeStruct((count, examples), F32)
    long = jax.ShapeDtypeStruct((count, comps), F32)
    small = jax.ShapeDtypeStruct((count, LANES), F32)
    message = jax.ShapeDtypeStruct((count, examples + LANES), F32)
    return pl.pallas_call(
        functools.partial(step_kernel, first, planes, examples, comps_all),
        out_shape=(message, long, long, long, wide, wide, small),
        scratch_shapes=[
            pltpu.VMEM((2 * count, examples), BF16),
            pltpu.VMEM((examples, 2 * count), F32),
            pltpu.VMEM((count, LANES), F32),
            pltpu.VMEM((count, LANES), F32),
        ],
        compiler_params=pltpu.CompilerParams(vmem_limit_bytes=STEP * MIB),
        cost_estimate=pl.CostEstimate(
            flops=12 * count * examples * comps,
            bytes_accessed=4 * examples * comps,
            transcendentals=0,
        ),
    )(mine, other, r, *rest, *highs, *lows)


def last_kernel(examples, comps_all, mine_ref, other_ref, r_ref, p_ref, x_ref, s_ref, y_ref, state_ref, x_out, y_out):
    s, _, _, _, beta, alpha = begin(
        False, examples, comps_all, mine_ref[...], other_ref[...], s_ref[...], state_ref[...]
    )
    scale = 1.0 / jnp.sqrt(F32(comps_all))
    y_out[...] = (y_ref[...] + alpha * s) * scale
    x_out[...] = x_ref[...] + alpha * (r_ref[...] + beta * p_ref[...])


def last_step(examples, comps_all, *arrays):
    x, y = arrays[4], arrays[6]
    return pl.pallas_call(
        functools.partial(last_kernel, examples, comps_all),
        out_shape=(jax.ShapeDtypeStruct(x.shape, F32), jax.ShapeDtypeStruct(y.shape, F32)),
        compiler_params=pltpu.CompilerParams(vmem_limit_bytes=STEP * MIB),
    )(*arrays)


def arrange_kernel(count, origin_ref, *refs):
    parts, outs, held = refs[:count], refs[count:-1], refs[-1]
    rows = parts[0].shape[0]
    for k, part in enumerate(parts):
        held[k * rows:(k + 1) * rows, :] = part[...]
    for k, out in enumerate(outs):
        out[...] = held[pl.ds(pl.multiple_of(origin_ref[k] * rows, rows), rows), :]


def arrange(origin, parts):
    rows, columns = parts[0].shape
    whole = pl.BlockSpec((rows, columns), lambda i, origin: (0, 0))
    return pl.pallas_call(
        functools.partial(arrange_kernel, len(parts)),
        out_shape=(jax.ShapeDtypeStruct((rows, columns), F32),) * origin.shape[0],
        grid_spec=pltpu.PrefetchScalarGridSpec(
            num_scalar_prefetch=1,
            grid=(1,),
            in_specs=[whole] * len(parts),
            out_specs=[whole] * origin.shape[0],
            scratch_shapes=[pltpu.VMEM((len(parts) * rows, columns), F32)],
        ),
        compiler_params=pltpu.CompilerParams(vmem_limit_bytes=8 * MIB),
    )(origin, *parts)


def place_kernel(slots, count, where_ref, *refs):
    arrays, out_ref, held = refs[:count], refs[count], refs[count + 1]
    rows = arrays[0].shape[0] // slots
    k = where_ref[pl.program_id(0)]
    for number, array in enumerate(arrays):
        to = where_ref[slots + number]
        held[pl.ds(pl.multiple_of(to * rows, rows), rows), :] = array[
            pl.ds(pl.multiple_of(k * rows, rows), rows), :
        ]
    out_ref[...] = held[...].T


def place(where, arrays, slots, planes):
    rows, comps = arrays[0].shape[0] // slots * planes, arrays[0].shape[1]
    whole = pl.BlockSpec(arrays[0].shape, lambda i, where: (0, 0))
    return pl.pallas_call(
        functools.partial(place_kernel, slots, len(arrays)),
        out_shape=jax.ShapeDtypeStruct((comps, slots * rows), F32),
        grid_spec=pltpu.PrefetchScalarGridSpec(
            num_scalar_prefetch=1,
            grid=(slots,),
            in_specs=[whole] * len(arrays),
            out_specs=pl.BlockSpec((comps, rows), lambda i, where: (0, i)),
            scratch_shapes=[pltpu.VMEM((rows, comps), F32)],
        ),
        compiler_params=pltpu.CompilerParams(vmem_limit_bytes=24 * MIB),
    )(where, *arrays)


def per_device(n_dp, n_t, activations, out_grads, proj_in, proj_out, example_ids, queries):
    tokens = activations.shape[0]
    ranks = proj_in.shape[1]
    comps_all = proj_in.shape[1] * proj_out.shape[1]
    examples = EX_DEV * n_dp
    n_c = n_t // 2
    j = lax.axis_index("tensor")
    i = lax.axis_index("dp")
    chip, core = j // 2, j % 2

    def swap(values, mask):
        return lax.ppermute(values, "tensor", [(a, a ^ mask) for a in range(n_t)])

    def shift(values, by):
        return lax.ppermute(values, "dp", [(a, (a + by) % n_dp) for a in range(n_dp)])

    def tie(values, token):
        return lax.optimization_barrier((values, token))[0]

    near_chip = [chip ^ k for k in range(n_c)]

    q_chip = queries.shape[0] // n_dp
    parts = [
        lax.dynamic_slice_in_dim(queries, (i + away) % n_dp * q_chip, q_chip, 0) for away in range(n_dp)
    ]
    origin = jnp.stack([(i - near_chip[k]) % n_dp for k in range(n_c)]).astype(jnp.int32)

    group = 8
    bounds = group * jnp.arange(EX_DEV // group, dtype=jnp.int32)
    starts = jnp.sum((example_ids[0][None, :] < bounds[:, None]).astype(F32), axis=1)
    starts = jnp.minimum(starts, F32(tokens - LANES))
    id_rows = tokens // LANES
    extra = jnp.concatenate(
        [
            example_ids.astype(F32).reshape((id_rows, LANES)),
            jnp.pad(starts[None, :], ((0, 7), (0, LANES - EX_DEV // group))),
        ],
        axis=0,
    )

    share = tokens // n_t
    blocks = jnp.stack(near_chip).astype(jnp.int32) * 2
    w_in, w_out = proj_in.T, proj_out.T
    give = project(blocks + 1 - core, activations, out_grads, w_in, w_out, share)
    keep = project(blocks + core, activations, out_grads, w_in, w_out, share)
    kept = (keep + swap(give, 1)).reshape((n_c, share, LANES))
    own, parts = lax.optimization_barrier((kept[0], parts))
    came = [swap(kept[k], 2 * k) for k in range(1, n_c)]
    came[0], extra = lax.optimization_barrier((came[0], extra))
    for part in came:
        own = own + part
    extras = [extra] + [shift(extra, away) for away in range(1, n_dp)]
    plane_ids = [one[:id_rows].reshape((1, tokens)) for one in extras]
    firsts = [one[id_rows, :EX_DEV // group].astype(jnp.int32) for one in extras]

    parts = [parts[0]] + [shift(parts[k], k) for k in range(1, n_dp)]
    own, parts = lax.optimization_barrier((own, parts))

    rings = [own]
    for _ in range(n_dp - 1):
        rings.append(shift(rings[-1], 1))

    per = comps_all // ranks // n_t
    wanted = [(near_chip[k] * 2 + core) * per + a + ranks for k in range(n_c) for a in range(per)]
    wanted = jnp.stack(wanted[0::2] + wanted[1::2])
    pick = (wanted[:, None] == jnp.arange(LANES)[None, :]).astype(BF16)

    offs = jnp.stack(
        [near_chip[k] * 2 + which for which in (core, 1 - core) for k in range(n_c)]
    ).astype(jnp.int32)
    offs, pick, plane_ids, firsts, slots = lax.optimization_barrier(
        (offs, pick, plane_ids, firsts, arrange(origin, parts))
    )

    highs, lows, squares = [], [], []
    for away in range(n_dp):
        piece = rings[away]
        near = [piece] + [swap(piece, 2 * k) for k in range(1, n_c)]
        sources = near + [
            swap(part, 1) for part in (tie(near, squares[-1]) if squares else near)
        ]
        high, low, square = build(
            offs, firsts[away], sources, plane_ids[away], pick, ranks, share, comps_all // 2
        )
        highs.append(high)
        lows.append(low)
        squares.append(square)

    slots = [slots[0]] + [swap(slots[k], 2 * k) for k in range(1, n_c)]
    message, b = join(highs, lows, squares, slots)
    r, rest = b, ()
    for step in range(ITERS - 1):
        other = swap(message, 1)
        message, r, p, x, s, y, state = one_step(
            step == 0, examples, comps_all, message, other, r, rest, highs, lows
        )
        rest = (p, x, s, y, state)
    other = swap(message, 1)
    x, y = last_step(examples, comps_all, message, other, r, *rest)

    n_half = n_dp // 2
    per_slot = comps_all // n_t

    def send(values, by):
        pairs = [
            (a * n_t + 2 * c + a // n_half, (a + by) % n_dp * n_t + 2 * c + a // n_half)
            for a in range(n_dp) for c in range(n_c)
        ]
        return lax.ppermute(values, ("dp", "tensor"), pairs)

    by_plane = jnp.zeros((n_dp, q_chip, EX_DEV), F32)
    for away in range(n_dp):
        part = y[:, away * EX_DEV:(away + 1) * EX_DEV]
        if away:
            part = send(part, -away)
        by_plane = lax.dynamic_update_slice(by_plane, part[None], ((i + away) % n_dp, 0, 0))
    scores = lax.dynamic_slice_in_dim(by_plane, core * n_half, n_half, 0)

    ring = [x[:, k * per_slot:(k + 1) * per_slot] for k in range(n_c)]
    ring = jnp.concatenate([ring[0]] + [swap(ring[k], 2 * k) for k in range(1, n_c)], axis=0)
    arrays, places = [ring], [i]
    for away in range(1, n_dp):
        ring = shift(tie(ring, scores) if away == 2 else ring, 1)
        arrays.append(ring)
        places.append((i - away) % n_dp)
    where = jnp.stack([chip ^ c for c in range(n_c)] + places).astype(jnp.int32)
    out = place(where, arrays, n_c, n_dp)
    return (out, scores.reshape((n_half * q_chip, EX_DEV)))


def solution(mesh):
    in_specs = (
        P("dp", "tensor"),
        P("dp", "tensor"),
        P("tensor", None),
        P("tensor", None),
        P("dp", None),
        P("dp", "tensor"),
    )
    out_specs = (P("tensor", None), P("tensor", "dp"))
    body = functools.partial(per_device, mesh.shape["dp"], mesh.shape["tensor"])
    return jax.shard_map(body, mesh=mesh, in_specs=in_specs, out_specs=out_specs, check_vma=False)
```

```python
import functools

import jax
import jax.numpy as jnp
from jax import lax
from jax.experimental import pallas as pl
from jax.experimental.pallas import tpu as pltpu
from jax.sharding import PartitionSpec as P

ITERS = 4
EX_DEV = 512
LANES = 128
WINDOW = 256
PARTS = 4
F32 = jnp.float32
BF16 = jnp.bfloat16
MIB = 1024 * 1024
BUILD = 24
STEP = 24


def split2(values):
    high = values.astype(BF16)
    low = (values - high.astype(F32)).astype(BF16)
    return high, low


def dot_nn(left, right):
    return lax.dot_general(left, right, (((1,), (0,)), ((), ())), preferred_element_type=F32)


def dot_nt(left, right):
    return lax.dot_general(left, right, (((1,), (1,)), ((), ())), preferred_element_type=F32)


def project_kernel(order_ref, *refs):
    del order_ref
    acts, grads = refs[:PARTS], refs[PARTS:2 * PARTS]
    wi_ref, wo_ref, out_ref = refs[2 * PARTS:]
    rows = acts[0].shape[0]
    for part, (act_ref, grad_ref) in enumerate(zip(acts, grads)):
        out_ref[part * rows:(part + 1) * rows, :] = jnp.concatenate(
            [dot_nt(act_ref[...], wi_ref[...]), dot_nt(grad_ref[...], wo_ref[...])], axis=1
        )


def project(order, activations, out_grads, w_in, w_out, block):
    steps = order.shape[0]
    feats, hidden = activations.shape[1], out_grads.shape[1]
    rows = block // PARTS

    def parts(width):
        return [
            pl.BlockSpec((rows, width), lambda i, order, part=part: (order[i] * PARTS + part, 0))
            for part in range(PARTS)
        ]

    return pl.pallas_call(
        project_kernel,
        out_shape=jax.ShapeDtypeStruct((steps * block, LANES), F32),
        grid_spec=pltpu.PrefetchScalarGridSpec(
            num_scalar_prefetch=1,
            grid=(steps,),
            in_specs=parts(feats) + parts(hidden) + [
                pl.BlockSpec(w_in.shape, lambda i, order: (0, 0)),
                pl.BlockSpec(w_out.shape, lambda i, order: (0, 0)),
            ],
            out_specs=pl.BlockSpec((block, LANES), lambda i, order: (i, 0)),
        ),
        compiler_params=pltpu.CompilerParams(vmem_limit_bytes=61 * MIB),
        cost_estimate=pl.CostEstimate(
            flops=2 * steps * block * (feats + hidden) * 4 * WINDOW,
            bytes_accessed=2 * steps * block * (feats + hidden),
            transcendentals=0,
        ),
    )(order, *[activations] * PARTS, *[out_grads] * PARTS, w_in, w_out)


def build_kernel(ranks, share, ex_block, n_sources, *refs):
    offs_ref, start_ref = refs[:2]
    sources = refs[2:2 + n_sources]
    ids_ref, pick_ref = refs[2 + n_sources:4 + n_sources]
    high_ref, low_ref, sq_ref = refs[4 + n_sources:7 + n_sources]
    out_t, in_twice, ids_wide, rows, sketch = refs[7 + n_sources:]
    step = pl.program_id(0)
    half_ranks = pick_ref.shape[0]
    pairs = half_ranks // 2
    tokens = ids_ref.shape[1]

    @pl.when(step == 0)
    def _():
        lane = lax.broadcasted_iota(jnp.int32, (share, LANES), 1)
        block = 0
        for source in sources:
            for k in range(source.shape[0] // share):
                values = source[k * share:(k + 1) * share, :]
                at = pl.multiple_of(offs_ref[block] * share, share)
                block += 1
                high, low = split2(values)
                out_t[:, pl.ds(at, share)] = dot_nt(pick_ref[...], high) + dot_nt(pick_ref[...], low)
                in_twice[pl.ds(at, share), :] = jnp.where(
                    lane < ranks, values, pltpu.roll(values, ranks, 1)
                )
        ids_wide[...] = jnp.broadcast_to(ids_ref[...], ids_wide.shape)
        sq_ref[...] = jnp.zeros_like(sq_ref)

    slots = rows.shape[0]
    group = rows.shape[1] // pairs
    lane = lax.broadcasted_iota(jnp.int32, (LANES, LANES), 1)
    left_lanes = (lane < ranks).astype(F32).astype(BF16)
    right_lanes = (lane >= ranks).astype(F32).astype(BF16)

    def one_group(g, slot):
        number = step * (ex_block // group) + g
        start = start_ref[number]
        at = jnp.minimum(lax.div(start, LANES) * LANES, tokens - WINDOW)
        turn = lax.rem(WINDOW - (start - at), WINDOW)
        at = pl.multiple_of(at, LANES)
        out_win = pltpu.roll(out_t[:, pl.ds(at, WINDOW)], turn, 1)[:, :LANES]
        ids_win = pltpu.roll(ids_wide[:, pl.ds(at, WINDOW)], turn, 1)[:, :LANES]
        base = (number * group).astype(F32)
        lefts = ([], [])
        terms = split2(out_win)
        for e in range(group):
            mask = (ids_win == base + float(e)).astype(F32)
            mask = jnp.concatenate([mask] * (pairs // 8), axis=0).astype(BF16)
            for left, term in zip(lefts, terms):
                left.append(jnp.concatenate([term[:pairs] * mask, term[pairs:] * mask], axis=1))
        left = jnp.concatenate(lefts[0] + lefts[1], axis=0)
        high, low = split2(in_twice[pl.ds(start, LANES), :])
        right = jnp.concatenate(
            [
                jnp.concatenate([high * lanes, low * lanes], axis=1)
                for lanes in (left_lanes, right_lanes)
            ],
            axis=0,
        )
        res = dot_nn(left, right)
        top = group * pairs
        rows[slot] = (
            (res[:top, :LANES] + res[top:, :LANES]) + (res[:top, LANES:] + res[top:, LANES:])
        )
        to = pl.multiple_of(g * group, group)
        for pair in range(pairs):
            sketch[pl.ds(to, group), pair * LANES:(pair + 1) * LANES] = rows[
                slot, pl.ds(pair, group, stride=pairs), :
            ]

    @pl.loop(0, ex_block // group // slots)
    def _(turn):
        for slot in range(slots):
            one_group(turn * slots + slot, slot)

    values = sketch[...]
    high, low = split2(values)
    high_ref[...] = high
    low_ref[...] = low
    sq = jnp.sum((values * values).reshape(ex_block // 8, 8, -1), axis=0)
    total = sq[:, 0:LANES]
    for k in range(1, values.shape[1] // LANES):
        total = total + sq[:, k * LANES:(k + 1) * LANES]
    sq_ref[...] += total


def build(offs, starts, sources, ids, pick, ranks, share, comps):
    tokens = ids.shape[1]
    half_ranks = pick.shape[0]
    ex_block = 256
    group = 8
    whole = lambda i, *_: (0, 0)
    return pl.pallas_call(
        functools.partial(build_kernel, ranks, share, ex_block, len(sources)),
        out_shape=(
            jax.ShapeDtypeStruct((EX_DEV, comps), BF16),
            jax.ShapeDtypeStruct((EX_DEV, comps), BF16),
            jax.ShapeDtypeStruct((8, LANES), F32),
        ),
        grid_spec=pltpu.PrefetchScalarGridSpec(
            num_scalar_prefetch=2,
            grid=(EX_DEV // ex_block,),
            in_specs=[pl.BlockSpec(a.shape, whole) for a in (*sources, ids, pick)],
            out_specs=[
                pl.BlockSpec((ex_block, comps), lambda i, *_: (i, 0)),
                pl.BlockSpec((ex_block, comps), lambda i, *_: (i, 0)),
                pl.BlockSpec((8, LANES), whole),
            ],
            scratch_shapes=[
                pltpu.VMEM((half_ranks, tokens), F32),
                pltpu.VMEM((tokens, LANES), F32),
                pltpu.VMEM((8, tokens), F32),
                pltpu.VMEM((8, group * half_ranks // 2, LANES), F32),
                pltpu.VMEM((ex_block, comps), F32),
            ],
        ),
        compiler_params=pltpu.CompilerParams(vmem_limit_bytes=BUILD * MIB),
        cost_estimate=pl.CostEstimate(
            flops=12 * EX_DEV * half_ranks * WINDOW * 2 * LANES,
            bytes_accessed=4 * EX_DEV * comps + 4 * tokens * LANES,
            transcendentals=0,
        ),
    )(offs, starts, *sources, ids, pick)


def join_kernel(planes, *refs):
    highs, lows, squares = refs[:planes], refs[planes:2 * planes], refs[2 * planes:3 * planes]
    slots, out_ref, b_ref = refs[3 * planes:-2], refs[-2], refs[-1]
    width = slots[0].shape[1]
    for k, slot in enumerate(slots):
        b_ref[:, k * width:(k + 1) * width] = slot[...]
    b = b_ref[...]
    count = b.shape[0]
    b_both = jnp.concatenate(split2(b), axis=0)
    for k in range(planes):
        both = (dot_nt(highs[k][...], b_both) + dot_nt(lows[k][...], b_both)).T
        out_ref[:, k * EX_DEV:(k + 1) * EX_DEV] = both[:count] + both[count:]
    total = squares[0][...]
    for square in squares[1:]:
        total = total + square[...]
    total = jnp.sum(jnp.sum(total, axis=1, keepdims=True), axis=0, keepdims=True)
    norm = jnp.sum(b * b, axis=1, keepdims=True)
    out_ref[:, planes * EX_DEV:] = lanes_of([norm, total], (count, LANES))


def join(highs, lows, squares, slots):
    planes = len(highs)
    count, comps = slots[0].shape[0], highs[0].shape[1]
    return pl.pallas_call(
        functools.partial(join_kernel, planes),
        out_shape=(
            jax.ShapeDtypeStruct((count, planes * EX_DEV + LANES), F32),
            jax.ShapeDtypeStruct((count, comps), F32),
        ),
        compiler_params=pltpu.CompilerParams(vmem_limit_bytes=STEP * MIB),
        cost_estimate=pl.CostEstimate(
            flops=6 * planes * EX_DEV * count * comps,
            bytes_accessed=4 * planes * EX_DEV * comps,
            transcendentals=0,
        ),
    )(*highs, *lows, *squares, *slots)


def column(values, k):
    return values[:, k:k + 1]


def lanes_of(columns, shape):
    lane = lax.broadcasted_iota(jnp.int32, shape, 1)
    out = jnp.zeros(shape, F32)
    for k, one in enumerate(columns):
        out = jnp.where(lane == k, one, out)
    return out


def begin(first, examples, comps_all, mine, other, s_prev, state):
    total = mine + other
    inner, stats = total[:, :examples], total[:, examples:]
    norm = column(stats, 0)
    if first:
        damping = 0.1 * column(stats, 1) / (examples * comps_all)
        s, length, beta = inner, norm, None
    else:
        beta = norm / column(state, 0)
        s = inner + beta * s_prev
        length = norm + 2.0 * beta * column(stats, 1) + beta * beta * column(state, 1)
        damping = column(state, 2)
    bend = jnp.sum(s * s, axis=1, keepdims=True) / examples + damping * length
    return s, norm, length, damping, beta, norm / bend


def step_kernel(first, planes, examples, comps_all, *refs):
    refs = list(refs)
    take = lambda n: [refs.pop(0) for _ in range(n)]
    mine_ref, other_ref, r_ref = take(3)
    if not first:
        p_ref, x_ref, s_ref, y_ref, state_ref = take(5)
    highs, lows = take(planes), take(planes)
    msg_out, r_out, p_out, x_out, s_out, y_out, state_out = take(7)
    s_two, z_acc, stats_acc, scal = take(4)
    count, comps = r_ref.shape
    s, norm, length, damping, beta, alpha = begin(
        first, examples, comps_all, mine_ref[...], other_ref[...],
        None if first else s_ref[...], None if first else state_ref[...],
    )
    s_out[...] = s
    y_out[...] = alpha * s if first else y_ref[...] + alpha * s
    high, low = split2(s)
    s_two[0:count, :] = high
    s_two[count:2 * count, :] = low
    state_out[...] = lanes_of([norm, length, damping], state_out.shape)
    scal[...] = lanes_of([alpha, damping] + ([] if first else [beta]), scal.shape)
    z_acc[...] = jnp.zeros_like(z_acc)
    stats_acc[...] = jnp.zeros_like(stats_acc)
    block = 512

    @pl.loop(0, comps // block)
    def _(turn):
        at = pl.ds(pl.multiple_of(turn * block, block), block)
        alpha, damping = scal[:, 0:1], scal[:, 1:2]
        r = r_ref[:, at]
        if first:
            p = r
            x_out[:, at] = alpha * p
        else:
            p = r + scal[:, 2:3] * p_ref[:, at]
            x_out[:, at] = x_ref[:, at] + alpha * p
        p_out[:, at] = p
        q = jnp.zeros(r.shape, F32)
        for k in range(planes):
            part = slice(k * EX_DEV, (k + 1) * EX_DEV)
            both = dot_nn(s_two[:, part], highs[k][:, at])
            q = q + both[:count] + both[count:] + dot_nn(s_two[0:count, part], lows[k][:, at])
        r_new = r - alpha * (q / examples + damping * p)
        r_out[:, at] = r_new
        stacked = jnp.concatenate(split2(r_new), axis=0)
        for k in range(planes):
            part = slice(k * EX_DEV, (k + 1) * EX_DEV)
            z_acc[part, :] += dot_nt(highs[k][:, at], stacked) + dot_nt(lows[k][:, at], stacked)
        stats_acc[...] += lanes_of(
            [
                jnp.sum(r_new * r_new, axis=1, keepdims=True),
                jnp.sum(r_new * p, axis=1, keepdims=True),
            ],
            stats_acc.shape,
        )

    both = z_acc[...].T
    msg_out[:, 0:examples] = both[:count] + both[count:]
    msg_out[:, examples:] = stats_acc[...]


def one_step(first, examples, comps_all, mine, other, r, rest, highs, lows):
    planes = len(highs)
    count, comps = r.shape
    wide = jax.ShapeDtypeStruct((count, examples), F32)
    long = jax.ShapeDtypeStruct((count, comps), F32)
    small = jax.ShapeDtypeStruct((count, LANES), F32)
    message = jax.ShapeDtypeStruct((count, examples + LANES), F32)
    return pl.pallas_call(
        functools.partial(step_kernel, first, planes, examples, comps_all),
        out_shape=(message, long, long, long, wide, wide, small),
        scratch_shapes=[
            pltpu.VMEM((2 * count, examples), BF16),
            pltpu.VMEM((examples, 2 * count), F32),
            pltpu.VMEM((count, LANES), F32),
            pltpu.VMEM((count, LANES), F32),
        ],
        compiler_params=pltpu.CompilerParams(vmem_limit_bytes=STEP * MIB),
        cost_estimate=pl.CostEstimate(
            flops=12 * count * examples * comps,
            bytes_accessed=4 * examples * comps,
            transcendentals=0,
        ),
    )(mine, other, r, *rest, *highs, *lows)


def last_kernel(examples, comps_all, mine_ref, other_ref, r_ref, p_ref, x_ref, s_ref, y_ref, state_ref, x_out, y_out):
    s, _, _, _, beta, alpha = begin(
        False, examples, comps_all, mine_ref[...], other_ref[...], s_ref[...], state_ref[...]
    )
    scale = 1.0 / jnp.sqrt(F32(comps_all))
    y_out[...] = (y_ref[...] + alpha * s) * scale
    x_out[...] = x_ref[...] + alpha * (r_ref[...] + beta * p_ref[...])


def last_step(examples, comps_all, *arrays):
    x, y = arrays[4], arrays[6]
    return pl.pallas_call(
        functools.partial(last_kernel, examples, comps_all),
        out_shape=(jax.ShapeDtypeStruct(x.shape, F32), jax.ShapeDtypeStruct(y.shape, F32)),
        compiler_params=pltpu.CompilerParams(vmem_limit_bytes=STEP * MIB),
    )(*arrays)


def arrange_kernel(count, origin_ref, *refs):
    parts, outs, held = refs[:count], refs[count:-1], refs[-1]
    rows = parts[0].shape[0]
    for k, part in enumerate(parts):
        held[k * rows:(k + 1) * rows, :] = part[...]
    for k, out in enumerate(outs):
        out[...] = held[pl.ds(pl.multiple_of(origin_ref[k] * rows, rows), rows), :]


def arrange(origin, parts):
    rows, columns = parts[0].shape
    whole = pl.BlockSpec((rows, columns), lambda i, origin: (0, 0))
    return pl.pallas_call(
        functools.partial(arrange_kernel, len(parts)),
        out_shape=(jax.ShapeDtypeStruct((rows, columns), F32),) * origin.shape[0],
        grid_spec=pltpu.PrefetchScalarGridSpec(
            num_scalar_prefetch=1,
            grid=(1,),
            in_specs=[whole] * len(parts),
            out_specs=[whole] * origin.shape[0],
            scratch_shapes=[pltpu.VMEM((len(parts) * rows, columns), F32)],
        ),
        compiler_params=pltpu.CompilerParams(vmem_limit_bytes=8 * MIB),
    )(origin, *parts)


def place_kernel(slots, count, where_ref, *refs):
    arrays, out_ref, held = refs[:count], refs[count], refs[count + 1]
    rows = arrays[0].shape[0] // slots
    k = where_ref[pl.program_id(0)]
    for number, array in enumerate(arrays):
        to = where_ref[slots + number]
        held[pl.ds(pl.multiple_of(to * rows, rows), rows), :] = array[
            pl.ds(pl.multiple_of(k * rows, rows), rows), :
        ]
    out_ref[...] = held[...].T


def place(where, arrays, slots, planes):
    rows, comps = arrays[0].shape[0] // slots * planes, arrays[0].shape[1]
    whole = pl.BlockSpec(arrays[0].shape, lambda i, where: (0, 0))
    return pl.pallas_call(
        functools.partial(place_kernel, slots, len(arrays)),
        out_shape=jax.ShapeDtypeStruct((comps, slots * rows), F32),
        grid_spec=pltpu.PrefetchScalarGridSpec(
            num_scalar_prefetch=1,
            grid=(slots,),
            in_specs=[whole] * len(arrays),
            out_specs=pl.BlockSpec((comps, rows), lambda i, where: (0, i)),
            scratch_shapes=[pltpu.VMEM((rows, comps), F32)],
        ),
        compiler_params=pltpu.CompilerParams(vmem_limit_bytes=24 * MIB),
    )(where, *arrays)


def per_device(n_dp, n_t, activations, out_grads, proj_in, proj_out, example_ids, queries):
    tokens = activations.shape[0]
    ranks = proj_in.shape[1]
    comps_all = proj_in.shape[1] * proj_out.shape[1]
    examples = EX_DEV * n_dp
    n_c = n_t // 2
    j = lax.axis_index("tensor")
    i = lax.axis_index("dp")
    chip, core = j // 2, j % 2

    def swap(values, mask):
        return lax.ppermute(values, "tensor", [(a, a ^ mask) for a in range(n_t)])

    def shift(values, by):
        return lax.ppermute(values, "dp", [(a, (a + by) % n_dp) for a in range(n_dp)])

    def tie(values, token):
        return lax.optimization_barrier((values, token))[0]

    near_chip = [chip ^ k for k in range(n_c)]

    q_chip = queries.shape[0] // n_dp
    parts = [
        lax.dynamic_slice_in_dim(queries, (i + away) % n_dp * q_chip, q_chip, 0) for away in range(n_dp)
    ]
    origin = jnp.stack([(i - near_chip[k]) % n_dp for k in range(n_c)]).astype(jnp.int32)

    group = 8
    bounds = group * jnp.arange(EX_DEV // group, dtype=jnp.int32)
    starts = jnp.sum((example_ids[0][None, :] < bounds[:, None]).astype(F32), axis=1)
    starts = jnp.minimum(starts, F32(tokens - LANES))
    id_rows = tokens // LANES
    extra = jnp.concatenate(
        [
            example_ids.astype(F32).reshape((id_rows, LANES)),
            jnp.pad(starts[None, :], ((0, 7), (0, LANES - EX_DEV // group))),
        ],
        axis=0,
    )

    share = tokens // n_t
    blocks = jnp.stack(near_chip).astype(jnp.int32) * 2
    w_in, w_out = proj_in.T, proj_out.T
    give = project(blocks + 1 - core, activations, out_grads, w_in, w_out, share)
    keep = project(blocks + core, activations, out_grads, w_in, w_out, share)
    kept = (keep + swap(give, 1)).reshape((n_c, share, LANES))
    kept, extra, parts = lax.optimization_barrier((kept, extra, parts))
    extras = [extra] + [shift(extra, away) for away in range(1, n_dp)]
    plane_ids = [one[:id_rows].reshape((1, tokens)) for one in extras]
    firsts = [one[id_rows, :EX_DEV // group].astype(jnp.int32) for one in extras]
    own = kept[0]
    for k in range(1, n_c):
        own = own + swap(kept[k], 2 * k)

    parts = [parts[0]] + [shift(parts[k], k) for k in range(1, n_dp)]
    own, parts, plane_ids, firsts = lax.optimization_barrier((own, parts, plane_ids, firsts))

    rings = [own]
    for _ in range(n_dp - 1):
        rings.append(shift(rings[-1], 1))

    per = comps_all // ranks // n_t
    wanted = [(near_chip[k] * 2 + core) * per + a + ranks for k in range(n_c) for a in range(per)]
    wanted = jnp.stack(wanted[0::2] + wanted[1::2])
    pick = (wanted[:, None] == jnp.arange(LANES)[None, :]).astype(BF16)

    offs = jnp.stack(
        [near_chip[k] * 2 + which for which in (core, 1 - core) for k in range(n_c)]
    ).astype(jnp.int32)
    offs, pick, plane_ids, firsts, slots = lax.optimization_barrier(
        (offs, pick, plane_ids, firsts, arrange(origin, parts))
    )

    highs, lows, squares = [], [], []
    for away in range(n_dp):
        piece = rings[away]
        near = [piece] + [swap(piece, 2 * k) for k in range(1, n_c)]
        sources = near + [
            swap(part, 1) for part in (tie(near, squares[-1]) if squares else near)
        ]
        high, low, square = build(
            offs, firsts[away], sources, plane_ids[away], pick, ranks, share, comps_all // 2
        )
        highs.append(high)
        lows.append(low)
        squares.append(square)

    slots = [slots[0]] + [swap(slots[k], 2 * k) for k in range(1, n_c)]
    message, b = join(highs, lows, squares, slots)
    r, rest = b, ()
    for step in range(ITERS - 1):
        other = swap(message, 1)
        message, r, p, x, s, y, state = one_step(
            step == 0, examples, comps_all, message, other, r, rest, highs, lows
        )
        rest = (p, x, s, y, state)
    other = swap(message, 1)
    x, y = last_step(examples, comps_all, message, other, r, *rest)

    n_half = n_dp // 2
    per_slot = comps_all // n_t

    def send(values, by):
        pairs = [
            (a * n_t + 2 * c + a // n_half, (a + by) % n_dp * n_t + 2 * c + a // n_half)
            for a in range(n_dp) for c in range(n_c)
        ]
        return lax.ppermute(values, ("dp", "tensor"), pairs)

    by_plane = jnp.zeros((n_dp, q_chip, EX_DEV), F32)
    for away in range(n_dp):
        part = y[:, away * EX_DEV:(away + 1) * EX_DEV]
        if away:
            part = send(part, -away)
        by_plane = lax.dynamic_update_slice(by_plane, part[None], ((i + away) % n_dp, 0, 0))
    scores = lax.dynamic_slice_in_dim(by_plane, core * n_half, n_half, 0)

    ring = [x[:, k * per_slot:(k + 1) * per_slot] for k in range(n_c)]
    ring = jnp.concatenate([ring[0]] + [swap(ring[k], 2 * k) for k in range(1, n_c)], axis=0)
    arrays, places = [ring], [i]
    for away in range(1, n_dp):
        ring = shift(tie(ring, scores) if away == 2 else ring, 1)
        arrays.append(ring)
        places.append((i - away) % n_dp)
    where = jnp.stack([chip ^ c for c in range(n_c)] + places).astype(jnp.int32)
    out = place(where, arrays, n_c, n_dp)
    return (out, scores.reshape((n_half * q_chip, EX_DEV)))


def solution(mesh):
    in_specs = (
        P("dp", "tensor"),
        P("dp", "tensor"),
        P("tensor", None),
        P("tensor", None),
        P("dp", None),
        P("dp", "tensor"),
    )
    out_specs = (P("tensor", None), P("tensor", "dp"))
    body = functools.partial(per_device, mesh.shape["dp"], mesh.shape["tensor"])
    return jax.shard_map(body, mesh=mesh, in_specs=in_specs, out_specs=out_specs, check_vma=False)
```
